32 devices in a mesh: tm: 4 (over z), space: 8 (over y, x, core).
Axes of the slice: x: 2, y: 2, z: 4, core: 2. Of those that a mesh axis runs over, the one named last changes fastest.
Arguments:
- probes: bfloat16 [192, 128, 1024], P('tm', 'space'), may hold values from -6 to 6
- local_links: int32 [128, 4], P('space'), may hold values from 0 to 15
- remote_links: int32 [128, 2], P('space'), may hold values from 0 to 15
- shared_blocks: int32 [8, 2], P('space'), may hold values from 0 to 15, as said below
- slab_days: int32 [4], P('tm'), may hold values from 1 to 48, 120 in all
- local_coupling: bfloat16 [128, 4, 64, 64], P('space'), may hold values from -0.3125 to 0.3125
- remote_coupling: bfloat16 [128, 2, 64, 64], P('space'), may hold values from -0.3125 to 0.3125
- block_inverse: bfloat16 [128, 64, 64], P('space'), may hold values from -0.0546875 to 0.0546875
- retention: float32 [192, 8192], P('tm', 'space'), as said below
Outputs:
- variance: float32 [192, 8192], P('tm', 'space')
The draws below stay inside these ranges and needn't reach their ends.
Inputs may be any that keep to these rules, and one draw needn't show every extreme that they name: `shared_blocks`: each group's 2 numbers differ, and each list holds the group's last local block. `retention`: share of a node's state carried from one day to the next.
All inputs are finite; a program needn't handle non-finite values. No bound on the sum of `slab_days` on one device may be relied on, other than what follows from the above.
Results may differ from the reference program's by a relative error of at most 0.0028.
Values may be sent and summed in bfloat16 or wider, within the bound.
No kernel may reach another device: no remote copies, remote signals or barrier semaphores. Data moves between devices by JAX's collectives and lax.ppermute only.
A program may use at most 192 MiB of HBM per device.

```python
import math
import jax
import jax.numpy as jnp
import numpy as np
from jax import lax

BS = 64
P_SIZE = 16
KLOC = 4
KREM = 2
BND = 2
DAYS = 48
BLK_DEV = 16
CALENDAR_LENGTH = 192
NBLK = 128
MESH_POINT_COUNT = 8192
N_TM = 4
N_SPACE = 8


def draw_shared_blocks(key, part):
    keys = jax.random.split(key, N_SPACE)

    def single_group(group_key):
        order = jax.random.permutation(group_key, BLK_DEV).astype(jnp.int32)
        topmost = BLK_DEV - 1
        order = jnp.where(order == topmost, order[0], order)
        order = order.at[0].set(topmost)
        return order[:BND]
    return jax.vmap(single_group)(keys).astype(jnp.int32)


def draw_retention(key, part):
    intensity_seed = jax.random.fold_in(key, 11)
    shower_seed = jax.random.fold_in(key, 12)
    multiplier_seed = jax.random.fold_in(key, 13)
    lower_limit = 0.05 / CALENDAR_LENGTH
    upper_limit = 1.0 / 30.0
    shower_intensity = jnp.exp(jax.random.uniform(intensity_seed, (1, MESH_POINT_COUNT), jnp.float32, math.log(lower_limit), math.log(upper_limit)))
    shower_sequence = jax.random.uniform(shower_seed, (CALENDAR_LENGTH, 1), jnp.float32) < 4.0 / CALENDAR_LENGTH
    shower_multiplier = jax.random.uniform(multiplier_seed, (CALENDAR_LENGTH, 1), jnp.float32, 0.5, 0.8)
    return (jnp.exp(-shower_intensity) * jnp.where(shower_sequence, shower_multiplier, 1.0)).astype(jnp.float32)


def plant(values, key, least, high):
    shape = values.shape
    place = [jax.random.randint(jax.random.fold_in(key, axis), (), 0, shape[axis]) for axis in range(len(shape))]
    values = values.at[tuple(place)].set(least)
    longest = shape.index(max(shape))
    place[longest] = (place[longest] + 1) % shape[longest]
    return values.at[tuple(place)].set(high)


def shard_levels(rng, shape, cuts, smallest, top_value):
    loudness, own = 1.0, jax.random.fold_in(rng, 6)
    for axis_at, blocks in cuts:
        draws = jnp.exp(jax.random.uniform(jax.random.fold_in(own, axis_at), (blocks,), jnp.float32, smallest / len(cuts), top_value / len(cuts)))
        loudness = loudness * jnp.repeat(draws, shape[axis_at] // blocks).reshape([-1 if axis == axis_at else 1 for axis in range(len(shape))])
    return loudness


def length_profile(number_of, total, bound, skew):
    loads = [(1 << 20) // math.isqrt(standing ** skew) + 1 for standing in range(2, number_of + 1)]
    spare, counts = total - bound - (number_of - 1), [1] * (number_of - 1)
    while spare > 0:
        free = [i for i in range(number_of - 1) if counts[i] < bound]
        pool, left = sum([loads[i] for i in free]), spare
        for i in free:
            addition = min(bound - counts[i], max(1, left * loads[i] // pool), spare)
            counts[i] = counts[i] + addition
            spare = spare - addition
    return np.array([bound] + counts)


def ragged_sizes(own_key, amount, total, bound, skew):
    if amount == 2:
        one = jax.random.randint(own_key, (), max(1, total - bound), min(bound, total - 1) + 1)
        return jnp.stack([one, total - one])
    sizes = jnp.asarray(length_profile(amount, total, bound, skew), jnp.int32)
    twos = (amount - 1) // 2
    giver, sink = sizes[1:1 + 2 * twos:2], sizes[2:2 + 2 * twos:2]
    slack = jnp.minimum(giver - 1, bound - sink)
    moved = jax.random.randint(jax.random.fold_in(own_key, 1), (twos,), 0, 1 << 20) % (slack + 1)
    sizes = sizes.at[1:1 + 2 * twos:2].set(giver - moved).at[2:2 + 2 * twos:2].set(sink + moved)
    return sizes[jax.random.permutation(jax.random.fold_in(own_key, 2), amount)]


def gaussian(rng, shape, deviation, most, cuts=(), kind=jnp.bfloat16):
    drawn = deviation * jax.random.normal(rng, shape, jnp.float32)
    if cuts:
        drawn = drawn * shard_levels(rng, shape, cuts, -0.22, 0.18)
    return jnp.clip(drawn, -most, most).astype(kind)


def setup_inputs(seed: int = 0) -> dict:
    arg_keys = jax.random.split(jax.random.key(seed), 10)
    return {
        "probes": gaussian(arg_keys[0], (CALENDAR_LENGTH, NBLK, BS * P_SIZE), 1.0, 6.0, ((0, 4), (1, 8))),
        "local_links": plant(jax.random.randint(arg_keys[1], (NBLK, KLOC), 0, BLK_DEV), jax.random.fold_in(arg_keys[1], 1), 0, BLK_DEV - 1).astype(jnp.int32),
        "remote_links": plant(jax.random.randint(arg_keys[2], (NBLK, KREM), 0, N_SPACE * BND), jax.random.fold_in(arg_keys[2], 1), 0, (N_SPACE * BND) - 1).astype(jnp.int32),
        "shared_blocks": draw_shared_blocks(jax.random.fold_in(arg_keys[9], 71), 0),
        "slab_days": ragged_sizes(arg_keys[4], N_TM, DAYS + (N_TM - 1) * (DAYS // 2), DAYS, 2).astype(jnp.int32),
        "local_coupling": gaussian(arg_keys[5], (NBLK, KLOC, BS, BS), (BS * (KLOC + KREM)) ** -0.5, 0.3125, ((0, 8),)),
        "remote_coupling": gaussian(arg_keys[6], (NBLK, KREM, BS, BS), (BS * (KLOC + KREM)) ** -0.5, 0.3125, ((0, 8),)),
        "block_inverse": gaussian(arg_keys[7], (NBLK, BS, BS), (BS * CALENDAR_LENGTH) ** -0.5, 0.0546875, ((0, 8),)),
        "retention": draw_retention(jax.random.fold_in(arg_keys[9], 71), 0),
    }


def reference(probes, local_links, remote_links, shared_blocks, slab_days, local_coupling, remote_coupling, block_inverse, retention):
    shaped = probes.reshape(CALENDAR_LENGTH, NBLK, BS, P_SIZE)
    owners = (jnp.arange(NBLK) // BLK_DEV).astype(jnp.int32)[:, None]
    local_global = owners * BLK_DEV + local_links
    shared_global = (jnp.arange(N_SPACE).astype(jnp.int32)[:, None] * BLK_DEV + shared_blocks).reshape(-1)
    remote_global = shared_global[remote_links]
    day_index = jnp.arange(CALENDAR_LENGTH).astype(jnp.int32)
    active = (day_index % DAYS < slab_days[day_index // DAYS]).astype(jnp.float32)
    retain = jnp.where(active[:, None] > 0, retention, 1.0).reshape(CALENDAR_LENGTH, NBLK, BS, 1)
    local_wide = local_coupling.astype(jnp.float32)
    remote_wide = remote_coupling.astype(jnp.float32)
    inverse_wide = block_inverse.astype(jnp.float32)

    def advance(propagated_vector, argument_bundle):
        present_date, shower_multiplier, marked_entries = argument_bundle
        wide = present_date.astype(jnp.float32)
        running = wide
        for column in range(KLOC):
            running = running - jnp.einsum("bij,bjp->bip", local_wide[:, column], wide[local_global[:, column]])
        for column in range(KREM):
            running = running - jnp.einsum("bij,bjp->bip", remote_wide[:, column], wide[remote_global[:, column]])
        source = running.astype(jnp.bfloat16)
        driving_source = jnp.einsum("bij,bjp->bip", inverse_wide, source.astype(jnp.float32)) * marked_entries
        propagated_vector = shower_multiplier * propagated_vector + driving_source
        return propagated_vector, propagated_vector.astype(jnp.bfloat16)

    start = jnp.zeros((NBLK, BS, P_SIZE), jnp.float32)
    unused, stored = lax.scan(advance, start, (shaped, retain, active))

    def retreat(propagated_vector, argument_bundle):
        saved_calendar_index, present_date, shower_multiplier, marked_entries = argument_bundle
        adjoint = jnp.einsum("bji,bjp->bip", inverse_wide, saved_calendar_index.astype(jnp.float32)) * marked_entries
        present_vector = adjoint + propagated_vector
        approximation = jnp.mean(present_date.astype(jnp.float32) * present_vector, axis=-1).reshape(-1)
        return shower_multiplier * present_vector, approximation

    unused_back, variance = lax.scan(retreat, start, (stored, shaped, retain, active), reverse=True)
    return variance
```

```python
import functools

import jax
import jax.numpy as jnp
from jax import lax
from jax.experimental import pallas as pl
from jax.experimental.pallas import tpu as pltpu
from jax.sharding import PartitionSpec as P

LANES = 128
GROUPS = 8
VMEM_LIMIT = 56 * 1024 * 1024


def swap_groups(rows, width):
    group = lax.broadcasted_iota(jnp.int32, rows[0].shape, 1) // width
    rows = list(rows)
    for level in range(3):
        step = 1 << level
        low = (group >> level) % 2 == 0
        for r in range(GROUPS):
            if (r >> level) % 2 == 0:
                first, second = rows[r], rows[r + step]
                rows[r] = jnp.where(low, first, pltpu.roll(second, width * step, 1))
                rows[r + step] = jnp.where(low, pltpu.roll(first, LANES - width * step, 1), second)
    return rows


def spread_matrix(nodes, probes, parts):
    row = lax.broadcasted_iota(jnp.int32, (nodes * parts, nodes * probes), 0) % nodes
    column = lax.broadcasted_iota(jnp.int32, (nodes * parts, nodes * probes), 1) // probes
    return (row == column).astype(jnp.bfloat16)


def three_terms(value):
    high = value.astype(jnp.bfloat16)
    rest = value - high.astype(jnp.float32)
    mid = rest.astype(jnp.bfloat16)
    low = (rest - mid.astype(jnp.float32)).astype(jnp.bfloat16)
    return jnp.concatenate([high, mid, low], axis=1)


def spread(value, matrix):
    return jnp.dot(three_terms(value), matrix, preferred_element_type=jnp.float32)


def load_tile(ref, block, blocks, size, tile):
    return ref[tile, pl.ds(block, size, stride=blocks), :]


def turn_kernel(dims, shared_ref, z_ref, turned_ref, outgoing_ref, stage):
    days, blocks, size, probes = dims
    for tile in range(days // GROUPS):
        for part in range(size // GROUPS):
            lanes = pl.ds(part * LANES, LANES)
            rows = [z_ref[tile * GROUPS + r, :, lanes].astype(jnp.float32) for r in range(GROUPS)]
            for i, row in enumerate(swap_groups(rows, probes)):
                stage[tile, pl.ds((part * GROUPS + i) * blocks, blocks), :] = row
    for block in range(blocks):
        for tile in range(days // GROUPS):
            value = load_tile(stage, block, blocks, size, tile)
            turned_ref[block, :, pl.ds(tile * LANES, LANES)] = value.astype(jnp.bfloat16)
    for m in range(outgoing_ref.shape[0]):
        outgoing_ref[m] = turned_ref[shared_ref[0, m]]


def local_kernel(dims, links_ref, days_ref, turned_ref, weight_ref, retention_ref, running_ref, retain_ref, product_ref):
    days, blocks, size, probes = dims
    count = links_ref.shape[1]
    for block in range(blocks):
        near = jnp.concatenate([turned_ref[links_ref[block, k]] for k in range(count)], axis=0)
        total = jnp.dot(weight_ref[block], near, preferred_element_type=jnp.float32)
        running_ref[block] = turned_ref[block].astype(jnp.float32) - total
    matrix = spread_matrix(size, probes, 3)
    observed = days_ref[0]
    rows = GROUPS * blocks
    for tile in range(days // GROUPS):
        day = lax.broadcasted_iota(jnp.int32, (rows, size), 0) // blocks + tile * GROUPS
        value = jnp.where(day < observed, retention_ref[pl.ds(tile * rows, rows), :], 1.0)
        wide = spread(value, matrix)
        retain_ref[pl.ds(tile * GROUPS, GROUPS)] = wide.reshape(GROUPS, blocks, size * probes)
    product = jnp.ones((blocks, size), jnp.float32)
    for day in range(days):
        factor = retention_ref[pl.ds(day * blocks, blocks), :]
        product = product * jnp.where(day < observed, factor, 1.0)
    product_ref[...] = jnp.concatenate([product, jnp.zeros((blocks, LANES - size), jnp.float32)], axis=1)


def forward_kernel(
    dims, links_ref, days_ref, running_ref, remote_ref, weight_ref, inverse_ref, retain_ref, product_ref,
    forcing_ref, message_ref, stage,
):
    days, blocks, size, probes = dims
    count = links_ref.shape[1]
    for block in range(blocks):
        far = jnp.concatenate([remote_ref[links_ref[block, k]] for k in range(count)], axis=0)
        total = jnp.dot(weight_ref[block], far, preferred_element_type=jnp.float32)
        source = (running_ref[block] - total).astype(jnp.bfloat16)
        drive = jnp.dot(inverse_ref[block], source, preferred_element_type=jnp.float32)
        for tile in range(days // GROUPS):
            stage[tile, pl.ds(block, size, stride=blocks), :] = drive[:, tile * LANES : (tile + 1) * LANES]
    observed = days_ref[0]
    for part in range(size // GROUPS):
        lanes = pl.ds(part * LANES, LANES)
        state = jnp.zeros((blocks, LANES), jnp.float32)
        for tile in range(days // GROUPS):
            rows = [stage[tile, pl.ds((part * GROUPS + i) * blocks, blocks), :] for i in range(GROUPS)]
            for r, row in enumerate(swap_groups(rows, probes)):
                day = tile * GROUPS + r
                row = jnp.where(day < observed, row, 0.0)
                forcing_ref[day, :, lanes] = row
                state = retain_ref[day, :, lanes] * state + row
        message_ref[:, lanes] = state
    message_ref[:, pl.ds(size * probes, LANES)] = product_ref[...]


def carried(dims, message_refs):
    days, blocks, size, probes = dims
    matrix = spread_matrix(size, probes, 3)
    width = size * probes
    carry = message_refs[-1][:, pl.ds(0, width)]
    for ref in reversed(message_refs[:-1]):
        factor = spread(ref[:, pl.ds(width, LANES)][:, :size], matrix)
        carry = ref[:, pl.ds(0, width)] + factor * carry
    return carry


def adjoint_kernel(dims, hops, days_ref, forcing_ref, retain_ref, product_ref, inverse_ref, *rest):
    days, blocks, size, probes = dims
    message_refs = rest[:hops]
    adjoint_ref, message_ref, stage, enter = rest[hops:]
    enter[...] = carried(dims, message_refs)
    observed = days_ref[0]
    for part in range(size // GROUPS):
        lanes = pl.ds(part * LANES, LANES)
        state = enter[:, lanes]
        for tile in range(days // GROUPS):
            rows = []
            for r in range(GROUPS):
                day = tile * GROUPS + r
                state = retain_ref[day, :, lanes] * state + forcing_ref[day, :, lanes]
                rows.append(state)
            for i, row in enumerate(swap_groups(rows, probes)):
                stage[tile, pl.ds((part * GROUPS + i) * blocks, blocks), :] = row
    for block in range(blocks):
        stored = jnp.concatenate(
            [load_tile(stage, block, blocks, size, tile).astype(jnp.bfloat16) for tile in range(days // GROUPS)], axis=1
        )
        adjoint = jnp.dot(inverse_ref[block], stored, preferred_element_type=jnp.float32)
        for tile in range(days // GROUPS):
            stage[tile, pl.ds(block, size, stride=blocks), :] = adjoint[:, tile * LANES : (tile + 1) * LANES]
    for part in range(size // GROUPS):
        lanes = pl.ds(part * LANES, LANES)
        carry = jnp.zeros((blocks, LANES), jnp.float32)
        for tile in reversed(range(days // GROUPS)):
            rows = [stage[tile, pl.ds((part * GROUPS + i) * blocks, blocks), :] for i in range(GROUPS)]
            rows = swap_groups(rows, probes)
            for r in reversed(range(GROUPS)):
                day = tile * GROUPS + r
                row = jnp.where(day < observed, rows[r], 0.0)
                adjoint_ref[day, :, lanes] = row
                carry = retain_ref[day, :, lanes] * (row + carry)
        message_ref[:, lanes] = carry
    message_ref[:, pl.ds(size * probes, LANES)] = product_ref[...]


def variance_kernel(dims, hops, adjoint_ref, retain_ref, z_ref, *rest):
    days, blocks, size, probes = dims
    message_refs = rest[:hops]
    out_ref, stage, enter = rest[hops:]
    enter[...] = carried(dims, message_refs)
    width = size * probes
    for part in range(size // GROUPS):
        lanes = pl.ds(part * LANES, LANES)
        carry = enter[:, lanes]
        for day in reversed(range(days)):
            smoothed = adjoint_ref[day, :, lanes] + carry
            carry = retain_ref[day, :, lanes] * smoothed
            stage[pl.ds(day * blocks, blocks), lanes] = smoothed * z_ref[day, :, lanes].astype(jnp.float32)
    row = lax.broadcasted_iota(jnp.int32, (width, size), 0) // probes
    column = lax.broadcasted_iota(jnp.int32, (width, size), 1)
    gather = (row == column).astype(jnp.bfloat16)
    rows = GROUPS * blocks
    for tile in range(days // GROUPS):
        value = stage[pl.ds(tile * rows, rows), :]
        high = value.astype(jnp.bfloat16)
        low = (value - high.astype(jnp.float32)).astype(jnp.bfloat16)
        total = jnp.dot(high, gather, preferred_element_type=jnp.float32)
        total = total + jnp.dot(low, gather, preferred_element_type=jnp.float32)
        out_ref[pl.ds(tile * rows, rows), :] = total * (1.0 / probes)


def call(kernel, outs, scratch, flops, moved, scalars, *operands):
    in_specs = [
        pl.BlockSpec(memory_space=pltpu.SMEM if i < scalars else pltpu.VMEM) for i in range(len(operands))
    ]
    return pl.pallas_call(
        kernel,
        out_shape=[jax.ShapeDtypeStruct(shape, kind) for shape, kind in outs],
        in_specs=in_specs,
        out_specs=[pl.BlockSpec(memory_space=pltpu.VMEM) for _ in outs],
        scratch_shapes=scratch,
        compiler_params=pltpu.CompilerParams(vmem_limit_bytes=VMEM_LIMIT),
        cost_estimate=pl.CostEstimate(flops=flops, bytes_accessed=moved, transcendentals=0),
    )(*operands)


def shifted(block, axis, distance):
    count = lax.axis_size(axis)
    route = [(i, i + distance) for i in range(count) if 0 <= i + distance < count]
    return lax.ppermute(block, axis, route)


def local(
    probes,
    local_links,
    remote_links,
    shared_blocks,
    slab_days,
    local_coupling,
    remote_coupling,
    block_inverse,
    retention,
):
    days, blocks, width = probes.shape
    size = block_inverse.shape[1]
    count = width // size
    dims = (days, blocks, size, count)
    columns = days * count
    f32, bf16 = jnp.float32, jnp.bfloat16
    stage = pltpu.VMEM((days // GROUPS, size * blocks, LANES), f32)
    bound = shared_blocks.shape[1]
    near = local_links.shape[1]
    far = remote_links.shape[1]
    tm_count = lax.axis_size("tm")
    hops = tm_count - 1
    local_weight = local_coupling.transpose(0, 2, 1, 3).reshape(blocks, size, near * size)
    remote_weight = remote_coupling.transpose(0, 2, 1, 3).reshape(blocks, size, far * size)
    retention_rows = retention.reshape(days * blocks, size)
    inverse_turned = block_inverse.transpose(0, 2, 1)

    turned, outgoing = call(
        functools.partial(turn_kernel, dims),
        [((blocks, size, columns), bf16), ((bound, size, columns), bf16)],
        [stage], 10**7, 4 * 10**6, 1, shared_blocks, probes,
    )
    remote = lax.all_gather(outgoing, "space", axis=0, tiled=True)
    running, retain, product = call(
        functools.partial(local_kernel, dims),
        [((blocks, size, columns), f32), ((days, blocks, width), f32), ((blocks, LANES), f32)],
        [], 10**9, 10**7, 2, local_links, slab_days, turned, local_weight, retention_rows,
    )
    message_shape = ((blocks, width + LANES), f32)
    forcing, message = call(
        functools.partial(forward_kernel, dims),
        [((days, blocks, width), f32), message_shape],
        [stage], 10**9, 10**7, 2,
        remote_links, slab_days, running, remote, remote_weight, block_inverse, retain, product,
    )
    received = [shifted(message, "tm", distance) for distance in range(1, tm_count)]
    adjoint, message = call(
        functools.partial(adjoint_kernel, dims, hops),
        [((days, blocks, width), f32), message_shape],
        [stage, pltpu.VMEM((blocks, width), f32)], 10**9, 10**7, 1,
        slab_days, forcing, retain, product, inverse_turned, *received,
    )
    received = [shifted(message, "tm", -distance) for distance in range(1, tm_count)]
    (variance,) = call(
        functools.partial(variance_kernel, dims, hops),
        [((days * blocks, size), f32)],
        [pltpu.VMEM((days * blocks, width), f32), pltpu.VMEM((blocks, width), f32)], 10**9, 10**7, 0,
        adjoint, retain, probes, *received,
    )
    return variance.reshape(days, -1)


def solution(mesh):
    placed = (
        P("tm", "space", None),
        P("space", None),
        P("space", None),
        P("space", None),
        P("tm"),
        P("space", None, None, None),
        P("space", None, None, None),
        P("space", None, None),
        P("tm", "space"),
    )
    return jax.shard_map(
        local, mesh=mesh, in_specs=placed, out_specs=P("tm", "space"), check_vma=False
    )
```

```python
import functools

import jax
import jax.numpy as jnp
from jax import lax
from jax.experimental import pallas as pl
from jax.experimental.pallas import tpu as pltpu
from jax.sharding import PartitionSpec as P

LANES = 128
VMEM_LIMIT = 56 * 1024 * 1024
TURNED = (((1,), (1,)), ((), ()))


def permutation(size, probes, start, width):
    total = size * probes
    column = lax.broadcasted_iota(jnp.int32, (total, width), 1) + start
    origin = (column % size) * probes + column // size
    row = lax.broadcasted_iota(jnp.int32, (total, width), 0)
    return (row == origin).astype(jnp.float32).astype(jnp.bfloat16)


def doubled(weight, size):
    wide = weight.astype(jnp.float32)
    return jnp.concatenate([wide, pltpu.roll(wide, size, 1)], axis=0).astype(jnp.bfloat16)


def outgoing_kernel(dims, shared_ref, z_ref, outgoing_ref):
    days, blocks, size, probes = dims
    count = outgoing_ref.shape[0]
    z = z_ref[...].reshape(days * blocks, size * probes)
    row = lax.broadcasted_iota(jnp.int32, (days, days * blocks), 0)
    column = lax.broadcasted_iota(jnp.int32, (days, days * blocks), 1)
    picks = [
        (column == row * blocks + shared_ref[0, m]).astype(jnp.float32).astype(jnp.bfloat16) for m in range(count)
    ]
    picked = jnp.dot(jnp.concatenate(picks, axis=0), z, preferred_element_type=jnp.float32).astype(jnp.bfloat16)
    step = 2 * LANES
    for start in range(0, size * probes, step):
        moved = jnp.dot(picked, permutation(size, probes, start, step), preferred_element_type=jnp.float32)
        moved = moved.astype(jnp.bfloat16)
        for half in range(2):
            pair = start // LANES + half
            for m in range(count):
                outgoing_ref[m, pl.ds(pair * days, days), :] = moved[
                    m * days : (m + 1) * days, half * LANES : (half + 1) * LANES
                ]


def local_kernel(
    dims, links_ref, days_ref, z_ref, weight_ref, retention_ref, running_ref, moved_ref, retain_ref, product_ref, stage, turned
):
    days, blocks, size, probes = dims
    pairs = size * probes // LANES
    count = links_ref.shape[1]
    z = z_ref[...].reshape(days * blocks, size * probes)
    step = 2 * LANES
    for start in range(0, size * probes, step):
        moved = jnp.dot(z, permutation(size, probes, start, step), preferred_element_type=jnp.float32)
        for half in range(2):
            pair = start // LANES + half
            stage[pair] = moved[:, half * LANES : (half + 1) * LANES]
            moved_ref[pair] = moved[:, half * LANES : (half + 1) * LANES].astype(jnp.bfloat16)
    for block in range(blocks):
        for pair in range(pairs):
            rows = stage[pair, pl.ds(block, days, stride=blocks), :]
            turned[block, pl.ds(pair * days, days), :] = rows.astype(jnp.bfloat16)
    for block in range(blocks):
        near = jnp.concatenate([turned[links_ref[block, k]] for k in range(count)], axis=1)
        weight = jnp.concatenate([doubled(weight_ref[block, k], size) for k in range(count)], axis=1)
        total = lax.dot_general(near, weight, TURNED, preferred_element_type=jnp.float32)
        running_ref[block] = turned[block].astype(jnp.float32) - total
    observed = days_ref[0]
    product = jnp.ones((blocks, LANES), jnp.float32)
    for day in range(days):
        factor = retention_ref[pl.ds(day * blocks, blocks), :]
        factor = jnp.where(day < observed, factor, 1.0)
        retain_ref[day] = factor
        product = product * factor
    product_ref[...] = product


def forward_kernel(
    dims, links_ref, days_ref, running_ref, remote_ref, weight_ref, inverse_ref, retain_ref, product_ref,
    forcing_ref, message_ref,
):
    days, blocks, size, probes = dims
    pairs = size * probes // LANES
    count = links_ref.shape[1]
    for block in range(blocks):
        far = jnp.concatenate([remote_ref[links_ref[block, k]] for k in range(count)], axis=1)
        weight = jnp.concatenate([doubled(weight_ref[block, k], size) for k in range(count)], axis=1)
        total = lax.dot_general(far, weight, TURNED, preferred_element_type=jnp.float32)
        source = (running_ref[block] - total).astype(jnp.bfloat16)
        inverse = doubled(inverse_ref[block], size)
        drive = lax.dot_general(source, inverse, TURNED, preferred_element_type=jnp.float32)
        for pair in range(pairs):
            forcing_ref[pair, pl.ds(block, days, stride=blocks), :] = drive[pair * days : (pair + 1) * days]
    observed = days_ref[0]
    states = [jnp.zeros((blocks, LANES), jnp.float32)] * pairs
    for day in range(days):
        factor = retain_ref[day]
        rows = pl.ds(day * blocks, blocks)
        for pair in range(pairs):
            drive = jnp.where(day < observed, forcing_ref[pair, rows, :], 0.0)
            states[pair] = factor * states[pair] + drive
    for pair in range(pairs):
        message_ref[pair] = states[pair]
    message_ref[pairs] = product_ref[...]


def carried(pairs, message_refs):
    carries = [message_refs[-1][pair] for pair in range(pairs)]
    for ref in reversed(message_refs[:-1]):
        factor = ref[pairs]
        carries = [ref[pair] + factor * carries[pair] for pair in range(pairs)]
    return carries


def adjoint_kernel(dims, hops, days_ref, forcing_ref, retain_ref, product_ref, inverse_ref, *rest):
    days, blocks, size, probes = dims
    pairs = size * probes // LANES
    message_refs = rest[:hops]
    adjoint_ref, message_ref, stage = rest[hops:]
    observed = days_ref[0]
    states = carried(pairs, message_refs)
    for day in range(days):
        factor = retain_ref[day]
        rows = pl.ds(day * blocks, blocks)
        for pair in range(pairs):
            drive = jnp.where(day < observed, forcing_ref[pair, rows, :], 0.0)
            states[pair] = factor * states[pair] + drive
            stage[pair, rows, :] = states[pair]
    for block in range(blocks):
        stored = jnp.concatenate(
            [stage[pair, pl.ds(block, days, stride=blocks), :].astype(jnp.bfloat16) for pair in range(pairs)], axis=0
        )
        inverse = doubled(inverse_ref[block], size)
        adjoint = jnp.dot(stored, inverse, preferred_element_type=jnp.float32)
        for pair in range(pairs):
            adjoint_ref[pair, pl.ds(block, days, stride=blocks), :] = adjoint[pair * days : (pair + 1) * days]
    carries = [jnp.zeros((blocks, LANES), jnp.float32)] * pairs
    for day in reversed(range(days)):
        factor = retain_ref[day]
        rows = pl.ds(day * blocks, blocks)
        for pair in range(pairs):
            value = jnp.where(day < observed, adjoint_ref[pair, rows, :], 0.0)
            carries[pair] = factor * (value + carries[pair])
    for pair in range(pairs):
        message_ref[pair] = carries[pair]
    message_ref[pairs] = product_ref[...]


def variance_kernel(dims, hops, days_ref, adjoint_ref, retain_ref, moved_ref, *rest):
    days, blocks, size, probes = dims
    pairs = size * probes // LANES
    message_refs = rest[:hops]
    out_ref, stage = rest[hops:]
    observed = days_ref[0]
    carries = carried(pairs, message_refs)
    for day in reversed(range(days)):
        factor = retain_ref[day]
        rows = pl.ds(day * blocks, blocks)
        total = None
        for pair in range(pairs):
            smoothed = jnp.where(day < observed, adjoint_ref[pair, rows, :], 0.0) + carries[pair]
            carries[pair] = factor * smoothed
            term = smoothed * moved_ref[pair, rows, :].astype(jnp.float32)
            total = term if total is None else total + term
        stage[rows, :] = total
    lane = lax.broadcasted_iota(jnp.int32, (days, LANES), 1)
    for block in range(0, blocks, 2):
        both = [stage[pl.ds(block + half, days, stride=blocks), :] for half in range(2)]
        both = [value + pltpu.roll(value, size, 1) for value in both]
        out_ref[:, pl.ds(block * size, LANES)] = jnp.where(lane < size, both[0], both[1]) * (1.0 / probes)


def call(kernel, outs, scratch, flops, moved, scalars, *operands):
    in_specs = [
        pl.BlockSpec(memory_space=pltpu.SMEM if i < scalars else pltpu.VMEM) for i in range(len(operands))
    ]
    return pl.pallas_call(
        kernel,
        out_shape=[jax.ShapeDtypeStruct(shape, kind) for shape, kind in outs],
        in_specs=in_specs,
        out_specs=[pl.BlockSpec(memory_space=pltpu.VMEM) for _ in outs],
        scratch_shapes=scratch,
        compiler_params=pltpu.CompilerParams(vmem_limit_bytes=VMEM_LIMIT),
        cost_estimate=pl.CostEstimate(flops=flops, bytes_accessed=moved, transcendentals=0),
    )(*operands)


def shifted(block, axis, distance):
    count = lax.axis_size(axis)
    route = [(i, i + distance) for i in range(count) if 0 <= i + distance < count]
    return lax.ppermute(block, axis, route)


def local(
    probes,
    local_links,
    remote_links,
    shared_blocks,
    slab_days,
    local_coupling,
    remote_coupling,
    block_inverse,
    retention,
):
    days, blocks, width = probes.shape
    size = block_inverse.shape[1]
    dims = (days, blocks, size, width // size)
    pairs = width // LANES
    f32, bf16 = jnp.float32, jnp.bfloat16
    bound = shared_blocks.shape[1]
    tm_count = lax.axis_size("tm")
    hops = tm_count - 1
    rows = days * blocks
    padded = lambda weight: jnp.pad(weight, [(0, 0)] * (weight.ndim - 1) + [(0, LANES - size)])
    retention_rows = retention.reshape(rows, size)
    retention_rows = jnp.concatenate([retention_rows, retention_rows], axis=1)
    inverse = padded(block_inverse)

    (outgoing,) = call(
        functools.partial(outgoing_kernel, dims),
        [((bound, pairs * days, LANES), bf16)],
        [], 10**7, 4 * 10**6, 1, shared_blocks, probes,
    )
    remote = lax.all_gather(outgoing, "space", axis=0, tiled=True)
    running, moved, retain, product = call(
        functools.partial(local_kernel, dims),
        [
            ((blocks, pairs * days, LANES), f32),
            ((pairs, rows, LANES), bf16),
            ((days, blocks, LANES), f32),
            ((blocks, LANES), f32),
        ],
        [pltpu.VMEM((pairs, rows, LANES), f32), pltpu.VMEM((blocks, pairs * days, LANES), bf16)],
        10**9, 10**7, 2, local_links, slab_days, probes, padded(local_coupling), retention_rows,
    )
    message_shape = ((pairs + 1, blocks, LANES), f32)
    forcing, message = call(
        functools.partial(forward_kernel, dims),
        [((pairs, rows, LANES), f32), message_shape],
        [], 10**9, 10**7, 2,
        remote_links, slab_days, running, remote, padded(remote_coupling), inverse, retain, product,
    )
    received = [shifted(message, "tm", distance) for distance in range(1, tm_count)]
    adjoint, message = call(
        functools.partial(adjoint_kernel, dims, hops),
        [((pairs, rows, LANES), f32), message_shape],
        [pltpu.VMEM((pairs, rows, LANES), f32)], 10**9, 10**7, 1,
        slab_days, forcing, retain, product, inverse, *received,
    )
    received = [shifted(message, "tm", -distance) for distance in range(1, tm_count)]
    (variance,) = call(
        functools.partial(variance_kernel, dims, hops),
        [((days, blocks * size), f32)],
        [pltpu.VMEM((rows, LANES), f32)], 10**9, 10**7, 1,
        slab_days, adjoint, retain, moved, *received,
    )
    return variance


def solution(mesh):
    placed = (
        P("tm", "space", None),
        P("space", None),
        P("space", None),
        P("space", None),
        P("tm"),
        P("space", None, None, None),
        P("space", None, None, None),
        P("space", None, None),
        P("tm", "space"),
    )
    return jax.shard_map(
        local, mesh=mesh, in_specs=placed, out_specs=P("tm", "space"), check_vma=False
    )
```

```python
import functools

import jax
import jax.numpy as jnp
from jax import lax
from jax.experimental import pallas as pl
from jax.experimental.pallas import tpu as pltpu
from jax.sharding import PartitionSpec as P

LANES = 128
VMEM_LIMIT = 20 * 1024 * 1024
CHUNKS = 2
TURNED = (((1,), (1,)), ((), ()))


def permutation(size, probes, start, width):
    total = size * probes
    column = lax.broadcasted_iota(jnp.int32, (total, width), 1) + start
    origin = (column % size) * probes + column // size
    row = lax.broadcasted_iota(jnp.int32, (total, width), 0)
    return (row == origin).astype(jnp.float32).astype(jnp.bfloat16)


def doubled(weight):
    zero = jnp.zeros_like(weight)
    return jnp.concatenate(
        [jnp.concatenate([weight, zero], axis=1), jnp.concatenate([zero, weight], axis=1)], axis=0
    )


def outgoing_kernel(dims, shared_ref, z_ref, *outgoing_refs):
    days, blocks, size, probes = dims
    count = outgoing_refs[0].shape[0]
    per_chunk = size * probes // LANES // len(outgoing_refs)
    z = z_ref[...].reshape(days * blocks, size * probes)
    row = lax.broadcasted_iota(jnp.int32, (days, days * blocks), 0)
    column = lax.broadcasted_iota(jnp.int32, (days, days * blocks), 1)
    picks = [
        (column == row * blocks + shared_ref[0, m]).astype(jnp.float32).astype(jnp.bfloat16) for m in range(count)
    ]
    picked = jnp.dot(jnp.concatenate(picks, axis=0), z, preferred_element_type=jnp.float32).astype(jnp.bfloat16)
    step = 2 * LANES
    for start in range(0, size * probes, step):
        moved = jnp.dot(picked, permutation(size, probes, start, step), preferred_element_type=jnp.float32)
        moved = moved.astype(jnp.bfloat16)
        for half in range(2):
            pair = start // LANES + half
            for m in range(count):
                outgoing_refs[pair // per_chunk][m, pl.ds(pair % per_chunk * days, days), :] = moved[
                    m * days : (m + 1) * days, half * LANES : (half + 1) * LANES
                ]


def local_kernel(
    dims, chunks, links_ref, days_ref, z_ref, weight_ref, remote_weight_ref, inverse_ref, retention_ref, *rest
):
    days, blocks, size, probes = dims
    pairs = size * probes // LANES
    per_chunk = pairs // chunks
    running_refs, moved_refs = rest[:chunks], rest[chunks : 2 * chunks]
    retain_ref, product_ref, remote_doubled_ref, inverse_doubled_ref, stage, turned = rest[2 * chunks :]
    count = links_ref.shape[0]
    z = z_ref[...].reshape(days * blocks, size * probes)
    step = 2 * LANES
    for start in range(0, size * probes, step):
        moved = jnp.dot(z, permutation(size, probes, start, step), preferred_element_type=jnp.float32)
        for half in range(2):
            pair = start // LANES + half
            tile = moved[:, half * LANES : (half + 1) * LANES]
            stage[pair] = tile
            moved_refs[pair // per_chunk][pair % per_chunk] = tile.astype(jnp.bfloat16)
    for block in range(blocks):
        for pair in range(pairs):
            rows = stage[pair, pl.ds(block, days, stride=blocks), :]
            turned[block, pl.ds(pair * days, days), :] = rows.astype(jnp.bfloat16)
    for block in range(blocks):
        near = jnp.concatenate([turned[links_ref[k, block]] for k in range(count)], axis=1)
        weight = jnp.concatenate([doubled(weight_ref[block, k]) for k in range(count)], axis=1)
        total = lax.dot_general(near, weight, TURNED, preferred_element_type=jnp.float32)
        running = turned[block].astype(jnp.float32) - total
        for chunk in range(chunks):
            part = per_chunk * days
            running_refs[chunk][block] = running[chunk * part : (chunk + 1) * part]
        remote_doubled_ref[block] = jnp.concatenate(
            [doubled(remote_weight_ref[block, k]) for k in range(remote_weight_ref.shape[1])], axis=1
        )
        inverse_doubled_ref[block] = doubled(inverse_ref[block])
    observed = days_ref[0]
    shape = (days, LANES)
    first = lax.broadcasted_iota(jnp.int32, shape, 1) < size
    seen = lax.broadcasted_iota(jnp.int32, shape, 0) < observed
    for block in range(0, blocks, 2):
        factor = jnp.where(seen, retention_ref[:, pl.ds(block * size, LANES)], 1.0)
        other = pltpu.roll(factor, size, 1)
        retain_ref[pl.ds(block, days, stride=blocks), :] = jnp.where(first, factor, other)
        retain_ref[pl.ds(block + 1, days, stride=blocks), :] = jnp.where(first, other, factor)
    product = jnp.ones((blocks, LANES), jnp.float32)
    for day in range(days):
        product = product * retain_ref[pl.ds(day * blocks, blocks), :]
    high = product.astype(jnp.bfloat16)
    product_ref[0] = high
    product_ref[1] = (product - high.astype(jnp.float32)).astype(jnp.bfloat16)


def forward_kernel(
    dims, links_ref, days_ref, running_ref, remote_ref, weight_ref, inverse_ref, retain_ref, product_ref,
    forcing_ref, message_ref,
):
    days, blocks, size, probes = dims
    pairs = forcing_ref.shape[0]
    count = links_ref.shape[0]
    seen = lax.broadcasted_iota(jnp.int32, (days, LANES), 0) < days_ref[0]
    for block in range(blocks):
        far = jnp.concatenate([remote_ref[links_ref[k, block]] for k in range(count)], axis=1)
        total = lax.dot_general(far, weight_ref[block], TURNED, preferred_element_type=jnp.float32)
        source = (running_ref[block] - total).astype(jnp.bfloat16)
        drive = lax.dot_general(source, inverse_ref[block], TURNED, preferred_element_type=jnp.float32)
        for pair in range(pairs):
            forcing_ref[pair, pl.ds(block, days, stride=blocks), :] = jnp.where(
                seen, drive[pair * days : (pair + 1) * days], 0.0
            )
    states = [jnp.zeros((blocks, LANES), jnp.float32)] * pairs
    for day in range(days):
        rows = pl.ds(day * blocks, blocks)
        factor = retain_ref[rows, :]
        for pair in range(pairs):
            states[pair] = factor * states[pair] + forcing_ref[pair, rows, :]
    leave(message_ref, states, product_ref)


def leave(message_ref, values, product_ref):
    for pair, value in enumerate(values):
        message_ref[pair] = value.astype(jnp.bfloat16)
    message_ref[len(values)] = product_ref[0]
    message_ref[len(values) + 1] = product_ref[1]


def carried(pairs, message_refs):
    carries = [message_refs[-1][pair].astype(jnp.float32) for pair in range(pairs)]
    for ref in reversed(message_refs[:-1]):
        factor = ref[pairs].astype(jnp.float32) + ref[pairs + 1].astype(jnp.float32)
        carries = [ref[pair].astype(jnp.float32) + factor * carries[pair] for pair in range(pairs)]
    return carries


def adjoint_kernel(dims, hops, days_ref, forcing_ref, retain_ref, product_ref, inverse_ref, *rest):
    days, blocks, size, probes = dims
    pairs = forcing_ref.shape[0]
    message_refs = rest[:hops]
    adjoint_ref, message_ref, stage = rest[hops:]
    seen = lax.broadcasted_iota(jnp.int32, (days, LANES), 0) < days_ref[0]
    states = carried(pairs, message_refs)
    for day in range(days):
        rows = pl.ds(day * blocks, blocks)
        factor = retain_ref[rows, :]
        for pair in range(pairs):
            states[pair] = factor * states[pair] + forcing_ref[pair, rows, :]
            stage[pair, rows, :] = states[pair]
    for block in range(blocks):
        stored = jnp.concatenate(
            [stage[pair, pl.ds(block, days, stride=blocks), :].astype(jnp.bfloat16) for pair in range(pairs)], axis=0
        )
        adjoint = jnp.dot(stored, inverse_ref[block], preferred_element_type=jnp.float32)
        for pair in range(pairs):
            adjoint_ref[pair, pl.ds(block, days, stride=blocks), :] = jnp.where(
                seen, adjoint[pair * days : (pair + 1) * days], 0.0
            )
    carries = [jnp.zeros((blocks, LANES), jnp.float32)] * pairs
    for day in reversed(range(days)):
        rows = pl.ds(day * blocks, blocks)
        factor = retain_ref[rows, :]
        for pair in range(pairs):
            carries[pair] = factor * (adjoint_ref[pair, rows, :] + carries[pair])
    leave(message_ref, carries, product_ref)


def variance_kernel(dims, hops, last, first, adjoint_ref, retain_ref, moved_ref, *rest):
    days, blocks, size, probes = dims
    pairs = adjoint_ref.shape[0]
    message_refs = rest[:hops]
    rest = rest[hops:]
    if not first:
        partial_ref, rest = rest[0], rest[1:]
    out_ref = rest[0]
    stage = rest[1] if last else out_ref
    carries = carried(pairs, message_refs)
    for day in reversed(range(days)):
        rows = pl.ds(day * blocks, blocks)
        factor = retain_ref[rows, :]
        total = None if first else partial_ref[rows, :]
        for pair in range(pairs):
            smoothed = adjoint_ref[pair, rows, :] + carries[pair]
            carries[pair] = factor * smoothed
            term = smoothed * moved_ref[pair, rows, :].astype(jnp.float32)
            total = term if total is None else total + term
        stage[rows, :] = total
    if last:
        lane = lax.broadcasted_iota(jnp.int32, (days, LANES), 1)
        for block in range(0, blocks, 2):
            both = [stage[pl.ds(block + half, days, stride=blocks), :] for half in range(2)]
            both = [value + pltpu.roll(value, size, 1) for value in both]
            out_ref[:, pl.ds(block * size, LANES)] = jnp.where(lane < size, both[0], both[1]) * (1.0 / probes)


def call(kernel, outs, scratch, flops, moved, scalars, *operands):
    in_specs = [
        pl.BlockSpec(memory_space=pltpu.SMEM if i < scalars else pltpu.VMEM) for i in range(len(operands))
    ]
    return pl.pallas_call(
        kernel,
        out_shape=[jax.ShapeDtypeStruct(shape, kind) for shape, kind in outs],
        in_specs=in_specs,
        out_specs=[pl.BlockSpec(memory_space=pltpu.VMEM) for _ in outs],
        scratch_shapes=scratch,
        compiler_params=pltpu.CompilerParams(vmem_limit_bytes=VMEM_LIMIT),
        cost_estimate=pl.CostEstimate(flops=flops, bytes_accessed=moved, transcendentals=0),
    )(*operands)


def shifted(block, axis, distance):
    count = lax.axis_size(axis)
    route = [(i, i + distance) for i in range(count) if 0 <= i + distance < count]
    return lax.ppermute(block, axis, route)


def local(
    probes,
    local_links,
    remote_links,
    shared_blocks,
    slab_days,
    local_coupling,
    remote_coupling,
    block_inverse,
    retention,
):
    days, blocks, width = probes.shape
    size = block_inverse.shape[1]
    dims = (days, blocks, size, width // size)
    pairs = width // LANES
    per_chunk = pairs // CHUNKS
    f32, bf16 = jnp.float32, jnp.bfloat16
    bound = shared_blocks.shape[1]
    far = remote_links.shape[1]
    tm_count = lax.axis_size("tm")
    hops = tm_count - 1
    rows = days * blocks
    near_table, far_table = local_links.T, remote_links.T

    outgoing = call(
        functools.partial(outgoing_kernel, dims),
        [((bound, per_chunk * days, LANES), bf16)] * CHUNKS,
        [], 10**9, 4 * 10**6, 1, shared_blocks, probes,
    )
    remote = [lax.all_gather(part, "space", axis=0, tiled=True) for part in outgoing]
    results = call(
        functools.partial(local_kernel, dims, CHUNKS),
        [((blocks, per_chunk * days, LANES), f32)] * CHUNKS
        + [((per_chunk, rows, LANES), bf16)] * CHUNKS
        + [
            ((rows, LANES), f32),
            ((2, blocks, LANES), bf16),
            ((blocks, LANES, far * LANES), bf16),
            ((blocks, LANES, LANES), bf16),
        ],
        [pltpu.VMEM((pairs, rows, LANES), f32), pltpu.VMEM((blocks, pairs * days, LANES), bf16)],
        10**10, 10**7, 2,
        near_table, slab_days, probes, local_coupling, remote_coupling, block_inverse, retention,
    )
    running, moved = results[:CHUNKS], results[CHUNKS : 2 * CHUNKS]
    retain, product, remote_weight, inverse = results[2 * CHUNKS :]
    message_shape = ((per_chunk + 2, blocks, LANES), bf16)
    partial = None
    for chunk in range(CHUNKS):
        forcing, message = call(
            functools.partial(forward_kernel, dims),
            [((per_chunk, rows, LANES), f32), message_shape],
            [], 10**10 // CHUNKS, 10**7 // CHUNKS, 2,
            far_table, slab_days, running[chunk], remote[chunk], remote_weight, inverse, retain, product,
        )
        received = [shifted(message, "tm", distance) for distance in range(1, tm_count)]
        adjoint, message = call(
            functools.partial(adjoint_kernel, dims, hops),
            [((per_chunk, rows, LANES), f32), message_shape],
            [pltpu.VMEM((per_chunk, rows, LANES), f32)], 10**10 // CHUNKS, 10**7 // CHUNKS, 1,
            slab_days, forcing, retain, product, inverse, *received,
        )
        received = [shifted(message, "tm", -distance) for distance in range(1, tm_count)]
        first, last = chunk == 0, chunk == CHUNKS - 1
        (partial,) = call(
            functools.partial(variance_kernel, dims, hops, last, first),
            [((days, blocks * size), f32) if last else ((rows, LANES), f32)],
            [pltpu.VMEM((rows, LANES), f32)] if last else [], 10**10 // CHUNKS, 10**7 // CHUNKS, 0,
            adjoint, retain, moved[chunk], *received, *([] if first else [partial]),
        )
    return partial


def solution(mesh):
    placed = (
        P("tm", "space", None),
        P("space", None),
        P("space", None),
        P("space", None),
        P("tm"),
        P("space", None, None, None),
        P("space", None, None, None),
        P("space", None, None),
        P("tm", "space"),
    )
    return jax.shard_map(
        local, mesh=mesh, in_specs=placed, out_specs=P("tm", "space"), check_vma=False
    )
```

```python
import functools

import jax
import jax.numpy as jnp
from jax import lax
from jax.experimental import pallas as pl
from jax.experimental.pallas import tpu as pltpu
from jax.sharding import PartitionSpec as P

LANES = 128
VMEM_LIMIT = 20 * 1024 * 1024
TURNED = (((1,), (1,)), ((), ()))


def permutation(size, probes, start, width):
    total = size * probes
    column = lax.broadcasted_iota(jnp.int32, (total, width), 1) + start
    origin = (column % size) * probes + column // size
    row = lax.broadcasted_iota(jnp.int32, (total, width), 0)
    return (row == origin).astype(jnp.float32).astype(jnp.bfloat16)


def doubled(weight):
    zero = jnp.zeros_like(weight)
    return jnp.concatenate(
        [jnp.concatenate([weight, zero], axis=1), jnp.concatenate([zero, weight], axis=1)], axis=0
    )


def outgoing_kernel(dims, shared_ref, z_ref, outgoing_ref):
    days, blocks, size, probes = dims
    count = outgoing_ref.shape[0]
    z = z_ref[...].reshape(days * blocks, size * probes)
    row = lax.broadcasted_iota(jnp.int32, (days, days * blocks), 0)
    column = lax.broadcasted_iota(jnp.int32, (days, days * blocks), 1)
    picks = [
        (column == row * blocks + shared_ref[0, m]).astype(jnp.float32).astype(jnp.bfloat16) for m in range(count)
    ]
    picked = jnp.dot(jnp.concatenate(picks, axis=0), z, preferred_element_type=jnp.float32).astype(jnp.bfloat16)
    step = 2 * LANES
    for start in range(0, size * probes, step):
        moved = jnp.dot(picked, permutation(size, probes, start, step), preferred_element_type=jnp.float32)
        moved = moved.astype(jnp.bfloat16)
        for half in range(2):
            pair = start // LANES + half
            for m in range(count):
                outgoing_ref[m, pl.ds(pair * days, days), :] = moved[
                    m * days : (m + 1) * days, half * LANES : (half + 1) * LANES
                ]


def local_kernel(
    dims, links_ref, days_ref, z_ref, weight_ref, remote_weight_ref, inverse_ref, retention_ref,
    running_ref, moved_ref, retain_ref, product_ref, remote_doubled_ref, inverse_doubled_ref, stage, turned,
):
    days, blocks, size, probes = dims
    pairs = size * probes // LANES
    count = links_ref.shape[0]
    z = z_ref[...].reshape(days * blocks, size * probes)
    step = 2 * LANES
    for start in range(0, size * probes, step):
        moved = jnp.dot(z, permutation(size, probes, start, step), preferred_element_type=jnp.float32)
        for half in range(2):
            pair = start // LANES + half
            tile = moved[:, half * LANES : (half + 1) * LANES]
            stage[pair] = tile
            moved_ref[pair] = tile.astype(jnp.bfloat16)
    for block in range(blocks):
        for pair in range(pairs):
            rows = stage[pair, pl.ds(block, days, stride=blocks), :]
            turned[block, pl.ds(pair * days, days), :] = rows.astype(jnp.bfloat16)
    for block in range(blocks):
        near = jnp.concatenate([turned[links_ref[k, block]] for k in range(count)], axis=1)
        weight = jnp.concatenate([doubled(weight_ref[block, k]) for k in range(count)], axis=1)
        total = lax.dot_general(near, weight, TURNED, preferred_element_type=jnp.float32)
        running_ref[block] = turned[block].astype(jnp.float32) - total
        remote_doubled_ref[block] = jnp.concatenate(
            [doubled(remote_weight_ref[block, k]) for k in range(remote_weight_ref.shape[1])], axis=1
        )
        inverse_doubled_ref[block] = doubled(inverse_ref[block])
    observed = days_ref[0]
    shape = (days, LANES)
    first = lax.broadcasted_iota(jnp.int32, shape, 1) < size
    seen = lax.broadcasted_iota(jnp.int32, shape, 0) < observed
    for block in range(0, blocks, 2):
        factor = jnp.where(seen, retention_ref[:, pl.ds(block * size, LANES)], 1.0)
        other = pltpu.roll(factor, size, 1)
        retain_ref[pl.ds(block, days, stride=blocks), :] = jnp.where(first, factor, other)
        retain_ref[pl.ds(block + 1, days, stride=blocks), :] = jnp.where(first, other, factor)
    product = jnp.ones((blocks, LANES), jnp.float32)
    for day in range(days):
        product = product * retain_ref[pl.ds(day * blocks, blocks), :]
    high = product.astype(jnp.bfloat16)
    product_ref[0] = high
    product_ref[1] = (product - high.astype(jnp.float32)).astype(jnp.bfloat16)


def assemble_kernel(*refs):
    *piece_refs, product_ref, out_ref = refs
    count = piece_refs[0].shape[0]
    for i, ref in enumerate(piece_refs):
        out_ref[pl.ds(i * count, count)] = ref[...]


def forward_kernel(
    dims, links_ref, days_ref, running_ref, same_ref, other_ref, weight_ref, inverse_ref, retain_ref, product_ref,
    forcing_ref, message_ref, remote,
):
    days, blocks, size, probes = dims
    pairs = forcing_ref.shape[0]
    count = links_ref.shape[0]
    held = same_ref.shape[0]
    bound = 2 * held // lax.axis_size("space")
    me = lax.axis_index("space")
    remote[pl.ds(0, held)] = same_ref[...]
    remote[pl.ds(held, held)] = other_ref[...]
    seen = lax.broadcasted_iota(jnp.int32, (days, LANES), 0) < days_ref[0]
    for block in range(blocks):
        places = []
        for k in range(count):
            link = links_ref[k, block]
            distance = (link // bound) ^ me
            places.append((distance % 2) * held + (distance // 2) * bound + link % bound)
        far = jnp.concatenate([remote[place] for place in places], axis=1)
        total = lax.dot_general(far, weight_ref[block], TURNED, preferred_element_type=jnp.float32)
        source = (running_ref[block] - total).astype(jnp.bfloat16)
        drive = lax.dot_general(source, inverse_ref[block], TURNED, preferred_element_type=jnp.float32)
        for pair in range(pairs):
            forcing_ref[pair, pl.ds(block, days, stride=blocks), :] = jnp.where(
                seen, drive[pair * days : (pair + 1) * days], 0.0
            )
    states = [jnp.zeros((blocks, LANES), jnp.float32)] * pairs
    for day in range(days):
        rows = pl.ds(day * blocks, blocks)
        factor = retain_ref[rows, :]
        for pair in range(pairs):
            states[pair] = factor * states[pair] + forcing_ref[pair, rows, :]
    leave(message_ref, states, product_ref)


def leave(message_ref, values, product_ref):
    for pair, value in enumerate(values):
        message_ref[pair] = value.astype(jnp.bfloat16)
    message_ref[len(values)] = product_ref[0]
    message_ref[len(values) + 1] = product_ref[1]


def carried(pairs, messages_ref, backward):
    me, count = lax.axis_index("tm"), messages_ref.shape[0]
    order = reversed(range(1, count)) if backward else range(count - 1)
    carries = [jnp.zeros(messages_ref.shape[2:], jnp.float32)] * pairs
    for slab in order:
        valid = slab > me if backward else slab < me
        factor = messages_ref[slab, pairs].astype(jnp.float32) + messages_ref[slab, pairs + 1].astype(jnp.float32)
        for pair in range(pairs):
            update = messages_ref[slab, pair].astype(jnp.float32) + factor * carries[pair]
            carries[pair] = jnp.where(valid, update, carries[pair])
    return carries


def adjoint_kernel(
    dims, days_ref, forcing_ref, retain_ref, product_ref, inverse_ref, messages_ref, adjoint_ref, message_ref, stage
):
    days, blocks, size, probes = dims
    pairs = forcing_ref.shape[0]
    seen = lax.broadcasted_iota(jnp.int32, (days, LANES), 0) < days_ref[0]
    states = carried(pairs, messages_ref, False)
    for day in range(days):
        rows = pl.ds(day * blocks, blocks)
        factor = retain_ref[rows, :]
        for pair in range(pairs):
            states[pair] = factor * states[pair] + forcing_ref[pair, rows, :]
            stage[pair, rows, :] = states[pair]
    for block in range(blocks):
        stored = jnp.concatenate(
            [stage[pair, pl.ds(block, days, stride=blocks), :].astype(jnp.bfloat16) for pair in range(pairs)], axis=0
        )
        adjoint = jnp.dot(stored, inverse_ref[block], preferred_element_type=jnp.float32)
        for pair in range(pairs):
            adjoint_ref[pair, pl.ds(block, days, stride=blocks), :] = jnp.where(
                seen, adjoint[pair * days : (pair + 1) * days], 0.0
            )
    carries = [jnp.zeros((blocks, LANES), jnp.float32)] * pairs
    for day in reversed(range(days)):
        rows = pl.ds(day * blocks, blocks)
        factor = retain_ref[rows, :]
        for pair in range(pairs):
            carries[pair] = factor * (adjoint_ref[pair, rows, :] + carries[pair])
    leave(message_ref, carries, product_ref)


def variance_kernel(dims, adjoint_ref, retain_ref, moved_ref, messages_ref, out_ref, stage):
    days, blocks, size, probes = dims
    pairs = adjoint_ref.shape[0]
    carries = carried(pairs, messages_ref, True)
    for day in reversed(range(days)):
        rows = pl.ds(day * blocks, blocks)
        factor = retain_ref[rows, :]
        total = None
        for pair in range(pairs):
            smoothed = adjoint_ref[pair, rows, :] + carries[pair]
            carries[pair] = factor * smoothed
            term = smoothed * moved_ref[pair, rows, :].astype(jnp.float32)
            total = term if total is None else total + term
        stage[rows, :] = total
    lane = lax.broadcasted_iota(jnp.int32, (days, LANES), 1)
    for block in range(0, blocks, 2):
        both = [stage[pl.ds(block + half, days, stride=blocks), :] for half in range(2)]
        both = [value + pltpu.roll(value, size, 1) for value in both]
        out_ref[:, pl.ds(block * size, LANES)] = jnp.where(lane < size, both[0], both[1]) * (1.0 / probes)


def call(kernel, outs, scratch, flops, moved, scalars, *operands):
    in_specs = [
        pl.BlockSpec(memory_space=pltpu.SMEM if i < scalars else pltpu.VMEM) for i in range(len(operands))
    ]
    return pl.pallas_call(
        kernel,
        out_shape=[jax.ShapeDtypeStruct(shape, kind) for shape, kind in outs],
        in_specs=in_specs,
        out_specs=[pl.BlockSpec(memory_space=pltpu.VMEM) for _ in outs],
        scratch_shapes=scratch,
        compiler_params=pltpu.CompilerParams(vmem_limit_bytes=VMEM_LIMIT),
        cost_estimate=pl.CostEstimate(flops=flops, bytes_accessed=moved, transcendentals=0),
    )(*operands)


def crossed(block, axis, bits):
    return lax.ppermute(block, axis, [(i, i ^ bits) for i in range(lax.axis_size(axis))])


def local(
    probes,
    local_links,
    remote_links,
    shared_blocks,
    slab_days,
    local_coupling,
    remote_coupling,
    block_inverse,
    retention,
):
    days, blocks, width = probes.shape
    size = block_inverse.shape[1]
    dims = (days, blocks, size, width // size)
    pairs = width // LANES
    f32, bf16 = jnp.float32, jnp.bfloat16
    bound = shared_blocks.shape[1]
    far = remote_links.shape[1]
    rows = days * blocks
    groups = lax.axis_size("space")
    held = groups // 2 * bound
    near_table, far_table = local_links.T, remote_links.T
    big = ((pairs, rows, LANES), f32)

    (outgoing,) = call(
        functools.partial(outgoing_kernel, dims),
        [((bound, pairs * days, LANES), bf16)],
        [], 10**9, 4 * 10**6, 1, shared_blocks, probes,
    )
    pieces = {bits: crossed(outgoing, "space", bits) for bits in range(groups - 2, 0, -2)}
    running, moved, retain, product, remote_weight, inverse = call(
        functools.partial(local_kernel, dims),
        [
            ((blocks, pairs * days, LANES), f32),
            ((pairs, rows, LANES), bf16),
            ((rows, LANES), f32),
            ((2, blocks, LANES), bf16),
            ((blocks, LANES, far * LANES), bf16),
            ((blocks, LANES, LANES), bf16),
        ],
        [pltpu.VMEM(*big), pltpu.VMEM((blocks, pairs * days, LANES), bf16)],
        10**10, 10**7, 2,
        near_table, slab_days, probes, local_coupling, remote_coupling, block_inverse, retention,
    )
    (same,) = call(
        assemble_kernel,
        [((held, pairs * days, LANES), bf16)],
        [], 0, 10**6, 0, outgoing, *[pieces[bits] for bits in range(2, groups, 2)], product,
    )
    other = crossed(same, "space", 1)
    message_shape = ((pairs + 2, blocks, LANES), bf16)
    forcing, message = call(
        functools.partial(forward_kernel, dims),
        [big, message_shape],
        [pltpu.VMEM((2 * held, pairs * days, LANES), bf16)], 10**10, 10**7, 2,
        far_table, slab_days, running, same, other, remote_weight, inverse, retain, product,
    )
    messages = lax.all_gather(message, "tm", axis=0)
    adjoint, message = call(
        functools.partial(adjoint_kernel, dims),
        [big, message_shape],
        [pltpu.VMEM(*big)], 10**10, 10**7, 1,
        slab_days, forcing, retain, product, inverse, messages,
    )
    messages = lax.all_gather(message, "tm", axis=0)
    (variance,) = call(
        functools.partial(variance_kernel, dims),
        [((days, blocks * size), f32)],
        [pltpu.VMEM((rows, LANES), f32)], 10**10, 10**7, 0,
        adjoint, retain, moved, messages,
    )
    return variance


def solution(mesh):
    placed = (
        P("tm", "space", None),
        P("space", None),
        P("space", None),
        P("space", None),
        P("tm"),
        P("space", None, None, None),
        P("space", None, None, None),
        P("space", None, None),
        P("tm", "space"),
    )
    return jax.shard_map(
        local, mesh=mesh, in_specs=placed, out_specs=P("tm", "space"), check_vma=False
    )
```

```python
import functools

import jax
import jax.numpy as jnp
from jax import lax
from jax.experimental import pallas as pl
from jax.experimental.pallas import tpu as pltpu
from jax.sharding import PartitionSpec as P

LANES = 128
VMEM_LIMIT = 20 * 1024 * 1024
TURNED = (((1,), (1,)), ((), ()))


def permutation(size, probes, start, width):
    total = size * probes
    column = lax.broadcasted_iota(jnp.int32, (total, width), 1) + start
    origin = (column % size) * probes + column // size
    row = lax.broadcasted_iota(jnp.int32, (total, width), 0)
    return (row == origin).astype(jnp.float32).astype(jnp.bfloat16)


def doubled(weight):
    zero = jnp.zeros_like(weight)
    return jnp.concatenate(
        [jnp.concatenate([weight, zero], axis=1), jnp.concatenate([zero, weight], axis=1)], axis=0
    )


def outgoing_kernel(dims, shared_ref, z_hbm, outgoing_ref, z_ref, arrived):
    days, blocks, size, probes = dims
    count = outgoing_ref.shape[0]
    part = 8
    copies = [
        pltpu.make_async_copy(z_hbm.at[pl.ds(i * part, part)], z_ref.at[pl.ds(i * part, part)], arrived.at[i])
        for i in range(days // part)
    ]
    for copy in copies:
        copy.start()
    step = 2 * LANES
    moves = [permutation(size, probes, start, step) for start in range(0, size * probes, step)]
    row = lax.broadcasted_iota(jnp.int32, (part, part * blocks), 0)
    column = lax.broadcasted_iota(jnp.int32, (part, part * blocks), 1)
    picks = [(column == row * blocks + shared_ref[0, m]).astype(jnp.float32) for m in range(count)]
    pick = jnp.concatenate(picks, axis=0).astype(jnp.bfloat16)
    picked = []
    for i, copy in enumerate(copies):
        copy.wait()
        z = z_ref[pl.ds(i * part, part)].reshape(part * blocks, size * probes)
        picked.append(jnp.dot(pick, z, preferred_element_type=jnp.float32))
    picked = jnp.concatenate([rows[m * part : (m + 1) * part] for m in range(count) for rows in picked], axis=0)
    picked = picked.astype(jnp.bfloat16)
    for i, move in enumerate(moves):
        moved = jnp.dot(picked, move, preferred_element_type=jnp.float32).astype(jnp.bfloat16)
        for half in range(2):
            pair = i * 2 + half
            for m in range(count):
                outgoing_ref[m, pl.ds(pair * days, days), :] = moved[
                    m * days : (m + 1) * days, half * LANES : (half + 1) * LANES
                ]


def local_kernel(
    dims, links_ref, days_ref, z_ref, weight_ref, remote_weight_ref, inverse_ref, retention_ref,
    running_ref, moved_ref, retain_ref, product_ref, remote_doubled_ref, inverse_doubled_ref, stage, turned,
):
    days, blocks, size, probes = dims
    pairs = size * probes // LANES
    count = links_ref.shape[0]
    z = z_ref[...].reshape(days * blocks, size * probes)
    step = 2 * LANES
    for start in range(0, size * probes, step):
        moved = jnp.dot(z, permutation(size, probes, start, step), preferred_element_type=jnp.float32)
        for half in range(2):
            pair = start // LANES + half
            tile = moved[:, half * LANES : (half + 1) * LANES]
            stage[pair] = tile
            moved_ref[pair] = tile.astype(jnp.bfloat16)
    for block in range(blocks):
        for pair in range(pairs):
            rows = stage[pair, pl.ds(block, days, stride=blocks), :]
            turned[block, pl.ds(pair * days, days), :] = rows.astype(jnp.bfloat16)
    for block in range(blocks):
        near = jnp.concatenate([turned[links_ref[k, block]] for k in range(count)], axis=1)
        weight = jnp.concatenate([doubled(weight_ref[block, k]) for k in range(count)], axis=1)
        total = lax.dot_general(near, weight, TURNED, preferred_element_type=jnp.float32)
        running_ref[block] = turned[block].astype(jnp.float32) - total
        remote_doubled_ref[block] = jnp.concatenate(
            [doubled(remote_weight_ref[block, k]) for k in range(remote_weight_ref.shape[1])], axis=1
        )
        inverse_doubled_ref[block] = doubled(inverse_ref[block])
    observed = days_ref[0]
    shape = (days, LANES)
    first = lax.broadcasted_iota(jnp.int32, shape, 1) < size
    seen = lax.broadcasted_iota(jnp.int32, shape, 0) < observed
    for block in range(0, blocks, 2):
        factor = jnp.where(seen, retention_ref[:, pl.ds(block * size, LANES)], 1.0)
        other = pltpu.roll(factor, size, 1)
        retain_ref[pl.ds(block, days, stride=blocks), :] = jnp.where(first, factor, other)
        retain_ref[pl.ds(block + 1, days, stride=blocks), :] = jnp.where(first, other, factor)
    product = jnp.ones((blocks, LANES), jnp.float32)
    for day in range(days):
        product = product * retain_ref[pl.ds(day * blocks, blocks), :]
    high = product.astype(jnp.bfloat16)
    product_ref[0] = high
    product_ref[1] = (product - high.astype(jnp.float32)).astype(jnp.bfloat16)


def assemble_kernel(*refs):
    *piece_refs, product_ref, out_ref = refs
    count = piece_refs[0].shape[0]
    for i, ref in enumerate(piece_refs):
        out_ref[pl.ds(i * count, count)] = ref[...]


def forward_kernel(
    dims, links_ref, days_ref, running_ref, same_ref, other_ref, weight_ref, inverse_ref, retain_ref, product_ref,
    forcing_ref, message_ref, remote,
):
    days, blocks, size, probes = dims
    pairs = forcing_ref.shape[0]
    count = links_ref.shape[0]
    held = same_ref.shape[0]
    bound = 2 * held // lax.axis_size("space")
    me = lax.axis_index("space")
    remote[pl.ds(0, held)] = same_ref[...]
    remote[pl.ds(held, held)] = other_ref[...]
    seen = lax.broadcasted_iota(jnp.int32, (days, LANES), 0) < days_ref[0]
    for block in range(blocks):
        places = []
        for k in range(count):
            link = links_ref[k, block]
            distance = (link // bound) ^ me
            places.append((distance % 2) * held + (distance // 2) * bound + link % bound)
        far = jnp.concatenate([remote[place] for place in places], axis=1)
        total = lax.dot_general(far, weight_ref[block], TURNED, preferred_element_type=jnp.float32)
        source = (running_ref[block] - total).astype(jnp.bfloat16)
        drive = lax.dot_general(source, inverse_ref[block], TURNED, preferred_element_type=jnp.float32)
        for pair in range(pairs):
            forcing_ref[pair, pl.ds(block, days, stride=blocks), :] = jnp.where(
                seen, drive[pair * days : (pair + 1) * days], 0.0
            )
    states = [jnp.zeros((blocks, LANES), jnp.float32)] * pairs
    for day in range(days):
        rows = pl.ds(day * blocks, blocks)
        factor = retain_ref[rows, :]
        for pair in range(pairs):
            states[pair] = factor * states[pair] + forcing_ref[pair, rows, :]
    leave(message_ref, states)
    message_ref[pairs] = product_ref[0]
    message_ref[pairs + 1] = product_ref[1]


def leave(message_ref, values):
    for pair, value in enumerate(values):
        message_ref[pair] = value.astype(jnp.bfloat16)


def collect(piece_refs, inbox):
    me = lax.axis_index("tm")
    for k, ref in enumerate(piece_refs):
        inbox[me ^ (k + 1)] = ref[...]


def carried(pairs, inbox, products, backward):
    me, count = lax.axis_index("tm"), inbox.shape[0]
    carries = [jnp.zeros(inbox.shape[2:], jnp.float32)] * pairs
    for slab in range(count - 1, 0, -1) if backward else range(count - 1):
        valid = slab > me if backward else slab < me
        factor = products[slab, pairs].astype(jnp.float32) + products[slab, pairs + 1].astype(jnp.float32)
        for pair in range(pairs):
            update = inbox[slab, pair].astype(jnp.float32) + factor * carries[pair]
            carries[pair] = jnp.where(valid, update, carries[pair])
    return carries


def adjoint_kernel(dims, hops, days_ref, forcing_ref, retain_ref, inverse_ref, *rest):
    days, blocks, size, probes = dims
    pairs = forcing_ref.shape[0]
    adjoint_ref, message_ref, stage, inbox = rest[hops:]
    collect(rest[:hops], inbox)
    seen = lax.broadcasted_iota(jnp.int32, (days, LANES), 0) < days_ref[0]
    states = carried(pairs, inbox, inbox, False)
    for day in range(days):
        rows = pl.ds(day * blocks, blocks)
        factor = retain_ref[rows, :]
        for pair in range(pairs):
            states[pair] = factor * states[pair] + forcing_ref[pair, rows, :]
            stage[pair, rows, :] = states[pair]
    for block in range(blocks):
        stored = jnp.concatenate(
            [stage[pair, pl.ds(block, days, stride=blocks), :].astype(jnp.bfloat16) for pair in range(pairs)], axis=0
        )
        adjoint = jnp.dot(stored, inverse_ref[block], preferred_element_type=jnp.float32)
        for pair in range(pairs):
            adjoint_ref[pair, pl.ds(block, days, stride=blocks), :] = jnp.where(
                seen, adjoint[pair * days : (pair + 1) * days], 0.0
            )
    carries = [jnp.zeros((blocks, LANES), jnp.float32)] * pairs
    for day in reversed(range(days)):
        rows = pl.ds(day * blocks, blocks)
        factor = retain_ref[rows, :]
        for pair in range(pairs):
            carries[pair] = factor * (adjoint_ref[pair, rows, :] + carries[pair])
    leave(message_ref, carries)


def variance_kernel(dims, hops, adjoint_ref, retain_ref, moved_ref, *rest):
    days, blocks, size, probes = dims
    pairs = adjoint_ref.shape[0]
    out_ref, stage, inbox, products = rest[2 * hops :]
    collect(rest[:hops], inbox)
    collect(rest[hops : 2 * hops], products)
    carries = carried(pairs, inbox, products, True)
    for day in reversed(range(days)):
        rows = pl.ds(day * blocks, blocks)
        factor = retain_ref[rows, :]
        total = None
        for pair in range(pairs):
            smoothed = adjoint_ref[pair, rows, :] + carries[pair]
            carries[pair] = factor * smoothed
            term = smoothed * moved_ref[pair, rows, :].astype(jnp.float32)
            total = term if total is None else total + term
        stage[rows, :] = total
    lane = lax.broadcasted_iota(jnp.int32, (days, LANES), 1)
    for block in range(0, blocks, 2):
        both = [stage[pl.ds(block + half, days, stride=blocks), :] for half in range(2)]
        both = [value + pltpu.roll(value, size, 1) for value in both]
        out_ref[:, pl.ds(block * size, LANES)] = jnp.where(lane < size, both[0], both[1]) * (1.0 / probes)


def call(kernel, outs, scratch, flops, moved, scalars, *operands, apart=(), limit=VMEM_LIMIT):
    in_specs = [
        pl.BlockSpec(memory_space=pltpu.SMEM if i < scalars else pl.ANY if i in apart else pltpu.VMEM)
        for i in range(len(operands))
    ]
    return pl.pallas_call(
        kernel,
        out_shape=[jax.ShapeDtypeStruct(shape, kind) for shape, kind in outs],
        in_specs=in_specs,
        out_specs=[pl.BlockSpec(memory_space=pltpu.VMEM) for _ in outs],
        scratch_shapes=scratch,
        compiler_params=pltpu.CompilerParams(vmem_limit_bytes=limit),
        cost_estimate=pl.CostEstimate(flops=flops, bytes_accessed=moved, transcendentals=0),
    )(*operands)


def crossed(block, axis, bits):
    return lax.ppermute(block, axis, [(i, i ^ bits) for i in range(lax.axis_size(axis))])


def local(
    probes,
    local_links,
    remote_links,
    shared_blocks,
    slab_days,
    local_coupling,
    remote_coupling,
    block_inverse,
    retention,
):
    days, blocks, width = probes.shape
    size = block_inverse.shape[1]
    dims = (days, blocks, size, width // size)
    pairs = width // LANES
    f32, bf16 = jnp.float32, jnp.bfloat16
    bound = shared_blocks.shape[1]
    far = remote_links.shape[1]
    rows = days * blocks
    groups = lax.axis_size("space")
    held = groups // 2 * bound
    near_table, far_table = local_links.T, remote_links.T
    big = ((pairs, rows, LANES), f32)

    (outgoing,) = call(
        functools.partial(outgoing_kernel, dims),
        [((bound, pairs * days, LANES), bf16)],
        [pltpu.VMEM(probes.shape, bf16), pltpu.SemaphoreType.DMA((days // 8,))], 10**9, 4 * 10**6, 1,
        shared_blocks, probes, apart=(1,), limit=56 * 1024 * 1024,
    )
    pieces = {bits: crossed(outgoing, "space", bits) for bits in range(groups - 2, 0, -2)}
    running, moved, retain, product, remote_weight, inverse = call(
        functools.partial(local_kernel, dims),
        [
            ((blocks, pairs * days, LANES), f32),
            ((pairs, rows, LANES), bf16),
            ((rows, LANES), f32),
            ((2, blocks, LANES), bf16),
            ((blocks, LANES, far * LANES), bf16),
            ((blocks, LANES, LANES), bf16),
        ],
        [pltpu.VMEM(*big), pltpu.VMEM((blocks, pairs * days, LANES), bf16)],
        10**10, 10**7, 2,
        near_table, slab_days, probes, local_coupling, remote_coupling, block_inverse, retention,
    )
    (same,) = call(
        assemble_kernel,
        [((held, pairs * days, LANES), bf16)],
        [], 0, 10**6, 0, outgoing, *[pieces[bits] for bits in range(2, groups, 2)], product,
    )
    other = crossed(same, "space", 1)
    slabs = lax.axis_size("tm")
    hops = slabs - 1
    exchange = lambda message: [crossed(message, "tm", bits) for bits in range(hops, 0, -1)][::-1]
    inbox = pltpu.VMEM((slabs, pairs + 2, blocks, LANES), bf16)
    forcing, message = call(
        functools.partial(forward_kernel, dims),
        [big, ((pairs + 2, blocks, LANES), bf16)],
        [pltpu.VMEM((2 * held, pairs * days, LANES), bf16)], 10**10, 10**7, 2,
        far_table, slab_days, running, same, other, remote_weight, inverse, retain, product,
    )
    ends = exchange(message)
    adjoint, message = call(
        functools.partial(adjoint_kernel, dims, hops),
        [big, ((pairs, blocks, LANES), bf16)],
        [pltpu.VMEM(*big), inbox], 10**10, 10**7, 1,
        slab_days, forcing, retain, inverse, *ends,
    )
    starts = exchange(message)
    (variance,) = call(
        functools.partial(variance_kernel, dims, hops),
        [((days, blocks * size), f32)],
        [pltpu.VMEM((rows, LANES), f32), pltpu.VMEM((slabs, pairs, blocks, LANES), bf16), inbox], 10**10, 10**7, 0,
        adjoint, retain, moved, *starts, *ends,
    )
    return variance


def solution(mesh):
    placed = (
        P("tm", "space", None),
        P("space", None),
        P("space", None),
        P("space", None),
        P("tm"),
        P("space", None, None, None),
        P("space", None, None, None),
        P("space", None, None),
        P("tm", "space"),
    )
    return jax.shard_map(
        local, mesh=mesh, in_specs=placed, out_specs=P("tm", "space"), check_vma=False
    )
```

```python
import functools

import jax
import jax.numpy as jnp
from jax import lax
from jax.experimental import pallas as pl
from jax.experimental.pallas import tpu as pltpu
from jax.sharding import PartitionSpec as P

LANES = 128
VMEM_LIMIT = 20 * 1024 * 1024
TURNED = (((1,), (1,)), ((), ()))


def permutation(size, probes, start, width):
    total = size * probes
    column = lax.broadcasted_iota(jnp.int32, (total, width), 1) + start
    origin = (column % size) * probes + column // size
    row = lax.broadcasted_iota(jnp.int32, (total, width), 0)
    return (row == origin).astype(jnp.float32).astype(jnp.bfloat16)


def doubled(weight):
    zero = jnp.zeros_like(weight)
    return jnp.concatenate(
        [jnp.concatenate([weight, zero], axis=1), jnp.concatenate([zero, weight], axis=1)], axis=0
    )


def outgoing_kernel(dims, shared_ref, z_hbm, outgoing_ref, z_ref, arrived):
    days, blocks, size, probes = dims
    count = outgoing_ref.shape[0]
    part = 8
    copies = [
        pltpu.make_async_copy(z_hbm.at[pl.ds(i * part, part)], z_ref.at[pl.ds(i * part, part)], arrived.at[i])
        for i in range(days // part)
    ]
    for copy in copies:
        copy.start()
    step = 2 * LANES
    moves = [permutation(size, probes, start, step) for start in range(0, size * probes, step)]
    row = lax.broadcasted_iota(jnp.int32, (part, part * blocks), 0)
    column = lax.broadcasted_iota(jnp.int32, (part, part * blocks), 1)
    picks = [(column == row * blocks + shared_ref[0, m]).astype(jnp.float32) for m in range(count)]
    pick = jnp.concatenate(picks, axis=0).astype(jnp.bfloat16)
    picked = []
    for i, copy in enumerate(copies):
        copy.wait()
        z = z_ref[pl.ds(i * part, part)].reshape(part * blocks, size * probes)
        picked.append(jnp.dot(pick, z, preferred_element_type=jnp.float32))
    picked = jnp.concatenate([rows[m * part : (m + 1) * part] for m in range(count) for rows in picked], axis=0)
    picked = picked.astype(jnp.bfloat16)
    for i, move in enumerate(moves):
        moved = jnp.dot(picked, move, preferred_element_type=jnp.float32).astype(jnp.bfloat16)
        for half in range(2):
            pair = i * 2 + half
            for m in range(count):
                outgoing_ref[m, pl.ds(pair * days, days), :] = moved[
                    m * days : (m + 1) * days, half * LANES : (half + 1) * LANES
                ]


def local_kernel(
    dims, links_ref, days_ref, z_ref, weight_ref, remote_weight_ref, inverse_ref, retention_ref,
    running_ref, moved_ref, retain_ref, product_ref, remote_doubled_ref, inverse_doubled_ref, stage, turned,
):
    days, blocks, size, probes = dims
    pairs = size * probes // LANES
    count = links_ref.shape[0]
    z = z_ref[...].reshape(days * blocks, size * probes)
    step = 2 * LANES
    for start in range(0, size * probes, step):
        moved = jnp.dot(z, permutation(size, probes, start, step), preferred_element_type=jnp.float32)
        for half in range(2):
            pair = start // LANES + half
            tile = moved[:, half * LANES : (half + 1) * LANES]
            stage[pair] = tile
            moved_ref[pair] = tile.astype(jnp.bfloat16)
    for block in range(blocks):
        for pair in range(pairs):
            rows = stage[pair, pl.ds(block, days, stride=blocks), :]
            turned[block, pl.ds(pair * days, days), :] = rows.astype(jnp.bfloat16)
    for block in range(blocks):
        near = jnp.concatenate([turned[links_ref[k, block]] for k in range(count)], axis=1)
        weight = jnp.concatenate([doubled(weight_ref[block, k]) for k in range(count)], axis=1)
        total = lax.dot_general(near, weight, TURNED, preferred_element_type=jnp.float32)
        running_ref[block] = turned[block].astype(jnp.float32) - total
        remote_doubled_ref[block] = jnp.concatenate(
            [doubled(remote_weight_ref[block, k]) for k in range(remote_weight_ref.shape[1])], axis=1
        )
        inverse_doubled_ref[block] = doubled(inverse_ref[block])
    observed = days_ref[0]
    shape = (days, LANES)
    first = lax.broadcasted_iota(jnp.int32, shape, 1) < size
    seen = lax.broadcasted_iota(jnp.int32, shape, 0) < observed
    for block in range(0, blocks, 2):
        factor = jnp.where(seen, retention_ref[:, pl.ds(block * size, LANES)], 1.0)
        other = pltpu.roll(factor, size, 1)
        retain_ref[pl.ds(block, days, stride=blocks), :] = jnp.where(first, factor, other)
        retain_ref[pl.ds(block + 1, days, stride=blocks), :] = jnp.where(first, other, factor)
    product = jnp.ones((blocks, LANES), jnp.float32)
    for day in range(days):
        product = product * retain_ref[pl.ds(day * blocks, blocks), :]
    high = product.astype(jnp.bfloat16)
    product_ref[0] = high
    product_ref[1] = (product - high.astype(jnp.float32)).astype(jnp.bfloat16)


def assemble_kernel(*refs):
    *piece_refs, product_ref, out_ref = refs
    count = piece_refs[0].shape[0]
    for i, ref in enumerate(piece_refs):
        out_ref[pl.ds(i * count, count)] = ref[...]


def forward_kernel(
    dims, links_ref, days_ref, running_ref, same_ref, other_ref, weight_ref, inverse_ref, retain_ref, product_ref,
    forcing_ref, message_ref, remote,
):
    days, blocks, size, probes = dims
    pairs = forcing_ref.shape[0]
    count = links_ref.shape[0]
    held = same_ref.shape[0]
    bound = 2 * held // lax.axis_size("space")
    me = lax.axis_index("space")
    remote[pl.ds(0, held)] = same_ref[...]
    remote[pl.ds(held, held)] = other_ref[...]
    seen = lax.broadcasted_iota(jnp.int32, (days, LANES), 0) < days_ref[0]
    for block in range(blocks):
        places = []
        for k in range(count):
            link = links_ref[k, block]
            distance = (link // bound) ^ me
            places.append((distance % 2) * held + (distance // 2) * bound + link % bound)
        far = jnp.concatenate([remote[place] for place in places], axis=1)
        total = lax.dot_general(far, weight_ref[block], TURNED, preferred_element_type=jnp.float32)
        source = (running_ref[block] - total).astype(jnp.bfloat16)
        drive = lax.dot_general(source, inverse_ref[block], TURNED, preferred_element_type=jnp.float32)
        for pair in range(pairs):
            forcing_ref[pair, pl.ds(block, days, stride=blocks), :] = jnp.where(
                seen, drive[pair * days : (pair + 1) * days], 0.0
            )
    states = [jnp.zeros((blocks, LANES), jnp.float32)] * pairs
    for day in range(days):
        rows = pl.ds(day * blocks, blocks)
        factor = retain_ref[rows, :]
        for pair in range(pairs):
            states[pair] = factor * states[pair] + forcing_ref[pair, rows, :]
    leave(message_ref, states)
    for slab in range(message_ref.shape[0]):
        message_ref[slab, pl.ds(pairs, 2)] = product_ref[...]


def leave(message_ref, values):
    for pair, value in enumerate(values):
        for slab in range(message_ref.shape[0]):
            message_ref[slab, pair] = value.astype(jnp.bfloat16)


def carried(pairs, inbox, products, backward):
    me, count = lax.axis_index("tm"), inbox.shape[0]
    carries = [jnp.zeros(inbox.shape[2:], jnp.float32)] * pairs
    for slab in range(count - 1, 0, -1) if backward else range(count - 1):
        valid = slab > me if backward else slab < me
        factor = products[slab, pairs].astype(jnp.float32) + products[slab, pairs + 1].astype(jnp.float32)
        for pair in range(pairs):
            update = inbox[slab, pair].astype(jnp.float32) + factor * carries[pair]
            carries[pair] = jnp.where(valid, update, carries[pair])
    return carries


def adjoint_kernel(dims, days_ref, forcing_ref, retain_ref, inverse_ref, inbox, adjoint_ref, message_ref, stage):
    days, blocks, size, probes = dims
    pairs = forcing_ref.shape[0]
    seen = lax.broadcasted_iota(jnp.int32, (days, LANES), 0) < days_ref[0]
    states = carried(pairs, inbox, inbox, False)
    for day in range(days):
        rows = pl.ds(day * blocks, blocks)
        factor = retain_ref[rows, :]
        for pair in range(pairs):
            states[pair] = factor * states[pair] + forcing_ref[pair, rows, :]
            stage[pair, rows, :] = states[pair]
    for block in range(blocks):
        stored = jnp.concatenate(
            [stage[pair, pl.ds(block, days, stride=blocks), :].astype(jnp.bfloat16) for pair in range(pairs)], axis=0
        )
        adjoint = jnp.dot(stored, inverse_ref[block], preferred_element_type=jnp.float32)
        for pair in range(pairs):
            adjoint_ref[pair, pl.ds(block, days, stride=blocks), :] = jnp.where(
                seen, adjoint[pair * days : (pair + 1) * days], 0.0
            )
    carries = [jnp.zeros((blocks, LANES), jnp.float32)] * pairs
    for day in reversed(range(days)):
        rows = pl.ds(day * blocks, blocks)
        factor = retain_ref[rows, :]
        for pair in range(pairs):
            carries[pair] = factor * (adjoint_ref[pair, rows, :] + carries[pair])
    leave(message_ref, carries)


def variance_kernel(dims, adjoint_ref, retain_ref, moved_ref, inbox, products, out_ref, stage):
    days, blocks, size, probes = dims
    pairs = adjoint_ref.shape[0]
    carries = carried(pairs, inbox, products, True)
    for day in reversed(range(days)):
        rows = pl.ds(day * blocks, blocks)
        factor = retain_ref[rows, :]
        total = None
        for pair in range(pairs):
            smoothed = adjoint_ref[pair, rows, :] + carries[pair]
            carries[pair] = factor * smoothed
            term = smoothed * moved_ref[pair, rows, :].astype(jnp.float32)
            total = term if total is None else total + term
        stage[rows, :] = total
    lane = lax.broadcasted_iota(jnp.int32, (days, LANES), 1)
    for block in range(0, blocks, 2):
        both = [stage[pl.ds(block + half, days, stride=blocks), :] for half in range(2)]
        both = [value + pltpu.roll(value, size, 1) for value in both]
        out_ref[:, pl.ds(block * size, LANES)] = jnp.where(lane < size, both[0], both[1]) * (1.0 / probes)


def call(kernel, outs, scratch, flops, moved, scalars, *operands, apart=(), limit=VMEM_LIMIT):
    in_specs = [
        pl.BlockSpec(memory_space=pltpu.SMEM if i < scalars else pl.ANY if i in apart else pltpu.VMEM)
        for i in range(len(operands))
    ]
    return pl.pallas_call(
        kernel,
        out_shape=[jax.ShapeDtypeStruct(shape, kind) for shape, kind in outs],
        in_specs=in_specs,
        out_specs=[pl.BlockSpec(memory_space=pltpu.VMEM) for _ in outs],
        scratch_shapes=scratch,
        compiler_params=pltpu.CompilerParams(vmem_limit_bytes=limit),
        cost_estimate=pl.CostEstimate(flops=flops, bytes_accessed=moved, transcendentals=0),
    )(*operands)


def crossed(block, axis, bits):
    return lax.ppermute(block, axis, [(i, i ^ bits) for i in range(lax.axis_size(axis))])


def local(
    probes,
    local_links,
    remote_links,
    shared_blocks,
    slab_days,
    local_coupling,
    remote_coupling,
    block_inverse,
    retention,
):
    days, blocks, width = probes.shape
    size = block_inverse.shape[1]
    dims = (days, blocks, size, width // size)
    pairs = width // LANES
    f32, bf16 = jnp.float32, jnp.bfloat16
    bound = shared_blocks.shape[1]
    far = remote_links.shape[1]
    rows = days * blocks
    groups = lax.axis_size("space")
    held = groups // 2 * bound
    near_table, far_table = local_links.T, remote_links.T
    big = ((pairs, rows, LANES), f32)

    (outgoing,) = call(
        functools.partial(outgoing_kernel, dims),
        [((bound, pairs * days, LANES), bf16)],
        [pltpu.VMEM(probes.shape, bf16), pltpu.SemaphoreType.DMA((days // 8,))], 10**9, 4 * 10**6, 1,
        shared_blocks, probes, apart=(1,), limit=63 * 1024 * 1024,
    )
    pieces = {bits: crossed(outgoing, "space", bits) for bits in range(groups - 2, 0, -2)}
    running, moved, retain, product, remote_weight, inverse = call(
        functools.partial(local_kernel, dims),
        [
            ((blocks, pairs * days, LANES), f32),
            ((pairs, rows, LANES), bf16),
            ((rows, LANES), f32),
            ((2, blocks, LANES), bf16),
            ((blocks, LANES, far * LANES), bf16),
            ((blocks, LANES, LANES), bf16),
        ],
        [pltpu.VMEM(*big), pltpu.VMEM((blocks, pairs * days, LANES), bf16)],
        10**10, 10**7, 2,
        near_table, slab_days, probes, local_coupling, remote_coupling, block_inverse, retention,
    )
    (same,) = call(
        assemble_kernel,
        [((held, pairs * days, LANES), bf16)],
        [], 0, 10**6, 0, outgoing, *[pieces[bits] for bits in range(2, groups, 2)], product,
    )
    other = crossed(same, "space", 1)
    slabs = lax.axis_size("tm")
    exchange = lambda message: lax.all_to_all(message, "tm", 0, 0)
    forcing, message = call(
        functools.partial(forward_kernel, dims),
        [big, ((slabs, pairs + 2, blocks, LANES), bf16)],
        [pltpu.VMEM((2 * held, pairs * days, LANES), bf16)], 10**10, 10**7, 2,
        far_table, slab_days, running, same, other, remote_weight, inverse, retain, product,
    )
    ends = exchange(message)
    adjoint, message = call(
        functools.partial(adjoint_kernel, dims),
        [big, ((slabs, pairs, blocks, LANES), bf16)],
        [pltpu.VMEM(*big)], 10**10, 10**7, 1,
        slab_days, forcing, retain, inverse, ends,
    )
    starts = exchange(message)
    (variance,) = call(
        functools.partial(variance_kernel, dims),
        [((days, blocks * size), f32)],
        [pltpu.VMEM((rows, LANES), f32)], 10**10, 10**7, 0,
        adjoint, retain, moved, starts, ends,
    )
    return variance


def solution(mesh):
    placed = (
        P("tm", "space", None),
        P("space", None),
        P("space", None),
        P("space", None),
        P("tm"),
        P("space", None, None, None),
        P("space", None, None, None),
        P("space", None, None),
        P("tm", "space"),
    )
    return jax.shard_map(
        local, mesh=mesh, in_specs=placed, out_specs=P("tm", "space"), check_vma=False
    )
```

```python
import functools

import jax
import jax.numpy as jnp
from jax import lax
from jax.experimental import pallas as pl
from jax.experimental.pallas import tpu as pltpu
from jax.sharding import PartitionSpec as P

LANES = 128
VMEM_LIMIT = 20 * 1024 * 1024
TURNED = (((1,), (1,)), ((), ()))


def permutation(size, probes, start, width):
    total = size * probes
    column = lax.broadcasted_iota(jnp.int32, (total, width), 1) + start
    origin = (column % size) * probes + column // size
    row = lax.broadcasted_iota(jnp.int32, (total, width), 0)
    return (row == origin).astype(jnp.float32).astype(jnp.bfloat16)


def doubled(weight):
    zero = jnp.zeros_like(weight)
    return jnp.concatenate(
        [jnp.concatenate([weight, zero], axis=1), jnp.concatenate([zero, weight], axis=1)], axis=0
    )


def locate(pair, sizes):
    chunk = 0
    while pair >= sizes[chunk]:
        pair -= sizes[chunk]
        chunk += 1
    return chunk, pair


def outgoing_kernel(dims, shared_ref, z_ref, *outgoing_refs):
    days, blocks, size, probes = dims
    count = outgoing_refs[0].shape[0]
    z = z_ref[...].reshape(days * blocks, size * probes)
    row = lax.broadcasted_iota(jnp.int32, (days, days * blocks), 0)
    column = lax.broadcasted_iota(jnp.int32, (days, days * blocks), 1)
    picks = [
        (column == row * blocks + shared_ref[m]).astype(jnp.float32).astype(jnp.bfloat16) for m in range(count)
    ]
    picked = jnp.dot(jnp.concatenate(picks, axis=0), z, preferred_element_type=jnp.float32).astype(jnp.bfloat16)
    step = 2 * LANES
    for start in range(0, size * probes, step):
        moved = jnp.dot(picked, permutation(size, probes, start, step), preferred_element_type=jnp.float32)
        moved = moved.astype(jnp.bfloat16)
        for half in range(2):
            pair = start // LANES + half
            for m in range(count):
                chunk, place = locate(pair, [ref.shape[1] // days for ref in outgoing_refs])
                outgoing_refs[chunk][m, pl.ds(place * days, days), :] = moved[
                    m * days : (m + 1) * days, half * LANES : (half + 1) * LANES
                ]


def local_kernel(
    dims, chunks, links_ref, days_ref, z_ref, weight_ref, remote_weight_ref, inverse_ref, retention_ref, *rest
):
    days, blocks, size, probes = dims
    running_refs, rest = rest[:chunks], rest[chunks:]
    moved_ref, retain_ref, product_ref, remote_doubled_ref, inverse_doubled_ref, stage, turned = rest
    pairs = size * probes // LANES
    count = links_ref.shape[0]
    z = z_ref[...].reshape(days * blocks, size * probes)
    step = 2 * LANES
    for start in range(0, size * probes, step):
        moved = jnp.dot(z, permutation(size, probes, start, step), preferred_element_type=jnp.float32)
        for half in range(2):
            pair = start // LANES + half
            tile = moved[:, half * LANES : (half + 1) * LANES]
            stage[pair] = tile
            moved_ref[pair] = tile.astype(jnp.bfloat16)
    for block in range(blocks):
        for pair in range(pairs):
            rows = stage[pair, pl.ds(block, days, stride=blocks), :]
            turned[block, pl.ds(pair * days, days), :] = rows.astype(jnp.bfloat16)
    for block in range(blocks):
        near = jnp.concatenate([turned[links_ref[k, block]] for k in range(count)], axis=1)
        weight = jnp.concatenate([doubled(weight_ref[block, k]) for k in range(count)], axis=1)
        total = lax.dot_general(near, weight, TURNED, preferred_element_type=jnp.float32)
        running = turned[block].astype(jnp.float32) - total
        start = 0
        for ref in running_refs:
            ref[block] = running[start : start + ref.shape[1]]
            start += ref.shape[1]
        remote_doubled_ref[block] = jnp.concatenate(
            [doubled(remote_weight_ref[block, k]) for k in range(remote_weight_ref.shape[1])], axis=1
        )
        inverse_doubled_ref[block] = doubled(inverse_ref[block])
    observed = days_ref[0]
    shape = (days, LANES)
    first = lax.broadcasted_iota(jnp.int32, shape, 1) < size
    seen = lax.broadcasted_iota(jnp.int32, shape, 0) < observed
    for block in range(0, blocks, 2):
        factor = jnp.where(seen, retention_ref[:, pl.ds(block * size, LANES)], 1.0)
        other = pltpu.roll(factor, size, 1)
        retain_ref[pl.ds(block, days, stride=blocks), :] = jnp.where(first, factor, other)
        retain_ref[pl.ds(block + 1, days, stride=blocks), :] = jnp.where(first, other, factor)
    product = jnp.ones((blocks, LANES), jnp.float32)
    for day in range(days):
        product = product * retain_ref[pl.ds(day * blocks, blocks), :]
    high = product.astype(jnp.bfloat16).astype(jnp.float32)
    half = lax.broadcasted_iota(jnp.int32, product.shape, 1) < size
    product_ref[...] = jnp.where(half, high, product - high).astype(jnp.bfloat16)


def assemble_kernel(*refs):
    *piece_refs, product_ref, out_ref = refs
    count = piece_refs[0].shape[0]
    for i, ref in enumerate(piece_refs):
        out_ref[pl.ds(i * count, count)] = ref[...]


def forward_kernel(
    dims, start, links_ref, days_ref, running_ref, same_ref, other_ref, weight_ref, inverse_ref, retain_ref, last_ref,
    forcing_ref, message_ref, remote,
):
    days, blocks, size, probes = dims
    pairs = forcing_ref.shape[0]
    count = links_ref.shape[0]
    held = same_ref.shape[0]
    bound = 2 * held // lax.axis_size("space")
    me = lax.axis_index("space")
    remote[pl.ds(0, held)] = same_ref[...]
    remote[pl.ds(held, held)] = other_ref[...]
    seen = lax.broadcasted_iota(jnp.int32, (days, LANES), 0) < days_ref[0]
    for block in range(blocks):
        places = []
        for k in range(count):
            link = links_ref[k, block]
            distance = (link // bound) ^ me
            places.append((distance % 2) * held + (distance // 2) * bound + link % bound)
        far = jnp.concatenate([remote[place] for place in places], axis=1)
        total = lax.dot_general(far, weight_ref[block], TURNED, preferred_element_type=jnp.float32)
        source = (running_ref[block] - total).astype(jnp.bfloat16)
        drive = lax.dot_general(source, inverse_ref[block], TURNED, preferred_element_type=jnp.float32)
        for pair in range(pairs):
            forcing_ref[pair, pl.ds(block, days, stride=blocks), :] = jnp.where(
                seen, drive[pair * days : (pair + 1) * days], 0.0
            )
    states = [jnp.zeros((blocks, LANES), jnp.float32)] * pairs
    for day in range(days):
        rows = pl.ds(day * blocks, blocks)
        factor = retain_ref[rows, :]
        for pair in range(pairs):
            states[pair] = factor * states[pair] + forcing_ref[pair, rows, :]
    end = message_ref.shape[0] - 1
    if start > 0:
        message_ref[pl.ds(0, start)] = last_ref[pl.ds(0, start)]
        message_ref[end] = last_ref[end]
    else:
        message_ref[end] = last_ref[...]
    leave(message_ref, states, start)


def leave(message_ref, values, start=0):
    for pair, value in enumerate(values):
        message_ref[start + pair] = value.astype(jnp.bfloat16)


def collect(piece_refs, inbox):
    me = lax.axis_index("tm")
    for k, ref in enumerate(piece_refs):
        inbox[me ^ (k + 1)] = ref[...]


def carried(pairs, inbox, products, backward):
    me, count = lax.axis_index("tm"), inbox.shape[0]
    carries = [jnp.zeros(inbox.shape[2:], jnp.float32)] * pairs
    for slab in range(count - 1, 0, -1) if backward else range(count - 1):
        valid = slab > me if backward else slab < me
        terms = products[slab, pairs].astype(jnp.float32)
        factor = terms + pltpu.roll(terms, LANES // 2, 1)
        for pair in range(pairs):
            update = inbox[slab, pair].astype(jnp.float32) + factor * carries[pair]
            carries[pair] = jnp.where(valid, update, carries[pair])
    return carries


def adjoint_kernel(dims, split, hops, days_ref, retain_ref, inverse_ref, *rest):
    days, blocks, size, probes = dims
    forcing_refs, rest = rest[: len(split)], rest[len(split) :]
    adjoint_ref, message_ref, stage, inbox = rest[hops:]
    pairs = adjoint_ref.shape[0]
    collect(rest[:hops], inbox)
    seen = lax.broadcasted_iota(jnp.int32, (days, LANES), 0) < days_ref[0]
    states = carried(pairs, inbox, inbox, False)
    for day in range(days):
        rows = pl.ds(day * blocks, blocks)
        factor = retain_ref[rows, :]
        for pair in range(pairs):
            chunk, place = locate(pair, split)
            states[pair] = factor * states[pair] + forcing_refs[chunk][place, rows, :]
            stage[pair, rows, :] = states[pair]
    for block in range(blocks):
        stored = jnp.concatenate(
            [stage[pair, pl.ds(block, days, stride=blocks), :].astype(jnp.bfloat16) for pair in range(pairs)], axis=0
        )
        adjoint = jnp.dot(stored, inverse_ref[block], preferred_element_type=jnp.float32)
        for pair in range(pairs):
            adjoint_ref[pair, pl.ds(block, days, stride=blocks), :] = jnp.where(
                seen, adjoint[pair * days : (pair + 1) * days], 0.0
            )
    carries = [jnp.zeros((blocks, LANES), jnp.float32)] * pairs
    for day in reversed(range(days)):
        rows = pl.ds(day * blocks, blocks)
        factor = retain_ref[rows, :]
        for pair in range(pairs):
            carries[pair] = factor * (adjoint_ref[pair, rows, :] + carries[pair])
    leave(message_ref, carries)


def variance_kernel(dims, hops, adjoint_ref, retain_ref, moved_ref, *rest):
    days, blocks, size, probes = dims
    pairs = adjoint_ref.shape[0]
    out_ref, stage, inbox, products = rest[2 * hops :]
    collect(rest[:hops], inbox)
    collect(rest[hops : 2 * hops], products)
    carries = carried(pairs, inbox, products, True)
    for day in reversed(range(days)):
        rows = pl.ds(day * blocks, blocks)
        factor = retain_ref[rows, :]
        total = None
        for pair in range(pairs):
            smoothed = adjoint_ref[pair, rows, :] + carries[pair]
            carries[pair] = factor * smoothed
            term = smoothed * moved_ref[pair, rows, :].astype(jnp.float32)
            total = term if total is None else total + term
        stage[rows, :] = total
    lane = lax.broadcasted_iota(jnp.int32, (days, LANES), 1)
    for block in range(0, blocks, 2):
        both = [stage[pl.ds(block + half, days, stride=blocks), :] for half in range(2)]
        both = [value + pltpu.roll(value, size, 1) for value in both]
        out_ref[:, pl.ds(block * size, LANES)] = jnp.where(lane < size, both[0], both[1]) * (1.0 / probes)


def call(kernel, outs, scratch, flops, moved, scalars, *operands, apart=(), limit=VMEM_LIMIT):
    in_specs = [
        pl.BlockSpec(memory_space=pltpu.SMEM if i < scalars else pl.ANY if i in apart else pltpu.VMEM)
        for i in range(len(operands))
    ]
    return pl.pallas_call(
        kernel,
        out_shape=[jax.ShapeDtypeStruct(shape, kind) for shape, kind in outs],
        in_specs=in_specs,
        out_specs=[pl.BlockSpec(memory_space=pltpu.VMEM) for _ in outs],
        scratch_shapes=scratch,
        compiler_params=pltpu.CompilerParams(vmem_limit_bytes=limit),
        cost_estimate=pl.CostEstimate(flops=flops, bytes_accessed=moved, transcendentals=0),
    )(*operands)


def crossed(block, axis, bits):
    return lax.ppermute(block, axis, [(i, i ^ bits) for i in range(lax.axis_size(axis))])


def local(
    probes,
    local_links,
    remote_links,
    shared_blocks,
    slab_days,
    local_coupling,
    remote_coupling,
    block_inverse,
    retention,
):
    days, blocks, width = probes.shape
    size = block_inverse.shape[1]
    dims = (days, blocks, size, width // size)
    pairs = width // LANES
    f32, bf16 = jnp.float32, jnp.bfloat16
    bound = shared_blocks.shape[1]
    far = remote_links.shape[1]
    rows = days * blocks
    groups = lax.axis_size("space")
    held = groups // 2 * bound
    near_table, far_table = local_links.T, remote_links.T
    shared = jnp.maximum(shared_blocks[0], 0)
    big = ((pairs, rows, LANES), f32)
    split = (pairs - 2, 2)

    outgoing = call(
        functools.partial(outgoing_kernel, dims),
        [((bound, part * days, LANES), bf16) for part in split],
        [], 10**9, 4 * 10**6, 1, shared, probes,
    )
    pieces = [{bits: crossed(own, "space", bits) for bits in range(groups - 2, 0, -2)} for own in outgoing]
    results = call(
        functools.partial(local_kernel, dims, len(split)),
        [((blocks, part * days, LANES), f32) for part in split]
        + [
            ((pairs, rows, LANES), bf16),
            ((rows, LANES), f32),
            ((blocks, LANES), bf16),
            ((blocks, LANES, far * LANES), bf16),
            ((blocks, LANES, LANES), bf16),
        ],
        [pltpu.VMEM(*big), pltpu.VMEM((blocks, pairs * days, LANES), bf16)],
        10**10, 10**7, 2,
        near_table, slab_days, probes, local_coupling, remote_coupling, block_inverse, retention,
    )
    running = results[: len(split)]
    moved, retain, product, remote_weight, inverse = results[len(split) :]
    same, other = [], []
    for chunk, part in enumerate(split):
        parts = [outgoing[chunk]] + [pieces[chunk][bits] for bits in range(2, groups, 2)]
        (whole,) = call(assemble_kernel, [((held, part * days, LANES), bf16)], [], 0, 10**6, 0, *parts, product)
        same.append(whole)
        other.append(crossed(whole, "space", 1))
    slabs = lax.axis_size("tm")
    hops = slabs - 1
    exchange = lambda message: [crossed(message, "tm", bits) for bits in range(hops, 0, -1)][::-1]
    inbox = pltpu.VMEM((slabs, pairs + 1, blocks, LANES), bf16)
    message, forcing = product, []
    for chunk, part in enumerate(split):
        drive, message = call(
            functools.partial(forward_kernel, dims, sum(split[:chunk])),
            [((part, rows, LANES), f32), ((pairs + 1, blocks, LANES), bf16)],
            [pltpu.VMEM((2 * held, part * days, LANES), bf16)], 10**8, 10**5, 2,
            far_table, slab_days, running[chunk], same[chunk], other[chunk], remote_weight, inverse, retain, message,
        )
        forcing.append(drive)
    ends = exchange(message)
    adjoint, message = call(
        functools.partial(adjoint_kernel, dims, split, hops),
        [big, ((pairs, blocks, LANES), bf16)],
        [pltpu.VMEM(*big), inbox], 10**10, 10**7, 1,
        slab_days, retain, inverse, *forcing, *ends,
    )
    starts = exchange(message)
    (variance,) = call(
        functools.partial(variance_kernel, dims, hops),
        [((days, blocks * size), f32)],
        [pltpu.VMEM((rows, LANES), f32), pltpu.VMEM((slabs, pairs, blocks, LANES), bf16), inbox], 10**10, 10**7, 0,
        adjoint, retain, moved, *starts, *ends,
    )
    return variance


def solution(mesh):
    placed = (
        P("tm", "space", None),
        P("space", None),
        P("space", None),
        P("space", None),
        P("tm"),
        P("space", None, None, None),
        P("space", None, None, None),
        P("space", None, None),
        P("tm", "space"),
    )
    return jax.shard_map(
        local, mesh=mesh, in_specs=placed, out_specs=P("tm", "space"), check_vma=False
    )
```

```python
import functools

import jax
import jax.numpy as jnp
from jax import lax
from jax.experimental import pallas as pl
from jax.experimental.pallas import tpu as pltpu
from jax.sharding import PartitionSpec as P

LANES = 128
VMEM_LIMIT = 20 * 1024 * 1024
TURNED = (((1,), (1,)), ((), ()))


def permutation(size, probes, start, width):
    total = size * probes
    column = lax.broadcasted_iota(jnp.int32, (total, width), 1) + start
    origin = (column % size) * probes + column // size
    row = lax.broadcasted_iota(jnp.int32, (total, width), 0)
    return (row == origin).astype(jnp.float32).astype(jnp.bfloat16)


def doubled(weight):
    zero = jnp.zeros_like(weight)
    return jnp.concatenate(
        [jnp.concatenate([weight, zero], axis=1), jnp.concatenate([zero, weight], axis=1)], axis=0
    )


def outgoing_kernel(dims, shared_ref, z_ref, outgoing_ref):
    days, blocks, size, probes = dims
    count = outgoing_ref.shape[0]
    z = z_ref[...].reshape(days * blocks, size * probes)
    row = lax.broadcasted_iota(jnp.int32, (days, days * blocks), 0)
    column = lax.broadcasted_iota(jnp.int32, (days, days * blocks), 1)
    picks = [
        (column == row * blocks + shared_ref[0, m]).astype(jnp.float32).astype(jnp.bfloat16) for m in range(count)
    ]
    picked = jnp.dot(jnp.concatenate(picks, axis=0), z, preferred_element_type=jnp.float32).astype(jnp.bfloat16)
    step = 2 * LANES
    for start in range(0, size * probes, step):
        moved = jnp.dot(picked, permutation(size, probes, start, step), preferred_element_type=jnp.float32)
        moved = moved.astype(jnp.bfloat16)
        for half in range(2):
            pair = start // LANES + half
            for m in range(count):
                outgoing_ref[m, pl.ds(pair * days, days), :] = moved[
                    m * days : (m + 1) * days, half * LANES : (half + 1) * LANES
                ]


def local_kernel(
    dims, links_ref, days_ref, z_ref, weight_ref, remote_weight_ref, inverse_ref, retention_ref,
    running_ref, moved_ref, retain_ref, product_ref, remote_doubled_ref, inverse_doubled_ref, stage, turned,
):
    days, blocks, size, probes = dims
    pairs = size * probes // LANES
    count = links_ref.shape[0]
    z = z_ref[...].reshape(days * blocks, size * probes)
    step = 2 * LANES
    for start in range(0, size * probes, step):
        moved = jnp.dot(z, permutation(size, probes, start, step), preferred_element_type=jnp.float32)
        for half in range(2):
            pair = start // LANES + half
            tile = moved[:, half * LANES : (half + 1) * LANES]
            stage[pair] = tile
            moved_ref[pair] = tile.astype(jnp.bfloat16)
    for block in range(blocks):
        for pair in range(pairs):
            rows = stage[pair, pl.ds(block, days, stride=blocks), :]
            turned[block, pl.ds(pair * days, days), :] = rows.astype(jnp.bfloat16)
    for block in range(blocks):
        near = jnp.concatenate([turned[links_ref[k, block]] for k in range(count)], axis=1)
        weight = jnp.concatenate([doubled(weight_ref[block, k]) for k in range(count)], axis=1)
        total = lax.dot_general(near, weight, TURNED, preferred_element_type=jnp.float32)
        running_ref[block] = turned[block].astype(jnp.float32) - total
        remote_doubled_ref[block] = jnp.concatenate(
            [doubled(remote_weight_ref[block, k]) for k in range(remote_weight_ref.shape[1])], axis=1
        )
        inverse_doubled_ref[block] = doubled(inverse_ref[block])
    observed = days_ref[0]
    shape = (days, LANES)
    first = lax.broadcasted_iota(jnp.int32, shape, 1) < size
    seen = lax.broadcasted_iota(jnp.int32, shape, 0) < observed
    for block in range(0, blocks, 2):
        factor = jnp.where(seen, retention_ref[:, pl.ds(block * size, LANES)], 1.0)
        other = pltpu.roll(factor, size, 1)
        retain_ref[pl.ds(block, days, stride=blocks), :] = jnp.where(first, factor, other)
        retain_ref[pl.ds(block + 1, days, stride=blocks), :] = jnp.where(first, other, factor)
    product = jnp.ones((blocks, LANES), jnp.float32)
    for day in range(days):
        product = product * retain_ref[pl.ds(day * blocks, blocks), :]
    high = product.astype(jnp.bfloat16).astype(jnp.float32)
    half = lax.broadcasted_iota(jnp.int32, product.shape, 1) < size
    product_ref[...] = jnp.where(half, high, product - high).astype(jnp.bfloat16)


def pass_kernel(piece_ref, product_ref, out_ref):
    out_ref[...] = piece_ref[...]


def forward_kernel(
    dims, pieces, links_ref, days_ref, running_ref, weight_ref, inverse_ref, retain_ref, product_ref, *rest
):
    days, blocks, size, probes = dims
    piece_refs = rest[: 2 * pieces]
    forcing_ref, message_ref, remote = rest[2 * pieces :]
    pairs = forcing_ref.shape[0]
    count = links_ref.shape[0]
    bound = piece_refs[0].shape[0]
    held = pieces * bound
    me = lax.axis_index("space")
    for k, ref in enumerate(piece_refs):
        remote[pl.ds(k * bound, bound)] = ref[...]
    seen = lax.broadcasted_iota(jnp.int32, (days, LANES), 0) < days_ref[0]
    for block in range(blocks):
        places = []
        for k in range(count):
            link = links_ref[k, block]
            distance = (link // bound) ^ me
            places.append((distance % 2) * held + (distance // 2) * bound + link % bound)
        far = jnp.concatenate([remote[place] for place in places], axis=1)
        total = lax.dot_general(far, weight_ref[block], TURNED, preferred_element_type=jnp.float32)
        source = (running_ref[block] - total).astype(jnp.bfloat16)
        drive = lax.dot_general(source, inverse_ref[block], TURNED, preferred_element_type=jnp.float32)
        for pair in range(pairs):
            forcing_ref[pair, pl.ds(block, days, stride=blocks), :] = jnp.where(
                seen, drive[pair * days : (pair + 1) * days], 0.0
            )
    states = [jnp.zeros((blocks, LANES), jnp.float32)] * pairs
    for day in range(days):
        rows = pl.ds(day * blocks, blocks)
        factor = retain_ref[rows, :]
        for pair in range(pairs):
            states[pair] = factor * states[pair] + forcing_ref[pair, rows, :]
    leave(message_ref, states)
    message_ref[pairs] = product_ref[...]


def leave(message_ref, values):
    for pair, value in enumerate(values):
        message_ref[pair] = value.astype(jnp.bfloat16)


def collect(piece_refs, inbox):
    me = lax.axis_index("tm")
    for k, ref in enumerate(piece_refs):
        inbox[me ^ (k + 1)] = ref[...]


def carried(pairs, inbox, products, backward):
    me, count = lax.axis_index("tm"), inbox.shape[0]
    carries = [jnp.zeros(inbox.shape[2:], jnp.float32)] * pairs
    for slab in range(count - 1, 0, -1) if backward else range(count - 1):
        valid = slab > me if backward else slab < me
        terms = products[slab, pairs].astype(jnp.float32)
        factor = terms + pltpu.roll(terms, LANES // 2, 1)
        for pair in range(pairs):
            update = inbox[slab, pair].astype(jnp.float32) + factor * carries[pair]
            carries[pair] = jnp.where(valid, update, carries[pair])
    return carries


def adjoint_kernel(dims, hops, days_ref, forcing_ref, retain_ref, inverse_ref, *rest):
    days, blocks, size, probes = dims
    pairs = forcing_ref.shape[0]
    adjoint_ref, message_ref, stage, inbox = rest[hops:]
    collect(rest[:hops], inbox)
    seen = lax.broadcasted_iota(jnp.int32, (days, LANES), 0) < days_ref[0]
    states = carried(pairs, inbox, inbox, False)
    for day in range(days):
        rows = pl.ds(day * blocks, blocks)
        factor = retain_ref[rows, :]
        for pair in range(pairs):
            states[pair] = factor * states[pair] + forcing_ref[pair, rows, :]
            stage[pair, rows, :] = states[pair]
    for block in range(blocks):
        stored = jnp.concatenate(
            [stage[pair, pl.ds(block, days, stride=blocks), :].astype(jnp.bfloat16) for pair in range(pairs)], axis=0
        )
        adjoint = jnp.dot(stored, inverse_ref[block], preferred_element_type=jnp.float32)
        for pair in range(pairs):
            adjoint_ref[pair, pl.ds(block, days, stride=blocks), :] = jnp.where(
                seen, adjoint[pair * days : (pair + 1) * days], 0.0
            )
    carries = [jnp.zeros((blocks, LANES), jnp.float32)] * pairs
    for day in reversed(range(days)):
        rows = pl.ds(day * blocks, blocks)
        factor = retain_ref[rows, :]
        for pair in range(pairs):
            carries[pair] = factor * (adjoint_ref[pair, rows, :] + carries[pair])
    leave(message_ref, carries)


def own_kernel(dims, adjoint_ref, retain_ref, moved_ref, partial_ref):
    days, blocks, size, probes = dims
    pairs = adjoint_ref.shape[0]
    carries = [jnp.zeros((blocks, LANES), jnp.float32)] * pairs
    for day in reversed(range(days)):
        rows = pl.ds(day * blocks, blocks)
        factor = retain_ref[rows, :]
        total = None
        for pair in range(pairs):
            smoothed = adjoint_ref[pair, rows, :] + carries[pair]
            carries[pair] = factor * smoothed
            term = smoothed * moved_ref[pair, rows, :].astype(jnp.float32)
            total = term if total is None else total + term
        partial_ref[rows, :] = total


def variance_kernel(dims, hops, partial_ref, retain_ref, moved_ref, *rest):
    days, blocks, size, probes = dims
    pairs = moved_ref.shape[0]
    out_ref, stage, inbox, products = rest[2 * hops :]
    collect(rest[:hops], inbox)
    collect(rest[hops : 2 * hops], products)
    carries = carried(pairs, inbox, products, True)
    reach = jnp.ones((blocks, LANES), jnp.float32)
    for day in reversed(range(days)):
        rows = pl.ds(day * blocks, blocks)
        total = None
        for pair in range(pairs):
            term = carries[pair] * moved_ref[pair, rows, :].astype(jnp.float32)
            total = term if total is None else total + term
        stage[rows, :] = partial_ref[rows, :] + reach * total
        reach = reach * retain_ref[rows, :]
    lane = lax.broadcasted_iota(jnp.int32, (days, LANES), 1)
    for block in range(0, blocks, 2):
        both = [stage[pl.ds(block + half, days, stride=blocks), :] for half in range(2)]
        both = [value + pltpu.roll(value, size, 1) for value in both]
        out_ref[:, pl.ds(block * size, LANES)] = jnp.where(lane < size, both[0], both[1]) * (1.0 / probes)


def call(kernel, outs, scratch, flops, moved, scalars, *operands, apart=(), limit=VMEM_LIMIT):
    in_specs = [
        pl.BlockSpec(memory_space=pltpu.SMEM if i < scalars else pl.ANY if i in apart else pltpu.VMEM)
        for i in range(len(operands))
    ]
    return pl.pallas_call(
        kernel,
        out_shape=[jax.ShapeDtypeStruct(shape, kind) for shape, kind in outs],
        in_specs=in_specs,
        out_specs=[pl.BlockSpec(memory_space=pltpu.VMEM) for _ in outs],
        scratch_shapes=scratch,
        compiler_params=pltpu.CompilerParams(vmem_limit_bytes=limit),
        cost_estimate=pl.CostEstimate(flops=flops, bytes_accessed=moved, transcendentals=0),
    )(*operands)


def crossed(block, axis, bits):
    return lax.ppermute(block, axis, [(i, i ^ bits) for i in range(lax.axis_size(axis))])


def local(
    probes,
    local_links,
    remote_links,
    shared_blocks,
    slab_days,
    local_coupling,
    remote_coupling,
    block_inverse,
    retention,
):
    days, blocks, width = probes.shape
    size = block_inverse.shape[1]
    dims = (days, blocks, size, width // size)
    pairs = width // LANES
    f32, bf16 = jnp.float32, jnp.bfloat16
    bound = shared_blocks.shape[1]
    far = remote_links.shape[1]
    rows = days * blocks
    groups = lax.axis_size("space")
    held = groups // 2 * bound
    near_table, far_table = local_links.T, remote_links.T
    big = ((pairs, rows, LANES), f32)

    (outgoing,) = call(
        functools.partial(outgoing_kernel, dims),
        [((bound, pairs * days, LANES), bf16)],
        [], 10**9, 4 * 10**6, 1, shared_blocks, probes, limit=63 * 1024 * 1024,
    )
    pieces = {bits: crossed(outgoing, "space", bits) for bits in range(groups - 2, 0, -2)}
    running, moved, retain, product, remote_weight, inverse = call(
        functools.partial(local_kernel, dims),
        [
            ((blocks, pairs * days, LANES), f32),
            ((pairs, rows, LANES), bf16),
            ((rows, LANES), f32),
            ((blocks, LANES), bf16),
            ((blocks, LANES, far * LANES), bf16),
            ((blocks, LANES, LANES), bf16),
        ],
        [pltpu.VMEM(*big), pltpu.VMEM((blocks, pairs * days, LANES), bf16)],
        10**10, 10**7, 2,
        near_table, slab_days, probes, local_coupling, remote_coupling, block_inverse, retention,
    )
    same = [outgoing]
    for bits in range(2, groups, 2):
        same += call(pass_kernel, [(outgoing.shape, bf16)], [], 0, 10**5, 0, pieces[bits], product)
    other = [crossed(piece, "space", 1) for piece in same]
    slabs = lax.axis_size("tm")
    hops = slabs - 1
    exchange = lambda message: [crossed(message, "tm", bits) for bits in range(hops, 0, -1)][::-1]
    inbox = pltpu.VMEM((slabs, pairs + 1, blocks, LANES), bf16)
    forcing, message = call(
        functools.partial(forward_kernel, dims, len(same)),
        [big, ((pairs + 1, blocks, LANES), bf16)],
        [pltpu.VMEM((2 * held, pairs * days, LANES), bf16)], 10**10, 10**7, 2,
        far_table, slab_days, running, remote_weight, inverse, retain, product, *same, *other,
    )
    ends = exchange(message)
    adjoint, message = call(
        functools.partial(adjoint_kernel, dims, hops),
        [big, ((pairs, blocks, LANES), bf16)],
        [pltpu.VMEM(*big), inbox], 10**10, 10**7, 1,
        slab_days, forcing, retain, inverse, *ends,
    )
    starts = exchange(message)
    (partial,) = call(
        functools.partial(own_kernel, dims), [((rows, LANES), f32)], [], 10**9, 10**6, 0, adjoint, retain, moved
    )
    (variance,) = call(
        functools.partial(variance_kernel, dims, hops),
        [((days, blocks * size), f32)],
        [pltpu.VMEM((rows, LANES), f32), pltpu.VMEM((slabs, pairs, blocks, LANES), bf16), inbox], 10**10, 10**7, 0,
        partial, retain, moved, *starts, *ends,
    )
    return variance


def solution(mesh):
    placed = (
        P("tm", "space", None),
        P("space", None),
        P("space", None),
        P("space", None),
        P("tm"),
        P("space", None, None, None),
        P("space", None, None, None),
        P("space", None, None),
        P("tm", "space"),
    )
    return jax.shard_map(
        local, mesh=mesh, in_specs=placed, out_specs=P("tm", "space"), check_vma=False
    )
```

```python
import functools

import jax
import jax.numpy as jnp
from jax import lax
from jax.experimental import pallas as pl
from jax.experimental.pallas import tpu as pltpu
from jax.sharding import PartitionSpec as P

LANES = 128
VMEM_LIMIT = 20 * 1024 * 1024
TURNED = (((1,), (1,)), ((), ()))


def permutation(size, probes, start, width):
    total = size * probes
    column = lax.broadcasted_iota(jnp.int32, (total, width), 1) + start
    origin = (column % size) * probes + column // size
    row = lax.broadcasted_iota(jnp.int32, (total, width), 0)
    return (row == origin).astype(jnp.float32).astype(jnp.bfloat16)


def doubled(weight):
    zero = jnp.zeros_like(weight)
    return jnp.concatenate(
        [jnp.concatenate([weight, zero], axis=1), jnp.concatenate([zero, weight], axis=1)], axis=0
    )


def outgoing_kernel(dims, shared_ref, z_ref, outgoing_ref, total):
    days, blocks, size, probes = dims
    count = outgoing_ref.shape[0]
    step, width = pl.program_id(0), z_ref.shape[2]
    z = z_ref[...].reshape(days * blocks, width)
    row = lax.broadcasted_iota(jnp.int32, (days, days * blocks), 0)
    column = lax.broadcasted_iota(jnp.int32, (days, days * blocks), 1)
    picks = [
        (column == row * blocks + shared_ref[0, m]).astype(jnp.float32).astype(jnp.bfloat16) for m in range(count)
    ]
    picked = jnp.dot(jnp.concatenate(picks, axis=0), z, preferred_element_type=jnp.float32).astype(jnp.bfloat16)
    place = lax.broadcasted_iota(jnp.int32, (width, size * probes), 1)
    origin = (place % size) * probes + place // size - step * width
    move = (lax.broadcasted_iota(jnp.int32, (width, size * probes), 0) == origin).astype(jnp.float32)
    moved = jnp.dot(picked, move.astype(jnp.bfloat16), preferred_element_type=jnp.float32)

    @pl.when(step == 0)
    def _():
        total[...] = moved

    @pl.when(step > 0)
    def _():
        total[...] += moved

    @pl.when(step == pl.num_programs(0) - 1)
    def _():
        for pair in range(size * probes // LANES):
            for m in range(count):
                outgoing_ref[m, pl.ds(pair * days, days), :] = total[
                    pl.ds(m * days, days), pl.ds(pair * LANES, LANES)
                ].astype(jnp.bfloat16)


def local_kernel(
    dims, links_ref, days_ref, z_ref, weight_ref, remote_weight_ref, inverse_ref, retention_ref,
    running_ref, moved_ref, retain_ref, product_ref, remote_doubled_ref, inverse_doubled_ref, stage, turned,
):
    days, blocks, size, probes = dims
    pairs = size * probes // LANES
    count = links_ref.shape[0]
    z = z_ref[...].reshape(days * blocks, size * probes)
    step = 2 * LANES
    for start in range(0, size * probes, step):
        moved = jnp.dot(z, permutation(size, probes, start, step), preferred_element_type=jnp.float32)
        for half in range(2):
            pair = start // LANES + half
            tile = moved[:, half * LANES : (half + 1) * LANES]
            stage[pair] = tile
            moved_ref[pair] = tile.astype(jnp.bfloat16)
    for block in range(blocks):
        for pair in range(pairs):
            rows = stage[pair, pl.ds(block, days, stride=blocks), :]
            turned[block, pl.ds(pair * days, days), :] = rows.astype(jnp.bfloat16)
    for block in range(blocks):
        near = jnp.concatenate([turned[links_ref[k, block]] for k in range(count)], axis=1)
        weight = jnp.concatenate([doubled(weight_ref[block, k]) for k in range(count)], axis=1)
        total = lax.dot_general(near, weight, TURNED, preferred_element_type=jnp.float32)
        running_ref[block] = turned[block].astype(jnp.float32) - total
        remote_doubled_ref[block] = jnp.concatenate(
            [doubled(remote_weight_ref[block, k]) for k in range(remote_weight_ref.shape[1])], axis=1
        )
        inverse_doubled_ref[block] = doubled(inverse_ref[block])
    observed = days_ref[0]
    shape = (days, LANES)
    first = lax.broadcasted_iota(jnp.int32, shape, 1) < size
    seen = lax.broadcasted_iota(jnp.int32, shape, 0) < observed
    for block in range(0, blocks, 2):
        factor = jnp.where(seen, retention_ref[:, pl.ds(block * size, LANES)], 1.0)
        other = pltpu.roll(factor, size, 1)
        retain_ref[pl.ds(block, days, stride=blocks), :] = jnp.where(first, factor, other)
        retain_ref[pl.ds(block + 1, days, stride=blocks), :] = jnp.where(first, other, factor)
    product = jnp.ones((blocks, LANES), jnp.float32)
    for day in range(days):
        product = product * retain_ref[pl.ds(day * blocks, blocks), :]
    high = product.astype(jnp.bfloat16).astype(jnp.float32)
    half = lax.broadcasted_iota(jnp.int32, product.shape, 1) < size
    product_ref[...] = jnp.where(half, high, product - high).astype(jnp.bfloat16)


def pass_kernel(piece_ref, product_ref, out_ref):
    out_ref[...] = piece_ref[...]


def forward_kernel(
    dims, pieces, links_ref, days_ref, running_ref, weight_ref, inverse_ref, retain_ref, product_ref, *rest
):
    days, blocks, size, probes = dims
    piece_refs = rest[: 2 * pieces]
    forcing_ref, message_ref, remote, source = rest[2 * pieces :]
    pairs = forcing_ref.shape[0]
    count = links_ref.shape[0]
    bound = piece_refs[0].shape[0]
    held = pieces * bound
    me = lax.axis_index("space")
    for k, ref in enumerate(piece_refs):
        remote[pl.ds(k * bound, bound)] = ref[...]
    seen = lax.broadcasted_iota(jnp.int32, (days, LANES), 0) < days_ref[0]
    for block in range(blocks):
        places = []
        for k in range(count):
            link = links_ref[k, block]
            distance = (link // bound) ^ me
            places.append((distance % 2) * held + (distance // 2) * bound + link % bound)
        far = jnp.concatenate([remote[place] for place in places], axis=1)
        total = lax.dot_general(far, weight_ref[block], TURNED, preferred_element_type=jnp.float32)
        source[block] = (running_ref[block] - total).astype(jnp.bfloat16)
    for block in range(blocks):
        drive = lax.dot_general(source[block], inverse_ref[block], TURNED, preferred_element_type=jnp.float32)
        for pair in range(pairs):
            forcing_ref[pair, pl.ds(block, days, stride=blocks), :] = jnp.where(
                seen, drive[pair * days : (pair + 1) * days], 0.0
            )
    states = [jnp.zeros((blocks, LANES), jnp.float32)] * pairs
    for day in range(days):
        rows = pl.ds(day * blocks, blocks)
        factor = retain_ref[rows, :]
        for pair in range(pairs):
            states[pair] = factor * states[pair] + forcing_ref[pair, rows, :]
    leave(message_ref, states)
    message_ref[pairs] = product_ref[...]


def leave(message_ref, values):
    for pair, value in enumerate(values):
        message_ref[pair] = value.astype(jnp.bfloat16)


def collect(piece_refs, inbox):
    me = lax.axis_index("tm")
    for k, ref in enumerate(piece_refs):
        inbox[me ^ (k + 1)] = ref[...]


def carried(pairs, inbox, products, backward):
    me, count = lax.axis_index("tm"), inbox.shape[0]
    carries = [jnp.zeros(inbox.shape[2:], jnp.float32)] * pairs
    for slab in range(count - 1, 0, -1) if backward else range(count - 1):
        valid = slab > me if backward else slab < me
        terms = products[slab, pairs].astype(jnp.float32)
        factor = terms + pltpu.roll(terms, LANES // 2, 1)
        for pair in range(pairs):
            update = inbox[slab, pair].astype(jnp.float32) + factor * carries[pair]
            carries[pair] = jnp.where(valid, update, carries[pair])
    return carries


def adjoint_kernel(dims, hops, days_ref, forcing_ref, retain_ref, inverse_ref, *rest):
    days, blocks, size, probes = dims
    pairs = forcing_ref.shape[0]
    adjoint_ref, message_ref, stage, inbox = rest[hops:]
    collect(rest[:hops], inbox)
    seen = lax.broadcasted_iota(jnp.int32, (days, LANES), 0) < days_ref[0]
    states = carried(pairs, inbox, inbox, False)
    for day in range(days):
        rows = pl.ds(day * blocks, blocks)
        factor = retain_ref[rows, :]
        for pair in range(pairs):
            states[pair] = factor * states[pair] + forcing_ref[pair, rows, :]
            stage[pair, rows, :] = states[pair]
    for block in range(blocks):
        stored = jnp.concatenate(
            [stage[pair, pl.ds(block, days, stride=blocks), :].astype(jnp.bfloat16) for pair in range(pairs)], axis=0
        )
        adjoint = jnp.dot(stored, inverse_ref[block], preferred_element_type=jnp.float32)
        for pair in range(pairs):
            adjoint_ref[pair, pl.ds(block, days, stride=blocks), :] = jnp.where(
                seen, adjoint[pair * days : (pair + 1) * days], 0.0
            )
    carries = [jnp.zeros((blocks, LANES), jnp.float32)] * pairs
    for day in reversed(range(days)):
        rows = pl.ds(day * blocks, blocks)
        factor = retain_ref[rows, :]
        for pair in range(pairs):
            carries[pair] = factor * (adjoint_ref[pair, rows, :] + carries[pair])
    leave(message_ref, carries)


def own_kernel(dims, adjoint_ref, retain_ref, moved_ref, partial_ref):
    days, blocks, size, probes = dims
    pairs = adjoint_ref.shape[0]
    carries = [jnp.zeros((blocks, LANES), jnp.float32)] * pairs
    for day in reversed(range(days)):
        rows = pl.ds(day * blocks, blocks)
        factor = retain_ref[rows, :]
        total = None
        for pair in range(pairs):
            smoothed = adjoint_ref[pair, rows, :] + carries[pair]
            carries[pair] = factor * smoothed
            term = smoothed * moved_ref[pair, rows, :].astype(jnp.float32)
            total = term if total is None else total + term
        partial_ref[rows, :] = total


def variance_kernel(dims, hops, partial_ref, retain_ref, moved_ref, *rest):
    days, blocks, size, probes = dims
    pairs = moved_ref.shape[0]
    out_ref, stage, inbox, products = rest[2 * hops :]
    collect(rest[:hops], inbox)
    collect(rest[hops : 2 * hops], products)
    carries = carried(pairs, inbox, products, True)
    reach = jnp.ones((blocks, LANES), jnp.float32)
    for day in reversed(range(days)):
        rows = pl.ds(day * blocks, blocks)
        total = None
        for pair in range(pairs):
            term = carries[pair] * moved_ref[pair, rows, :].astype(jnp.float32)
            total = term if total is None else total + term
        stage[rows, :] = partial_ref[rows, :] + reach * total
        reach = reach * retain_ref[rows, :]
    lane = lax.broadcasted_iota(jnp.int32, (days, LANES), 1)
    for block in range(0, blocks, 2):
        both = [stage[pl.ds(block + half, days, stride=blocks), :] for half in range(2)]
        both = [value + pltpu.roll(value, size, 1) for value in both]
        out_ref[:, pl.ds(block * size, LANES)] = jnp.where(lane < size, both[0], both[1]) * (1.0 / probes)


def call(kernel, outs, scratch, flops, moved, scalars, *operands, apart=(), limit=VMEM_LIMIT):
    in_specs = [
        pl.BlockSpec(memory_space=pltpu.SMEM if i < scalars else pl.ANY if i in apart else pltpu.VMEM)
        for i in range(len(operands))
    ]
    return pl.pallas_call(
        kernel,
        out_shape=[jax.ShapeDtypeStruct(shape, kind) for shape, kind in outs],
        in_specs=in_specs,
        out_specs=[pl.BlockSpec(memory_space=pltpu.VMEM) for _ in outs],
        scratch_shapes=scratch,
        compiler_params=pltpu.CompilerParams(vmem_limit_bytes=limit),
        cost_estimate=pl.CostEstimate(flops=flops, bytes_accessed=moved, transcendentals=0),
    )(*operands)


def crossed(block, axis, bits):
    return lax.ppermute(block, axis, [(i, i ^ bits) for i in range(lax.axis_size(axis))])


def local(
    probes,
    local_links,
    remote_links,
    shared_blocks,
    slab_days,
    local_coupling,
    remote_coupling,
    block_inverse,
    retention,
):
    days, blocks, width = probes.shape
    size = block_inverse.shape[1]
    dims = (days, blocks, size, width // size)
    pairs = width // LANES
    f32, bf16 = jnp.float32, jnp.bfloat16
    bound = shared_blocks.shape[1]
    far = remote_links.shape[1]
    rows = days * blocks
    groups = lax.axis_size("space")
    held = groups // 2 * bound
    near_table, far_table = local_links.T, remote_links.T
    big = ((pairs, rows, LANES), f32)

    steps = 4
    outgoing = pl.pallas_call(
        functools.partial(outgoing_kernel, dims),
        out_shape=jax.ShapeDtypeStruct((bound, pairs * days, LANES), bf16),
        grid=(steps,),
        in_specs=[
            pl.BlockSpec(memory_space=pltpu.SMEM),
            pl.BlockSpec((days, blocks, width // steps), lambda step: (0, 0, step)),
        ],
        out_specs=pl.BlockSpec((bound, pairs * days, LANES), lambda step: (0, 0, 0)),
        scratch_shapes=[pltpu.VMEM((bound * days, width), f32)],
        compiler_params=pltpu.CompilerParams(vmem_limit_bytes=63 * 1024 * 1024),
        cost_estimate=pl.CostEstimate(flops=10**9, bytes_accessed=4 * 10**6, transcendentals=0),
    )(shared_blocks, probes)
    pieces = {bits: crossed(outgoing, "space", bits) for bits in range(groups - 2, 0, -2)}
    running, moved, retain, product, remote_weight, inverse = call(
        functools.partial(local_kernel, dims),
        [
            ((blocks, pairs * days, LANES), f32),
            ((pairs, rows, LANES), bf16),
            ((rows, LANES), f32),
            ((blocks, LANES), bf16),
            ((blocks, LANES, far * LANES), bf16),
            ((blocks, LANES, LANES), bf16),
        ],
        [pltpu.VMEM(*big), pltpu.VMEM((blocks, pairs * days, LANES), bf16)],
        10**10, 10**7, 2,
        near_table, slab_days, probes, local_coupling, remote_coupling, block_inverse, retention,
    )
    same = [outgoing]
    for bits in range(2, groups, 2):
        same += call(pass_kernel, [(outgoing.shape, bf16)], [], 0, 10**5, 0, pieces[bits], product)
    other = [crossed(piece, "space", 1) for piece in same]
    slabs = lax.axis_size("tm")
    hops = slabs - 1
    exchange = lambda message: [crossed(message, "tm", bits) for bits in range(hops, 0, -1)][::-1]
    inbox = pltpu.VMEM((slabs, pairs + 1, blocks, LANES), bf16)
    forcing, message = call(
        functools.partial(forward_kernel, dims, len(same)),
        [big, ((pairs + 1, blocks, LANES), bf16)],
        [pltpu.VMEM((2 * held, pairs * days, LANES), bf16), pltpu.VMEM((blocks, pairs * days, LANES), bf16)],
        10**10, 10**7, 2,
        far_table, slab_days, running, remote_weight, inverse, retain, product, *same, *other,
    )
    ends = exchange(message)
    adjoint, message = call(
        functools.partial(adjoint_kernel, dims, hops),
        [big, ((pairs, blocks, LANES), bf16)],
        [pltpu.VMEM(*big), inbox], 10**10, 10**7, 1,
        slab_days, forcing, retain, inverse, *ends,
    )
    starts = exchange(message)
    (partial,) = call(
        functools.partial(own_kernel, dims), [((rows, LANES), f32)], [], 10**9, 10**6, 0, adjoint, retain, moved
    )
    (variance,) = call(
        functools.partial(variance_kernel, dims, hops),
        [((days, blocks * size), f32)],
        [pltpu.VMEM((rows, LANES), f32), pltpu.VMEM((slabs, pairs, blocks, LANES), bf16), inbox], 10**10, 10**7, 0,
        partial, retain, moved, *starts, *ends,
    )
    return variance


def solution(mesh):
    placed = (
        P("tm", "space", None),
        P("space", None),
        P("space", None),
        P("space", None),
        P("tm"),
        P("space", None, None, None),
        P("space", None, None, None),
        P("space", None, None),
        P("tm", "space"),
    )
    return jax.shard_map(
        local, mesh=mesh, in_specs=placed, out_specs=P("tm", "space"), check_vma=False
    )
```

```python
import functools

import jax
import jax.numpy as jnp
from jax import lax
from jax.experimental import pallas as pl
from jax.experimental.pallas import tpu as pltpu
from jax.sharding import PartitionSpec as P

LANES = 128
VMEM_LIMIT = 20 * 1024 * 1024
TURNED = (((1,), (1,)), ((), ()))


def permutation(size, probes, start, width):
    total = size * probes
    column = lax.broadcasted_iota(jnp.int32, (total, width), 1) + start
    origin = (column % size) * probes + column // size
    row = lax.broadcasted_iota(jnp.int32, (total, width), 0)
    return (row == origin).astype(jnp.float32).astype(jnp.bfloat16)


def doubled(weight):
    zero = jnp.zeros_like(weight)
    return jnp.concatenate(
        [jnp.concatenate([weight, zero], axis=1), jnp.concatenate([zero, weight], axis=1)], axis=0
    )


def outgoing_kernel(dims, shared_ref, z_ref, outgoing_ref):
    days, blocks, size, probes = dims
    count = outgoing_ref.shape[0]
    z = z_ref[...].reshape(days * blocks, size * probes)
    row = lax.broadcasted_iota(jnp.int32, (days, days * blocks), 0)
    column = lax.broadcasted_iota(jnp.int32, (days, days * blocks), 1)
    picks = [
        (column == row * blocks + shared_ref[0, m]).astype(jnp.float32).astype(jnp.bfloat16) for m in range(count)
    ]
    picked = jnp.dot(jnp.concatenate(picks, axis=0), z, preferred_element_type=jnp.float32).astype(jnp.bfloat16)
    step = 2 * LANES
    for start in range(0, size * probes, step):
        moved = jnp.dot(picked, permutation(size, probes, start, step), preferred_element_type=jnp.float32)
        moved = moved.astype(jnp.bfloat16)
        for half in range(2):
            pair = start // LANES + half
            for m in range(count):
                outgoing_ref[m, pl.ds(pair * days, days), :] = moved[
                    m * days : (m + 1) * days, half * LANES : (half + 1) * LANES
                ]


def local_kernel(
    dims, links_ref, days_ref, z_ref, weight_ref, remote_weight_ref, inverse_ref, retention_ref,
    running_ref, moved_ref, retain_ref, product_ref, remote_doubled_ref, inverse_doubled_ref, stage, turned,
):
    days, blocks, size, probes = dims
    pairs = size * probes // LANES
    count = links_ref.shape[0]
    z = z_ref[...].reshape(days * blocks, size * probes)
    step = 2 * LANES
    for start in range(0, size * probes, step):
        moved = jnp.dot(z, permutation(size, probes, start, step), preferred_element_type=jnp.float32)
        for half in range(2):
            pair = start // LANES + half
            tile = moved[:, half * LANES : (half + 1) * LANES]
            stage[pair] = tile
            moved_ref[pair] = tile.astype(jnp.bfloat16)
    for block in range(blocks):
        for pair in range(pairs):
            rows = stage[pair, pl.ds(block, days, stride=blocks), :]
            turned[block, pl.ds(pair * days, days), :] = rows.astype(jnp.bfloat16)
    for block in range(blocks):
        near = jnp.concatenate([turned[links_ref[k, block]] for k in range(count)], axis=1)
        weight = jnp.concatenate([doubled(weight_ref[block, k]) for k in range(count)], axis=1)
        total = lax.dot_general(near, weight, TURNED, preferred_element_type=jnp.float32)
        running_ref[block] = turned[block].astype(jnp.float32) - total
        remote_doubled_ref[block] = jnp.concatenate(
            [doubled(remote_weight_ref[block, k]) for k in range(remote_weight_ref.shape[1])], axis=1
        )
        inverse_doubled_ref[block] = doubled(inverse_ref[block])
    observed = days_ref[0]
    shape = (days, LANES)
    first = lax.broadcasted_iota(jnp.int32, shape, 1) < size
    seen = lax.broadcasted_iota(jnp.int32, shape, 0) < observed
    for block in range(0, blocks, 2):
        factor = jnp.where(seen, retention_ref[:, pl.ds(block * size, LANES)], 1.0)
        other = pltpu.roll(factor, size, 1)
        retain_ref[pl.ds(block, days, stride=blocks), :] = jnp.where(first, factor, other)
        retain_ref[pl.ds(block + 1, days, stride=blocks), :] = jnp.where(first, other, factor)
    product = jnp.ones((blocks, LANES), jnp.float32)
    for day in range(days):
        product = product * retain_ref[pl.ds(day * blocks, blocks), :]
    product_ref[...] = packed(product, size)


def packed(value, size):
    high = value.astype(jnp.bfloat16).astype(jnp.float32)
    half = lax.broadcasted_iota(jnp.int32, value.shape, 1) < size
    return jnp.where(half, high, value - high).astype(jnp.bfloat16)


def unpacked(terms):
    terms = terms.astype(jnp.float32)
    return terms + pltpu.roll(terms, LANES // 2, 1)


def pass_kernel(piece_ref, product_ref, out_ref):
    out_ref[...] = piece_ref[...]


def forward_kernel(
    dims, pieces, links_ref, days_ref, running_ref, weight_ref, inverse_ref, retain_ref, product_ref, *rest
):
    days, blocks, size, probes = dims
    piece_refs = rest[: 2 * pieces]
    forcing_ref, message_ref, remote, source = rest[2 * pieces :]
    pairs = forcing_ref.shape[0]
    count = links_ref.shape[0]
    bound = piece_refs[0].shape[0]
    held = pieces * bound
    me = lax.axis_index("space")
    for k, ref in enumerate(piece_refs):
        remote[pl.ds(k * bound, bound)] = ref[...]
    seen = lax.broadcasted_iota(jnp.int32, (days, LANES), 0) < days_ref[0]
    for block in range(blocks):
        places = []
        for k in range(count):
            link = links_ref[k, block]
            distance = (link // bound) ^ me
            places.append((distance % 2) * held + (distance // 2) * bound + link % bound)
        far = jnp.concatenate([remote[place] for place in places], axis=1)
        total = lax.dot_general(far, weight_ref[block], TURNED, preferred_element_type=jnp.float32)
        source[block] = (running_ref[block] - total).astype(jnp.bfloat16)
    for block in range(blocks):
        drive = lax.dot_general(source[block], inverse_ref[block], TURNED, preferred_element_type=jnp.float32)
        for pair in range(pairs):
            forcing_ref[pair, pl.ds(block, days, stride=blocks), :] = jnp.where(
                seen, drive[pair * days : (pair + 1) * days], 0.0
            )
    states = [jnp.zeros((blocks, LANES), jnp.float32)] * pairs
    for day in range(days):
        rows = pl.ds(day * blocks, blocks)
        factor = retain_ref[rows, :]
        for pair in range(pairs):
            states[pair] = factor * states[pair] + forcing_ref[pair, rows, :]
    leave(message_ref, states)
    message_ref[pairs] = product_ref[...]


def leave(message_ref, values):
    for pair, value in enumerate(values):
        message_ref[pair] = value.astype(jnp.bfloat16)


def carried(pairs, value_refs, factor_refs, backward):
    me = lax.axis_index("tm")
    shape = value_refs[0].shape[1:]
    carries, through = [jnp.zeros(shape, jnp.float32)] * pairs, jnp.ones(shape, jnp.float32)
    for level, (values, factors) in enumerate(zip(value_refs, factor_refs)):
        valid = (me >> level) % 2 == (0 if backward else 1)
        for pair in range(pairs):
            update = carries[pair] + through * values[pair].astype(jnp.float32)
            carries[pair] = jnp.where(valid, update, carries[pair])
        through = jnp.where(valid, through * unpacked(factors[pairs]), through)
    return carries


def merge_kernel(dims, level, backward, mine_ref, other_ref, mine_factor_ref, other_factor_ref, merged_ref):
    days, blocks, size, probes = dims
    pairs = size * probes // LANES
    upper = (lax.axis_index("tm") >> level) % 2 == 1
    mine_factor, other_factor = unpacked(mine_factor_ref[pairs]), unpacked(other_factor_ref[pairs])
    mine_last = jnp.logical_xor(upper, backward)
    factor = jnp.where(mine_last, mine_factor, other_factor)
    for pair in range(pairs):
        mine, other = mine_ref[pair].astype(jnp.float32), other_ref[pair].astype(jnp.float32)
        last, first = jnp.where(mine_last, mine, other), jnp.where(mine_last, other, mine)
        merged_ref[pair] = (last + factor * first).astype(jnp.bfloat16)
    if merged_ref.shape[0] > pairs:
        merged_ref[pairs] = packed(mine_factor * other_factor, size)


def adjoint_kernel(dims, hops, days_ref, forcing_ref, retain_ref, inverse_ref, *rest):
    days, blocks, size, probes = dims
    pairs = forcing_ref.shape[0]
    adjoint_ref, message_ref, stage, stored = rest[hops:]
    seen = lax.broadcasted_iota(jnp.int32, (days, LANES), 0) < days_ref[0]
    states = carried(pairs, rest[:hops], rest[:hops], False)
    for day in range(days):
        rows = pl.ds(day * blocks, blocks)
        factor = retain_ref[rows, :]
        for pair in range(pairs):
            states[pair] = factor * states[pair] + forcing_ref[pair, rows, :]
            stage[pair, rows, :] = states[pair]
    for block in range(blocks):
        for pair in range(pairs):
            rows = stage[pair, pl.ds(block, days, stride=blocks), :]
            stored[block, pl.ds(pair * days, days), :] = rows.astype(jnp.bfloat16)
    for block in range(blocks):
        adjoint = jnp.dot(stored[block], inverse_ref[block], preferred_element_type=jnp.float32)
        for pair in range(pairs):
            adjoint_ref[pair, pl.ds(block, days, stride=blocks), :] = jnp.where(
                seen, adjoint[pair * days : (pair + 1) * days], 0.0
            )
    carries = [jnp.zeros((blocks, LANES), jnp.float32)] * pairs
    for day in reversed(range(days)):
        rows = pl.ds(day * blocks, blocks)
        factor = retain_ref[rows, :]
        for pair in range(pairs):
            carries[pair] = factor * (adjoint_ref[pair, rows, :] + carries[pair])
    leave(message_ref, carries)


def own_kernel(dims, adjoint_ref, retain_ref, moved_ref, partial_ref):
    days, blocks, size, probes = dims
    pairs = adjoint_ref.shape[0]
    carries = [jnp.zeros((blocks, LANES), jnp.float32)] * pairs
    for day in reversed(range(days)):
        rows = pl.ds(day * blocks, blocks)
        factor = retain_ref[rows, :]
        total = None
        for pair in range(pairs):
            smoothed = adjoint_ref[pair, rows, :] + carries[pair]
            carries[pair] = factor * smoothed
            term = smoothed * moved_ref[pair, rows, :].astype(jnp.float32)
            total = term if total is None else total + term
        partial_ref[rows, :] = total


def variance_kernel(dims, hops, partial_ref, retain_ref, moved_ref, *rest):
    days, blocks, size, probes = dims
    pairs = moved_ref.shape[0]
    out_ref, stage = rest[2 * hops :]
    carries = carried(pairs, rest[:hops], rest[hops : 2 * hops], True)
    reach = jnp.ones((blocks, LANES), jnp.float32)
    for day in reversed(range(days)):
        rows = pl.ds(day * blocks, blocks)
        total = None
        for pair in range(pairs):
            term = carries[pair] * moved_ref[pair, rows, :].astype(jnp.float32)
            total = term if total is None else total + term
        stage[rows, :] = partial_ref[rows, :] + reach * total
        reach = reach * retain_ref[rows, :]
    lane = lax.broadcasted_iota(jnp.int32, (days, LANES), 1)
    for block in range(0, blocks, 2):
        both = [stage[pl.ds(block + half, days, stride=blocks), :] for half in range(2)]
        both = [value + pltpu.roll(value, size, 1) for value in both]
        out_ref[:, pl.ds(block * size, LANES)] = jnp.where(lane < size, both[0], both[1]) * (1.0 / probes)


def call(kernel, outs, scratch, flops, moved, scalars, *operands, apart=(), limit=VMEM_LIMIT):
    in_specs = [
        pl.BlockSpec(memory_space=pltpu.SMEM if i < scalars else pl.ANY if i in apart else pltpu.VMEM)
        for i in range(len(operands))
    ]
    return pl.pallas_call(
        kernel,
        out_shape=[jax.ShapeDtypeStruct(shape, kind) for shape, kind in outs],
        in_specs=in_specs,
        out_specs=[pl.BlockSpec(memory_space=pltpu.VMEM) for _ in outs],
        scratch_shapes=scratch,
        compiler_params=pltpu.CompilerParams(vmem_limit_bytes=limit),
        cost_estimate=pl.CostEstimate(flops=flops, bytes_accessed=moved, transcendentals=0),
    )(*operands)


def crossed(block, axis, bits):
    return lax.ppermute(block, axis, [(i, i ^ bits) for i in range(lax.axis_size(axis))])


def local(
    probes,
    local_links,
    remote_links,
    shared_blocks,
    slab_days,
    local_coupling,
    remote_coupling,
    block_inverse,
    retention,
):
    days, blocks, width = probes.shape
    size = block_inverse.shape[1]
    dims = (days, blocks, size, width // size)
    pairs = width // LANES
    f32, bf16 = jnp.float32, jnp.bfloat16
    bound = shared_blocks.shape[1]
    far = remote_links.shape[1]
    rows = days * blocks
    groups = lax.axis_size("space")
    held = groups // 2 * bound
    near_table, far_table = local_links.T, remote_links.T
    big = ((pairs, rows, LANES), f32)

    (outgoing,) = call(
        functools.partial(outgoing_kernel, dims),
        [((bound, pairs * days, LANES), bf16)],
        [], 10**9, 4 * 10**6, 1, shared_blocks, probes, limit=63 * 1024 * 1024,
    )
    pieces = {bits: crossed(outgoing, "space", bits) for bits in range(groups - 2, 0, -2)}
    running, moved, retain, product, remote_weight, inverse = call(
        functools.partial(local_kernel, dims),
        [
            ((blocks, pairs * days, LANES), f32),
            ((pairs, rows, LANES), bf16),
            ((rows, LANES), f32),
            ((blocks, LANES), bf16),
            ((blocks, LANES, far * LANES), bf16),
            ((blocks, LANES, LANES), bf16),
        ],
        [pltpu.VMEM(*big), pltpu.VMEM((blocks, pairs * days, LANES), bf16)],
        10**10, 10**7, 2,
        near_table, slab_days, probes, local_coupling, remote_coupling, block_inverse, retention,
    )
    same = [outgoing]
    for bits in range(2, groups, 2):
        same += call(pass_kernel, [(outgoing.shape, bf16)], [], 0, 10**5, 0, pieces[bits], product)
    other = [crossed(piece, "space", 1) for piece in same]
    hops = (lax.axis_size("tm") - 1).bit_length()

    def exchange(message, factors, others, backward):
        sent, received = [message], []
        for level in range(hops):
            received.append(crossed(sent[level], "tm", 1 << level))
            if level < hops - 1:
                mine, other = (factors[level], others[level]) if backward else (sent[level], received[level])
                sent += call(
                    functools.partial(merge_kernel, dims, level, backward),
                    [(message.shape, bf16)], [], 0, 10**5, 0, sent[level], received[level], mine, other,
                )
        return sent, received

    forcing, message = call(
        functools.partial(forward_kernel, dims, len(same)),
        [big, ((pairs + 1, blocks, LANES), bf16)],
        [pltpu.VMEM((2 * held, pairs * days, LANES), bf16), pltpu.VMEM((blocks, pairs * days, LANES), bf16)],
        10**10, 10**7, 2,
        far_table, slab_days, running, remote_weight, inverse, retain, product, *same, *other,
    )
    sent, ends = exchange(message, None, None, False)
    adjoint, message = call(
        functools.partial(adjoint_kernel, dims, hops),
        [big, ((pairs, blocks, LANES), bf16)],
        [pltpu.VMEM(*big), pltpu.VMEM((blocks, pairs * days, LANES), bf16)], 10**10, 10**7, 1,
        slab_days, forcing, retain, inverse, *ends,
    )
    _, starts = exchange(message, sent, ends, True)
    (partial,) = call(
        functools.partial(own_kernel, dims), [((rows, LANES), f32)], [], 10**9, 10**6, 0, adjoint, retain, moved
    )
    (variance,) = call(
        functools.partial(variance_kernel, dims, hops),
        [((days, blocks * size), f32)],
        [pltpu.VMEM((rows, LANES), f32)], 10**10, 10**7, 0,
        partial, retain, moved, *starts, *ends,
    )
    return variance


def solution(mesh):
    placed = (
        P("tm", "space", None),
        P("space", None),
        P("space", None),
        P("space", None),
        P("tm"),
        P("space", None, None, None),
        P("space", None, None, None),
        P("space", None, None),
        P("tm", "space"),
    )
    return jax.shard_map(
        local, mesh=mesh, in_specs=placed, out_specs=P("tm", "space"), check_vma=False
    )
```

```python
import functools

import jax
import jax.numpy as jnp
from jax import lax
from jax.experimental import pallas as pl
from jax.experimental.pallas import tpu as pltpu
from jax.sharding import PartitionSpec as P

LANES = 128
VMEM_LIMIT = 20 * 1024 * 1024
TURNED = (((1,), (1,)), ((), ()))


def permutation(size, probes, start, width):
    total = size * probes
    column = lax.broadcasted_iota(jnp.int32, (total, width), 1) + start
    origin = (column % size) * probes + column // size
    row = lax.broadcasted_iota(jnp.int32, (total, width), 0)
    return (row == origin).astype(jnp.float32).astype(jnp.bfloat16)


def doubled(weight):
    zero = jnp.zeros_like(weight)
    return jnp.concatenate(
        [jnp.concatenate([weight, zero], axis=1), jnp.concatenate([zero, weight], axis=1)], axis=0
    )


def paired(tiles):
    return jnp.concatenate([jnp.concatenate(tiles[half::2], axis=0) for half in range(2)], axis=1)


def unpaired(value, days):
    return [
        value[row : row + days, lane : lane + LANES] for row in range(0, value.shape[0], days) for lane in (0, LANES)
    ]


def outgoing_kernel(dims, shared_ref, z_ref, outgoing_ref):
    days, blocks, size, probes = dims
    count = outgoing_ref.shape[0]
    z = z_ref[...].reshape(days * blocks, size * probes)
    row = lax.broadcasted_iota(jnp.int32, (days, days * blocks), 0)
    column = lax.broadcasted_iota(jnp.int32, (days, days * blocks), 1)
    picks = [
        (column == row * blocks + shared_ref[0, m]).astype(jnp.float32).astype(jnp.bfloat16) for m in range(count)
    ]
    picked = jnp.dot(jnp.concatenate(picks, axis=0), z, preferred_element_type=jnp.float32).astype(jnp.bfloat16)
    step = 2 * LANES
    for start in range(0, size * probes, step):
        moved = jnp.dot(picked, permutation(size, probes, start, step), preferred_element_type=jnp.float32)
        moved = moved.astype(jnp.bfloat16)
        for half in range(2):
            pair = start // LANES + half
            for m in range(count):
                outgoing_ref[m, pl.ds(pair * days, days), :] = moved[
                    m * days : (m + 1) * days, half * LANES : (half + 1) * LANES
                ]


def local_kernel(
    dims, links_ref, days_ref, z_ref, weight_ref, remote_weight_ref, inverse_ref, retention_ref,
    running_ref, moved_ref, retain_ref, product_ref, remote_doubled_ref, inverse_fourfold_ref, stage, turned,
):
    days, blocks, size, probes = dims
    pairs = size * probes // LANES
    count = links_ref.shape[0]
    z = z_ref[...].reshape(days * blocks, size * probes)
    step = 2 * LANES
    for start in range(0, size * probes, step):
        moved = jnp.dot(z, permutation(size, probes, start, step), preferred_element_type=jnp.float32)
        for half in range(2):
            pair = start // LANES + half
            tile = moved[:, half * LANES : (half + 1) * LANES]
            stage[pair] = tile
            moved_ref[pair] = tile.astype(jnp.bfloat16)
    for block in range(blocks):
        for pair in range(pairs):
            rows = stage[pair, pl.ds(block, days, stride=blocks), :]
            turned[block, pl.ds(pair * days, days), :] = rows.astype(jnp.bfloat16)
    for block in range(blocks):
        near = jnp.concatenate([turned[links_ref[k, block]] for k in range(count)], axis=1)
        weight = jnp.concatenate([doubled(weight_ref[block, k]) for k in range(count)], axis=1)
        total = lax.dot_general(near, weight, TURNED, preferred_element_type=jnp.float32)
        running_ref[block] = turned[block].astype(jnp.float32) - total
        remote_doubled_ref[block] = jnp.concatenate(
            [doubled(remote_weight_ref[block, k]) for k in range(remote_weight_ref.shape[1])], axis=1
        )
        inverse_fourfold_ref[block] = doubled(doubled(inverse_ref[block]))
    observed = days_ref[0]
    shape = (days, LANES)
    first = lax.broadcasted_iota(jnp.int32, shape, 1) < size
    seen = lax.broadcasted_iota(jnp.int32, shape, 0) < observed
    for block in range(0, blocks, 2):
        factor = jnp.where(seen, retention_ref[:, pl.ds(block * size, LANES)], 1.0)
        other = pltpu.roll(factor, size, 1)
        retain_ref[pl.ds(block, days, stride=blocks), :] = jnp.where(first, factor, other)
        retain_ref[pl.ds(block + 1, days, stride=blocks), :] = jnp.where(first, other, factor)
    product = jnp.ones((blocks, LANES), jnp.float32)
    for day in range(days):
        product = product * retain_ref[pl.ds(day * blocks, blocks), :]
    high = product.astype(jnp.bfloat16).astype(jnp.float32)
    half = lax.broadcasted_iota(jnp.int32, product.shape, 1) < size
    product_ref[...] = jnp.where(half, high, product - high).astype(jnp.bfloat16)


def pass_kernel(piece_ref, product_ref, out_ref):
    out_ref[...] = piece_ref[...]


def forward_kernel(
    dims, pieces, links_ref, days_ref, running_ref, weight_ref, inverse_ref, retain_ref, product_ref, *rest
):
    days, blocks, size, probes = dims
    piece_refs = rest[: 2 * pieces]
    forcing_ref, message_ref, remote, source = rest[2 * pieces :]
    pairs = forcing_ref.shape[0]
    count = links_ref.shape[0]
    bound = piece_refs[0].shape[0]
    held = pieces * bound
    me = lax.axis_index("space")
    for k, ref in enumerate(piece_refs):
        remote[pl.ds(k * bound, bound)] = ref[...]
    seen = lax.broadcasted_iota(jnp.int32, (days, LANES), 0) < days_ref[0]
    for block in range(blocks):
        places = []
        for k in range(count):
            link = links_ref[k, block]
            distance = (link // bound) ^ me
            places.append((distance % 2) * held + (distance // 2) * bound + link % bound)
        far = jnp.concatenate([remote[place] for place in places], axis=1)
        total = lax.dot_general(far, weight_ref[block], TURNED, preferred_element_type=jnp.float32)
        source[block] = (running_ref[block] - total).astype(jnp.bfloat16)
    for block in range(blocks):
        drive = lax.dot_general(
            paired([source[block, pl.ds(pair * days, days), :] for pair in range(pairs)]),
            inverse_ref[block], TURNED, preferred_element_type=jnp.float32,
        )
        for pair, tile in enumerate(unpaired(drive, days)):
            forcing_ref[pair, pl.ds(block, days, stride=blocks), :] = jnp.where(seen, tile, 0.0)
    states = [jnp.zeros((blocks, LANES), jnp.float32)] * pairs
    for day in range(days):
        rows = pl.ds(day * blocks, blocks)
        factor = retain_ref[rows, :]
        for pair in range(pairs):
            states[pair] = factor * states[pair] + forcing_ref[pair, rows, :]
    leave(message_ref, states)
    message_ref[pairs] = product_ref[...]


def leave(message_ref, values):
    for pair, value in enumerate(values):
        message_ref[pair] = value.astype(jnp.bfloat16)


def collect(piece_refs, inbox):
    me = lax.axis_index("tm")
    for k, ref in enumerate(piece_refs):
        inbox[me ^ (k + 1)] = ref[...]


def carried(pairs, inbox, products, backward):
    me, count = lax.axis_index("tm"), inbox.shape[0]
    carries = [jnp.zeros(inbox.shape[2:], jnp.float32)] * pairs
    for slab in range(count - 1, 0, -1) if backward else range(count - 1):
        valid = slab > me if backward else slab < me
        terms = products[slab, pairs].astype(jnp.float32)
        factor = terms + pltpu.roll(terms, LANES // 2, 1)
        for pair in range(pairs):
            update = inbox[slab, pair].astype(jnp.float32) + factor * carries[pair]
            carries[pair] = jnp.where(valid, update, carries[pair])
    return carries


def states_kernel(dims, forcing_ref, retain_ref, states_ref, through_ref, stage, products):
    days, blocks, size, probes = dims
    pairs = forcing_ref.shape[0]
    states = [jnp.zeros((blocks, LANES), jnp.float32)] * pairs
    product = jnp.ones((blocks, LANES), jnp.float32)
    for day in range(days):
        rows = pl.ds(day * blocks, blocks)
        factor = retain_ref[rows, :]
        product = product * factor
        products[rows, :] = product
        for pair in range(pairs):
            states[pair] = factor * states[pair] + forcing_ref[pair, rows, :]
            stage[pair, rows, :] = states[pair]
    for block in range(blocks):
        through_ref[block] = products[pl.ds(block, days, stride=blocks), :]
        for pair in range(pairs):
            states_ref[block, pl.ds(pair * days, days), :] = stage[pair, pl.ds(block, days, stride=blocks), :]


def adjoint_kernel(dims, hops, days_ref, states_ref, through_ref, retain_ref, inverse_ref, *rest):
    days, blocks, size, probes = dims
    adjoint_ref, message_ref, inbox, enter = rest[hops:]
    pairs = adjoint_ref.shape[0]
    collect(rest[:hops], inbox)
    seen = lax.broadcasted_iota(jnp.int32, (days, LANES), 0) < days_ref[0]
    for pair, carry in enumerate(carried(pairs, inbox, inbox, False)):
        enter[pair] = carry
    for block in range(blocks):
        through = through_ref[block]
        stored = [
            (states_ref[block, pl.ds(pair * days, days), :] + through * enter[pair, pl.ds(block, 1), :])
            .astype(jnp.bfloat16)
            for pair in range(pairs)
        ]
        adjoint = jnp.dot(paired(stored), inverse_ref[block], preferred_element_type=jnp.float32)
        for pair, tile in enumerate(unpaired(adjoint, days)):
            adjoint_ref[pair, pl.ds(block, days, stride=blocks), :] = jnp.where(seen, tile, 0.0)
    carries = [jnp.zeros((blocks, LANES), jnp.float32)] * pairs
    for day in reversed(range(days)):
        rows = pl.ds(day * blocks, blocks)
        factor = retain_ref[rows, :]
        for pair in range(pairs):
            carries[pair] = factor * (adjoint_ref[pair, rows, :] + carries[pair])
    leave(message_ref, carries)


def own_kernel(dims, adjoint_ref, retain_ref, moved_ref, partial_ref):
    days, blocks, size, probes = dims
    pairs = adjoint_ref.shape[0]
    carries = [jnp.zeros((blocks, LANES), jnp.float32)] * pairs
    for day in reversed(range(days)):
        rows = pl.ds(day * blocks, blocks)
        factor = retain_ref[rows, :]
        total = None
        for pair in range(pairs):
            smoothed = adjoint_ref[pair, rows, :] + carries[pair]
            carries[pair] = factor * smoothed
            term = smoothed * moved_ref[pair, rows, :].astype(jnp.float32)
            total = term if total is None else total + term
        partial_ref[rows, :] = total


def variance_kernel(dims, hops, partial_ref, retain_ref, moved_ref, *rest):
    days, blocks, size, probes = dims
    pairs = moved_ref.shape[0]
    out_ref, stage, inbox, products = rest[2 * hops :]
    collect(rest[:hops], inbox)
    collect(rest[hops : 2 * hops], products)
    carries = carried(pairs, inbox, products, True)
    reach = jnp.ones((blocks, LANES), jnp.float32)
    for day in reversed(range(days)):
        rows = pl.ds(day * blocks, blocks)
        total = None
        for pair in range(pairs):
            term = carries[pair] * moved_ref[pair, rows, :].astype(jnp.float32)
            total = term if total is None else total + term
        stage[rows, :] = partial_ref[rows, :] + reach * total
        reach = reach * retain_ref[rows, :]
    lane = lax.broadcasted_iota(jnp.int32, (days, LANES), 1)
    for block in range(0, blocks, 2):
        both = [stage[pl.ds(block + half, days, stride=blocks), :] for half in range(2)]
        both = [value + pltpu.roll(value, size, 1) for value in both]
        out_ref[:, pl.ds(block * size, LANES)] = jnp.where(lane < size, both[0], both[1]) * (1.0 / probes)


def call(kernel, outs, scratch, flops, moved, scalars, *operands, apart=(), limit=VMEM_LIMIT):
    in_specs = [
        pl.BlockSpec(memory_space=pltpu.SMEM if i < scalars else pl.ANY if i in apart else pltpu.VMEM)
        for i in range(len(operands))
    ]
    return pl.pallas_call(
        kernel,
        out_shape=[jax.ShapeDtypeStruct(shape, kind) for shape, kind in outs],
        in_specs=in_specs,
        out_specs=[pl.BlockSpec(memory_space=pltpu.VMEM) for _ in outs],
        scratch_shapes=scratch,
        compiler_params=pltpu.CompilerParams(vmem_limit_bytes=limit),
        cost_estimate=pl.CostEstimate(flops=flops, bytes_accessed=moved, transcendentals=0),
    )(*operands)


def crossed(block, axis, bits):
    return lax.ppermute(block, axis, [(i, i ^ bits) for i in range(lax.axis_size(axis))])


def local(
    probes,
    local_links,
    remote_links,
    shared_blocks,
    slab_days,
    local_coupling,
    remote_coupling,
    block_inverse,
    retention,
):
    days, blocks, width = probes.shape
    size = block_inverse.shape[1]
    dims = (days, blocks, size, width // size)
    pairs = width // LANES
    f32, bf16 = jnp.float32, jnp.bfloat16
    bound = shared_blocks.shape[1]
    far = remote_links.shape[1]
    rows = days * blocks
    groups = lax.axis_size("space")
    held = groups // 2 * bound
    near_table, far_table = local_links.T, remote_links.T
    big = ((pairs, rows, LANES), f32)

    (outgoing,) = call(
        functools.partial(outgoing_kernel, dims),
        [((bound, pairs * days, LANES), bf16)],
        [], 10**9, 4 * 10**6, 1, shared_blocks, probes, limit=63 * 1024 * 1024,
    )
    pieces = {bits: crossed(outgoing, "space", bits) for bits in range(groups - 2, 0, -2)}
    running, moved, retain, product, remote_weight, inverse = call(
        functools.partial(local_kernel, dims),
        [
            ((blocks, pairs * days, LANES), f32),
            ((pairs, rows, LANES), bf16),
            ((rows, LANES), f32),
            ((blocks, LANES), bf16),
            ((blocks, LANES, far * LANES), bf16),
            ((blocks, 2 * LANES, 2 * LANES), bf16),
        ],
        [pltpu.VMEM(*big), pltpu.VMEM((blocks, pairs * days, LANES), bf16)],
        10**10, 10**7, 2,
        near_table, slab_days, probes, local_coupling, remote_coupling, block_inverse, retention,
    )
    same = [outgoing]
    for bits in range(2, groups, 2):
        same += call(pass_kernel, [(outgoing.shape, bf16)], [], 0, 10**5, 0, pieces[bits], product)
    other = [crossed(piece, "space", 1) for piece in same]
    slabs = lax.axis_size("tm")
    hops = slabs - 1
    exchange = lambda message: [crossed(message, "tm", bits) for bits in range(hops, 0, -1)][::-1]
    inbox = pltpu.VMEM((slabs, pairs + 1, blocks, LANES), bf16)
    forcing, message = call(
        functools.partial(forward_kernel, dims, len(same)),
        [big, ((pairs + 1, blocks, LANES), bf16)],
        [pltpu.VMEM((2 * held, pairs * days, LANES), bf16), pltpu.VMEM((blocks, pairs * days, LANES), bf16)],
        10**10, 10**7, 2,
        far_table, slab_days, running, remote_weight, inverse, retain, product, *same, *other,
    )
    ends = exchange(message)
    by_block = (blocks, pairs * days, LANES)
    states, through = call(
        functools.partial(states_kernel, dims),
        [(by_block, f32), ((blocks, days, LANES), f32)],
        [pltpu.VMEM(*big), pltpu.VMEM((rows, LANES), f32)], 10**9, 10**6, 0, forcing, retain,
    )
    adjoint, message = call(
        functools.partial(adjoint_kernel, dims, hops),
        [big, ((pairs, blocks, LANES), bf16)],
        [inbox, pltpu.VMEM((pairs, blocks, LANES), f32)], 10**10, 10**7, 1,
        slab_days, states, through, retain, inverse, *ends,
    )
    starts = exchange(message)
    (partial,) = call(
        functools.partial(own_kernel, dims), [((rows, LANES), f32)], [], 10**9, 10**6, 0, adjoint, retain, moved
    )
    (variance,) = call(
        functools.partial(variance_kernel, dims, hops),
        [((days, blocks * size), f32)],
        [pltpu.VMEM((rows, LANES), f32), pltpu.VMEM((slabs, pairs, blocks, LANES), bf16), inbox], 10**10, 10**7, 0,
        partial, retain, moved, *starts, *ends,
    )
    return variance


def solution(mesh):
    placed = (
        P("tm", "space", None),
        P("space", None),
        P("space", None),
        P("space", None),
        P("tm"),
        P("space", None, None, None),
        P("space", None, None, None),
        P("space", None, None),
        P("tm", "space"),
    )
    return jax.shard_map(
        local, mesh=mesh, in_specs=placed, out_specs=P("tm", "space"), check_vma=False
    )
```

```python
import functools

import jax
import jax.numpy as jnp
from jax import lax
from jax.experimental import pallas as pl
from jax.experimental.pallas import tpu as pltpu
from jax.sharding import PartitionSpec as P

LANES = 128
VMEM_LIMIT = 20 * 1024 * 1024
TURNED = (((1,), (1,)), ((), ()))


def permutation(size, probes, start, width):
    total = size * probes
    column = lax.broadcasted_iota(jnp.int32, (total, width), 1) + start
    origin = (column % size) * probes + column // size
    row = lax.broadcasted_iota(jnp.int32, (total, width), 0)
    return (row == origin).astype(jnp.float32).astype(jnp.bfloat16)


def doubled(weight):
    zero = jnp.zeros_like(weight)
    return jnp.concatenate(
        [jnp.concatenate([weight, zero], axis=1), jnp.concatenate([zero, weight], axis=1)], axis=0
    )


def outgoing_kernel(dims, shared_ref, z_ref, outgoing_ref):
    days, blocks, size, probes = dims
    count = outgoing_ref.shape[0]
    z = z_ref[...].reshape(days * blocks, size * probes)
    row = lax.broadcasted_iota(jnp.int32, (days, days * blocks), 0)
    column = lax.broadcasted_iota(jnp.int32, (days, days * blocks), 1)
    picks = [
        (column == row * blocks + shared_ref[0, m]).astype(jnp.float32).astype(jnp.bfloat16) for m in range(count)
    ]
    picked = jnp.dot(jnp.concatenate(picks, axis=0), z, preferred_element_type=jnp.float32)
    step = 2 * LANES
    shift = step // size
    ranges = size * probes // step
    shifted = [picked] + [pltpu.roll(picked, size * probes - i * shift, 1) for i in range(1, ranges)]
    shifted = jnp.concatenate(shifted, axis=0).astype(jnp.bfloat16)
    moved = jnp.dot(shifted, permutation(size, probes, 0, step), preferred_element_type=jnp.float32)
    moved = moved.astype(jnp.bfloat16)
    for pair in range(size * probes // LANES):
        for m in range(count):
            row, lane = (pair // 2 * count + m) * days, pair % 2 * LANES
            outgoing_ref[m, pl.ds(pair * days, days), :] = moved[row : row + days, lane : lane + LANES]


def turn_kernel(dims, z_ref, moved_ref, turned_ref, stage):
    days, blocks, size, probes = dims
    pairs = size * probes // LANES
    z = z_ref[...].reshape(days * blocks, size * probes)
    step = 2 * LANES
    for start in range(0, size * probes, step):
        moved = jnp.dot(z, permutation(size, probes, start, step), preferred_element_type=jnp.float32)
        for half in range(2):
            pair = start // LANES + half
            tile = moved[:, half * LANES : (half + 1) * LANES]
            stage[pair] = tile
            moved_ref[pair] = tile.astype(jnp.bfloat16)
    for block in range(blocks):
        for pair in range(pairs):
            rows = stage[pair, pl.ds(block, days, stride=blocks), :]
            turned_ref[block, pl.ds(pair * days, days), :] = rows.astype(jnp.bfloat16)


def local_kernel(
    dims, links_ref, days_ref, turned_ref, weight_ref, remote_weight_ref, inverse_ref, retention_ref,
    running_ref, retain_ref, product_ref, remote_doubled_ref, inverse_doubled_ref,
):
    days, blocks, size, probes = dims
    count = links_ref.shape[0]
    for block in range(blocks):
        near = jnp.concatenate([turned_ref[links_ref[k, block]] for k in range(count)], axis=1)
        weight = jnp.concatenate([doubled(weight_ref[block, k]) for k in range(count)], axis=1)
        total = lax.dot_general(near, weight, TURNED, preferred_element_type=jnp.float32)
        running_ref[block] = turned_ref[block].astype(jnp.float32) - total
        remote_doubled_ref[block] = jnp.concatenate(
            [doubled(remote_weight_ref[block, k]) for k in range(remote_weight_ref.shape[1])], axis=1
        )
        inverse_doubled_ref[block] = doubled(inverse_ref[block])
    observed = days_ref[0]
    shape = (days, LANES)
    first = lax.broadcasted_iota(jnp.int32, shape, 1) < size
    seen = lax.broadcasted_iota(jnp.int32, shape, 0) < observed
    for block in range(0, blocks, 2):
        factor = jnp.where(seen, retention_ref[:, pl.ds(block * size, LANES)], 1.0)
        other = pltpu.roll(factor, size, 1)
        retain_ref[pl.ds(block, days, stride=blocks), :] = jnp.where(first, factor, other)
        retain_ref[pl.ds(block + 1, days, stride=blocks), :] = jnp.where(first, other, factor)
    product = jnp.ones((blocks, LANES), jnp.float32)
    for day in range(days):
        product = product * retain_ref[pl.ds(day * blocks, blocks), :]
    high = product.astype(jnp.bfloat16).astype(jnp.float32)
    half = lax.broadcasted_iota(jnp.int32, product.shape, 1) < size
    product_ref[...] = jnp.where(half, high, product - high).astype(jnp.bfloat16)


def pass_kernel(piece_ref, product_ref, out_ref):
    out_ref[...] = piece_ref[...]


def forward_kernel(
    dims, pieces, links_ref, days_ref, running_ref, weight_ref, inverse_ref, retain_ref, product_ref, *rest
):
    days, blocks, size, probes = dims
    piece_refs = rest[: 2 * pieces]
    forcing_ref, message_ref, remote, source = rest[2 * pieces :]
    pairs = forcing_ref.shape[0]
    count = links_ref.shape[0]
    bound = piece_refs[0].shape[0]
    held = pieces * bound
    me = lax.axis_index("space")
    for k, ref in enumerate(piece_refs):
        chip = (pieces - k) % pieces
        remote[pl.ds(k // pieces * held + chip % pieces * bound, bound)] = ref[...]
    seen = lax.broadcasted_iota(jnp.int32, (days, LANES), 0) < days_ref[0]
    for block in range(blocks):
        places = []
        for k in range(count):
            link = links_ref[k, block]
            distance = (link // bound) ^ me
            places.append((distance % 2) * held + (distance // 2) * bound + link % bound)
        far = jnp.concatenate([remote[place] for place in places], axis=1)
        total = lax.dot_general(far, weight_ref[block], TURNED, preferred_element_type=jnp.float32)
        source[block] = (running_ref[block] - total).astype(jnp.bfloat16)
    for block in range(blocks):
        drive = lax.dot_general(source[block], inverse_ref[block], TURNED, preferred_element_type=jnp.float32)
        for pair in range(pairs):
            forcing_ref[pair, pl.ds(block, days, stride=blocks), :] = jnp.where(
                seen, drive[pair * days : (pair + 1) * days], 0.0
            )
    states = [jnp.zeros((blocks, LANES), jnp.float32)] * pairs
    for day in range(days):
        rows = pl.ds(day * blocks, blocks)
        factor = retain_ref[rows, :]
        for pair in range(pairs):
            states[pair] = factor * states[pair] + forcing_ref[pair, rows, :]
    leave(message_ref, states)
    message_ref[pairs] = product_ref[...]


def leave(message_ref, values):
    for pair, value in enumerate(values):
        message_ref[pair] = value.astype(jnp.bfloat16)


def collect(piece_refs, inbox):
    me = lax.axis_index("tm")
    for k, ref in enumerate(piece_refs):
        inbox[me ^ (k + 1)] = ref[...]


def carried(pairs, inbox, products, backward):
    me, count = lax.axis_index("tm"), inbox.shape[0]
    carries = [jnp.zeros(inbox.shape[2:], jnp.float32)] * pairs
    for slab in range(count - 1, 0, -1) if backward else range(count - 1):
        valid = slab > me if backward else slab < me
        terms = products[slab, pairs].astype(jnp.float32)
        factor = terms + pltpu.roll(terms, LANES // 2, 1)
        for pair in range(pairs):
            update = inbox[slab, pair].astype(jnp.float32) + factor * carries[pair]
            carries[pair] = jnp.where(valid, update, carries[pair])
    return carries


def states_kernel(dims, forcing_ref, retain_ref, states_ref, through_ref, stage, products):
    days, blocks, size, probes = dims
    pairs = forcing_ref.shape[0]
    states = [jnp.zeros((blocks, LANES), jnp.float32)] * pairs
    product = jnp.ones((blocks, LANES), jnp.float32)
    for day in range(days):
        rows = pl.ds(day * blocks, blocks)
        factor = retain_ref[rows, :]
        product = product * factor
        products[rows, :] = product
        for pair in range(pairs):
            states[pair] = factor * states[pair] + forcing_ref[pair, rows, :]
            stage[pair, rows, :] = states[pair]
    for block in range(blocks):
        through_ref[block] = products[pl.ds(block, days, stride=blocks), :]
        for pair in range(pairs):
            states_ref[block, pl.ds(pair * days, days), :] = stage[pair, pl.ds(block, days, stride=blocks), :]


def adjoint_kernel(dims, hops, days_ref, states_ref, through_ref, retain_ref, inverse_ref, *rest):
    days, blocks, size, probes = dims
    adjoint_ref, message_ref, inbox, enter = rest[hops:]
    pairs = adjoint_ref.shape[0]
    collect(rest[:hops], inbox)
    seen = lax.broadcasted_iota(jnp.int32, (days, LANES), 0) < days_ref[0]
    for pair, carry in enumerate(carried(pairs, inbox, inbox, False)):
        enter[pair] = carry
    for block in range(blocks):
        through = through_ref[block]
        stored = [
            (states_ref[block, pl.ds(pair * days, days), :] + through * enter[pair, pl.ds(block, 1), :])
            .astype(jnp.bfloat16)
            for pair in range(pairs)
        ]
        adjoint = jnp.dot(jnp.concatenate(stored, axis=0), inverse_ref[block], preferred_element_type=jnp.float32)
        for pair in range(pairs):
            adjoint_ref[pair, pl.ds(block, days, stride=blocks), :] = jnp.where(
                seen, adjoint[pair * days : (pair + 1) * days], 0.0
            )
    carries = [jnp.zeros((blocks, LANES), jnp.float32)] * pairs
    for day in reversed(range(days)):
        rows = pl.ds(day * blocks, blocks)
        factor = retain_ref[rows, :]
        for pair in range(pairs):
            carries[pair] = factor * (adjoint_ref[pair, rows, :] + carries[pair])
    leave(message_ref, carries)


def own_kernel(dims, adjoint_ref, retain_ref, moved_ref, partial_ref):
    days, blocks, size, probes = dims
    pairs = adjoint_ref.shape[0]
    carries = [jnp.zeros((blocks, LANES), jnp.float32)] * pairs
    for day in reversed(range(days)):
        rows = pl.ds(day * blocks, blocks)
        factor = retain_ref[rows, :]
        total = None
        for pair in range(pairs):
            smoothed = adjoint_ref[pair, rows, :] + carries[pair]
            carries[pair] = factor * smoothed
            term = smoothed * moved_ref[pair, rows, :].astype(jnp.float32)
            total = term if total is None else total + term
        partial_ref[rows, :] = total


def variance_kernel(dims, hops, partial_ref, retain_ref, moved_ref, *rest):
    days, blocks, size, probes = dims
    pairs = moved_ref.shape[0]
    out_ref, stage, inbox, products = rest[2 * hops :]
    collect(rest[:hops], inbox)
    collect(rest[hops : 2 * hops], products)
    carries = carried(pairs, inbox, products, True)
    reach = jnp.ones((blocks, LANES), jnp.float32)
    for day in reversed(range(days)):
        rows = pl.ds(day * blocks, blocks)
        total = None
        for pair in range(pairs):
            term = carries[pair] * moved_ref[pair, rows, :].astype(jnp.float32)
            total = term if total is None else total + term
        stage[rows, :] = partial_ref[rows, :] + reach * total
        reach = reach * retain_ref[rows, :]
    lane = lax.broadcasted_iota(jnp.int32, (days, LANES), 1)
    for block in range(0, blocks, 2):
        both = [stage[pl.ds(block + half, days, stride=blocks), :] for half in range(2)]
        both = [value + pltpu.roll(value, size, 1) for value in both]
        out_ref[:, pl.ds(block * size, LANES)] = jnp.where(lane < size, both[0], both[1]) * (1.0 / probes)


def call(kernel, outs, scratch, flops, moved, scalars, *operands, apart=(), limit=VMEM_LIMIT):
    in_specs = [
        pl.BlockSpec(memory_space=pltpu.SMEM if i < scalars else pl.ANY if i in apart else pltpu.VMEM)
        for i in range(len(operands))
    ]
    return pl.pallas_call(
        kernel,
        out_shape=[jax.ShapeDtypeStruct(shape, kind) for shape, kind in outs],
        in_specs=in_specs,
        out_specs=[pl.BlockSpec(memory_space=pltpu.VMEM) for _ in outs],
        scratch_shapes=scratch,
        compiler_params=pltpu.CompilerParams(vmem_limit_bytes=limit),
        cost_estimate=pl.CostEstimate(flops=flops, bytes_accessed=moved, transcendentals=0),
    )(*operands)


def crossed(block, axis, bits):
    return lax.ppermute(block, axis, [(i, i ^ bits) for i in range(lax.axis_size(axis))])


def local(
    probes,
    local_links,
    remote_links,
    shared_blocks,
    slab_days,
    local_coupling,
    remote_coupling,
    block_inverse,
    retention,
):
    days, blocks, width = probes.shape
    size = block_inverse.shape[1]
    dims = (days, blocks, size, width // size)
    pairs = width // LANES
    f32, bf16 = jnp.float32, jnp.bfloat16
    bound = shared_blocks.shape[1]
    far = remote_links.shape[1]
    rows = days * blocks
    groups = lax.axis_size("space")
    held = groups // 2 * bound
    near_table, far_table = local_links.T, remote_links.T
    big = ((pairs, rows, LANES), f32)

    (outgoing,) = call(
        functools.partial(outgoing_kernel, dims),
        [((bound, pairs * days, LANES), bf16)],
        [], 10**9, 4 * 10**6, 1, shared_blocks, probes, limit=63 * 1024 * 1024,
    )
    pieces = {bits: crossed(outgoing, "space", bits) for bits in range(groups - 2, 0, -2)}
    by_block = (blocks, pairs * days, LANES)
    moved, turned = call(
        functools.partial(turn_kernel, dims),
        [((pairs, rows, LANES), bf16), (by_block, bf16)],
        [pltpu.VMEM(*big)], 10**10, 10**7, 0, probes,
    )
    running, retain, product, remote_weight, inverse = call(
        functools.partial(local_kernel, dims),
        [
            (by_block, f32),
            ((rows, LANES), f32),
            ((blocks, LANES), bf16),
            ((blocks, LANES, far * LANES), bf16),
            ((blocks, LANES, LANES), bf16),
        ],
        [], 10**10, 10**7, 2,
        near_table, slab_days, turned, local_coupling, remote_coupling, block_inverse, retention,
    )
    same, other = {0: outgoing}, {0: crossed(outgoing, "space", 1)}
    for bits in range(groups - 2, 0, -2):
        (same[bits],) = call(pass_kernel, [(outgoing.shape, bf16)], [], 0, 10**5, 0, pieces[bits], product)
        other[bits] = crossed(same[bits], "space", 1)
    same, other = list(same.values()), list(other.values())
    slabs = lax.axis_size("tm")
    hops = slabs - 1
    exchange = lambda message: [crossed(message, "tm", bits) for bits in range(hops, 0, -1)][::-1]
    inbox = pltpu.VMEM((slabs, pairs + 1, blocks, LANES), bf16)
    forcing, message = call(
        functools.partial(forward_kernel, dims, len(same)),
        [big, ((pairs + 1, blocks, LANES), bf16)],
        [pltpu.VMEM((2 * held, pairs * days, LANES), bf16), pltpu.VMEM((blocks, pairs * days, LANES), bf16)],
        10**10, 10**7, 2,
        far_table, slab_days, running, remote_weight, inverse, retain, product, *same, *other,
    )
    ends = exchange(message)
    states, through = call(
        functools.partial(states_kernel, dims),
        [(by_block, f32), ((blocks, days, LANES), f32)],
        [pltpu.VMEM(*big), pltpu.VMEM((rows, LANES), f32)], 10**9, 10**6, 0, forcing, retain,
    )
    adjoint, message = call(
        functools.partial(adjoint_kernel, dims, hops),
        [big, ((pairs, blocks, LANES), bf16)],
        [inbox, pltpu.VMEM((pairs, blocks, LANES), f32)], 10**10, 10**7, 1,
        slab_days, states, through, retain, inverse, *ends,
    )
    starts = exchange(message)
    (partial,) = call(
        functools.partial(own_kernel, dims), [((rows, LANES), f32)], [], 10**9, 10**6, 0, adjoint, retain, moved
    )
    (variance,) = call(
        functools.partial(variance_kernel, dims, hops),
        [((days, blocks * size), f32)],
        [pltpu.VMEM((rows, LANES), f32), pltpu.VMEM((slabs, pairs, blocks, LANES), bf16), inbox], 10**10, 10**7, 0,
        partial, retain, moved, *starts, *ends,
    )
    return variance


def solution(mesh):
    placed = (
        P("tm", "space", None),
        P("space", None),
        P("space", None),
        P("space", None),
        P("tm"),
        P("space", None, None, None),
        P("space", None, None, None),
        P("space", None, None),
        P("tm", "space"),
    )
    return jax.shard_map(
        local, mesh=mesh, in_specs=placed, out_specs=P("tm", "space"), check_vma=False
    )
```

```python
import functools

import jax
import jax.numpy as jnp
from jax import lax
from jax.experimental import pallas as pl
from jax.experimental.pallas import tpu as pltpu
from jax.sharding import PartitionSpec as P

LANES = 128
VMEM_LIMIT = 20 * 1024 * 1024
TURNED = (((1,), (1,)), ((), ()))


def permutation(size, probes, start, width):
    total = size * probes
    column = lax.broadcasted_iota(jnp.int32, (total, width), 1) + start
    origin = (column % size) * probes + column // size
    row = lax.broadcasted_iota(jnp.int32, (total, width), 0)
    return (row == origin).astype(jnp.float32).astype(jnp.bfloat16)


def doubled(weight):
    zero = jnp.zeros_like(weight)
    return jnp.concatenate(
        [jnp.concatenate([weight, zero], axis=1), jnp.concatenate([zero, weight], axis=1)], axis=0
    )


def outgoing_kernel(dims, shared_ref, z_ref, outgoing_ref):
    days, blocks, size, probes = dims
    count = outgoing_ref.shape[0]
    z = z_ref[...].reshape(days * blocks, size * probes)
    row = lax.broadcasted_iota(jnp.int32, (days, days * blocks), 0)
    column = lax.broadcasted_iota(jnp.int32, (days, days * blocks), 1)
    picks = [
        (column == row * blocks + shared_ref[0, m]).astype(jnp.float32).astype(jnp.bfloat16) for m in range(count)
    ]
    picked = jnp.dot(jnp.concatenate(picks, axis=0), z, preferred_element_type=jnp.float32)
    step = 2 * LANES
    shift = step // size
    ranges = size * probes // step
    shifted = [picked] + [pltpu.roll(picked, size * probes - i * shift, 1) for i in range(1, ranges)]
    shifted = jnp.concatenate(shifted, axis=0).astype(jnp.bfloat16)
    moved = jnp.dot(shifted, permutation(size, probes, 0, step), preferred_element_type=jnp.float32)
    moved = moved.astype(jnp.bfloat16)
    for pair in range(size * probes // LANES):
        for m in range(count):
            row, lane = (pair // 2 * count + m) * days, pair % 2 * LANES
            outgoing_ref[m, pl.ds(pair * days, days), :] = moved[row : row + days, lane : lane + LANES]


def turn_kernel(dims, z_ref, moved_ref, turned_ref, stage):
    days, blocks, size, probes = dims
    pairs = size * probes // LANES
    z = z_ref[...].reshape(days * blocks, size * probes)
    step = 2 * LANES
    for start in range(0, size * probes, step):
        moved = jnp.dot(z, permutation(size, probes, start, step), preferred_element_type=jnp.float32)
        for half in range(2):
            pair = start // LANES + half
            tile = moved[:, half * LANES : (half + 1) * LANES]
            stage[pair] = tile
            moved_ref[pair] = tile.astype(jnp.bfloat16)
    for block in range(blocks):
        for pair in range(pairs):
            rows = stage[pair, pl.ds(block, days, stride=blocks), :]
            turned_ref[block, pl.ds(pair * days, days), :] = rows.astype(jnp.bfloat16)


def local_kernel(
    dims, links_ref, days_ref, turned_ref, weight_ref, remote_weight_ref, inverse_ref, retention_ref,
    running_ref, retain_ref, product_ref, remote_doubled_ref, inverse_doubled_ref,
):
    days, blocks, size, probes = dims
    count = links_ref.shape[0]
    for block in range(blocks):
        near = jnp.concatenate([turned_ref[links_ref[k, block]] for k in range(count)], axis=1)
        weight = jnp.concatenate([doubled(weight_ref[block, k]) for k in range(count)], axis=1)
        total = lax.dot_general(near, weight, TURNED, preferred_element_type=jnp.float32)
        running_ref[block] = turned_ref[block].astype(jnp.float32) - total
        remote_doubled_ref[block] = jnp.concatenate(
            [doubled(remote_weight_ref[block, k]) for k in range(remote_weight_ref.shape[1])], axis=1
        )
        inverse_doubled_ref[block] = doubled(inverse_ref[block])
    observed = days_ref[0]
    shape = (days, LANES)
    first = lax.broadcasted_iota(jnp.int32, shape, 1) < size
    seen = lax.broadcasted_iota(jnp.int32, shape, 0) < observed
    for block in range(0, blocks, 2):
        factor = jnp.where(seen, retention_ref[:, pl.ds(block * size, LANES)], 1.0)
        other = pltpu.roll(factor, size, 1)
        retain_ref[pl.ds(block, days, stride=blocks), :] = jnp.where(first, factor, other)
        retain_ref[pl.ds(block + 1, days, stride=blocks), :] = jnp.where(first, other, factor)
    product = jnp.ones((blocks, LANES), jnp.float32)
    for day in range(days):
        product = product * retain_ref[pl.ds(day * blocks, blocks), :]
    high = product.astype(jnp.bfloat16).astype(jnp.float32)
    half = lax.broadcasted_iota(jnp.int32, product.shape, 1) < size
    product_ref[...] = jnp.where(half, high, product - high).astype(jnp.bfloat16)


def pass_kernel(piece_ref, product_ref, out_ref):
    out_ref[...] = piece_ref[...]


def forward_kernel(
    dims, pieces, links_ref, days_ref, running_ref, weight_ref, inverse_ref, retain_ref, product_ref, *rest
):
    days, blocks, size, probes = dims
    piece_refs = rest[pieces - 1 : 3 * pieces - 1]
    forcing_ref, message_ref, remote, source = rest[3 * pieces - 1 :]
    pairs = forcing_ref.shape[0]
    count = links_ref.shape[0]
    bound = piece_refs[0].shape[0]
    held = pieces * bound
    me = lax.axis_index("space")
    for k, ref in enumerate(piece_refs):
        chip = (pieces - k) % pieces
        remote[pl.ds(k // pieces * held + chip % pieces * bound, bound)] = ref[...]
    seen = lax.broadcasted_iota(jnp.int32, (days, LANES), 0) < days_ref[0]
    for block in range(blocks):
        places = []
        for k in range(count):
            link = links_ref[k, block]
            distance = (link // bound) ^ me
            places.append((distance % 2) * held + (distance // 2) * bound + link % bound)
        far = jnp.concatenate([remote[place] for place in places], axis=1)
        total = lax.dot_general(far, weight_ref[block], TURNED, preferred_element_type=jnp.float32)
        source[block] = (running_ref[block] - total).astype(jnp.bfloat16)
    for block in range(blocks):
        drive = lax.dot_general(source[block], inverse_ref[block], TURNED, preferred_element_type=jnp.float32)
        for pair in range(pairs):
            forcing_ref[pair, pl.ds(block, days, stride=blocks), :] = jnp.where(
                seen, drive[pair * days : (pair + 1) * days], 0.0
            )
    states = [jnp.zeros((blocks, LANES), jnp.float32)] * pairs
    for day in range(days):
        rows = pl.ds(day * blocks, blocks)
        factor = retain_ref[rows, :]
        for pair in range(pairs):
            states[pair] = factor * states[pair] + forcing_ref[pair, rows, :]
    leave(message_ref, states)
    message_ref[pairs] = product_ref[...]


def leave(message_ref, values):
    for pair, value in enumerate(values):
        message_ref[pair] = value.astype(jnp.bfloat16)


def collect(piece_refs, inbox):
    me = lax.axis_index("tm")
    for k, ref in enumerate(piece_refs):
        inbox[me ^ (k + 1)] = ref[...]


def carried(pairs, inbox, products, backward):
    me, count = lax.axis_index("tm"), inbox.shape[0]
    carries = [jnp.zeros(inbox.shape[2:], jnp.float32)] * pairs
    for slab in range(count - 1, 0, -1) if backward else range(count - 1):
        valid = slab > me if backward else slab < me
        terms = products[slab, pairs].astype(jnp.float32)
        factor = terms + pltpu.roll(terms, LANES // 2, 1)
        for pair in range(pairs):
            update = inbox[slab, pair].astype(jnp.float32) + factor * carries[pair]
            carries[pair] = jnp.where(valid, update, carries[pair])
    return carries


def states_kernel(dims, forcing_ref, retain_ref, states_ref, through_ref, stage, products):
    days, blocks, size, probes = dims
    pairs = forcing_ref.shape[0]
    states = [jnp.zeros((blocks, LANES), jnp.float32)] * pairs
    product = jnp.ones((blocks, LANES), jnp.float32)
    for day in range(days):
        rows = pl.ds(day * blocks, blocks)
        factor = retain_ref[rows, :]
        product = product * factor
        products[rows, :] = product
        for pair in range(pairs):
            states[pair] = factor * states[pair] + forcing_ref[pair, rows, :]
            stage[pair, rows, :] = states[pair]
    for block in range(blocks):
        through_ref[block] = products[pl.ds(block, days, stride=blocks), :]
        for pair in range(pairs):
            states_ref[block, pl.ds(pair * days, days), :] = stage[pair, pl.ds(block, days, stride=blocks), :]


def adjoint_kernel(dims, hops, days_ref, states_ref, through_ref, retain_ref, inverse_ref, *rest):
    days, blocks, size, probes = dims
    adjoint_ref, message_ref, inbox, enter = rest[hops:]
    pairs = adjoint_ref.shape[0]
    collect(rest[:hops], inbox)
    seen = lax.broadcasted_iota(jnp.int32, (days, LANES), 0) < days_ref[0]
    for pair, carry in enumerate(carried(pairs, inbox, inbox, False)):
        enter[pair] = carry
    for block in range(blocks):
        through = through_ref[block]
        stored = [
            (states_ref[block, pl.ds(pair * days, days), :] + through * enter[pair, pl.ds(block, 1), :])
            .astype(jnp.bfloat16)
            for pair in range(pairs)
        ]
        adjoint = jnp.dot(jnp.concatenate(stored, axis=0), inverse_ref[block], preferred_element_type=jnp.float32)
        for pair in range(pairs):
            adjoint_ref[pair, pl.ds(block, days, stride=blocks), :] = jnp.where(
                seen, adjoint[pair * days : (pair + 1) * days], 0.0
            )
    carries = [jnp.zeros((blocks, LANES), jnp.float32)] * pairs
    for day in reversed(range(days)):
        rows = pl.ds(day * blocks, blocks)
        factor = retain_ref[rows, :]
        for pair in range(pairs):
            carries[pair] = factor * (adjoint_ref[pair, rows, :] + carries[pair])
    leave(message_ref, carries)


def own_kernel(dims, adjoint_ref, retain_ref, moved_ref, partial_ref):
    days, blocks, size, probes = dims
    pairs = adjoint_ref.shape[0]
    carries = [jnp.zeros((blocks, LANES), jnp.float32)] * pairs
    for day in reversed(range(days)):
        rows = pl.ds(day * blocks, blocks)
        factor = retain_ref[rows, :]
        total = None
        for pair in range(pairs):
            smoothed = adjoint_ref[pair, rows, :] + carries[pair]
            carries[pair] = factor * smoothed
            term = smoothed * moved_ref[pair, rows, :].astype(jnp.float32)
            total = term if total is None else total + term
        partial_ref[rows, :] = total


def variance_kernel(dims, hops, partial_ref, retain_ref, moved_ref, *rest):
    days, blocks, size, probes = dims
    pairs = moved_ref.shape[0]
    out_ref, stage, inbox, products = rest[2 * hops :]
    collect(rest[:hops], inbox)
    collect(rest[hops : 2 * hops], products)
    carries = carried(pairs, inbox, products, True)
    reach = jnp.ones((blocks, LANES), jnp.float32)
    for day in reversed(range(days)):
        rows = pl.ds(day * blocks, blocks)
        total = None
        for pair in range(pairs):
            term = carries[pair] * moved_ref[pair, rows, :].astype(jnp.float32)
            total = term if total is None else total + term
        stage[rows, :] = partial_ref[rows, :] + reach * total
        reach = reach * retain_ref[rows, :]
    lane = lax.broadcasted_iota(jnp.int32, (days, LANES), 1)
    for block in range(0, blocks, 2):
        both = [stage[pl.ds(block + half, days, stride=blocks), :] for half in range(2)]
        both = [value + pltpu.roll(value, size, 1) for value in both]
        out_ref[:, pl.ds(block * size, LANES)] = jnp.where(lane < size, both[0], both[1]) * (1.0 / probes)


def call(kernel, outs, scratch, flops, moved, scalars, *operands, apart=(), limit=VMEM_LIMIT):
    in_specs = [
        pl.BlockSpec(memory_space=pltpu.SMEM if i < scalars else pl.ANY if i in apart else pltpu.VMEM)
        for i in range(len(operands))
    ]
    return pl.pallas_call(
        kernel,
        out_shape=[jax.ShapeDtypeStruct(shape, kind) for shape, kind in outs],
        in_specs=in_specs,
        out_specs=[pl.BlockSpec(memory_space=pltpu.VMEM) for _ in outs],
        scratch_shapes=scratch,
        compiler_params=pltpu.CompilerParams(vmem_limit_bytes=limit),
        cost_estimate=pl.CostEstimate(flops=flops, bytes_accessed=moved, transcendentals=0),
    )(*operands)


def crossed(block, axis, bits):
    return lax.ppermute(block, axis, [(i, i ^ bits) for i in range(lax.axis_size(axis))])


def local(
    probes,
    local_links,
    remote_links,
    shared_blocks,
    slab_days,
    local_coupling,
    remote_coupling,
    block_inverse,
    retention,
):
    days, blocks, width = probes.shape
    size = block_inverse.shape[1]
    dims = (days, blocks, size, width // size)
    pairs = width // LANES
    f32, bf16 = jnp.float32, jnp.bfloat16
    bound = shared_blocks.shape[1]
    far = remote_links.shape[1]
    rows = days * blocks
    groups = lax.axis_size("space")
    held = groups // 2 * bound
    near_table, far_table = local_links.T, remote_links.T
    big = ((pairs, rows, LANES), f32)

    (outgoing,) = call(
        functools.partial(outgoing_kernel, dims),
        [((bound, pairs * days, LANES), bf16)],
        [], 10**9, 4 * 10**6, 1, shared_blocks, probes, limit=63 * 1024 * 1024,
    )
    pieces = {bits: crossed(outgoing, "space", bits) for bits in range(groups - 2, 0, -2)}
    by_block = (blocks, pairs * days, LANES)
    moved, turned = call(
        functools.partial(turn_kernel, dims),
        [((pairs, rows, LANES), bf16), (by_block, bf16)],
        [pltpu.VMEM(*big)], 10**10, 10**7, 0, probes,
    )
    running, retain, product, remote_weight, inverse = call(
        functools.partial(local_kernel, dims),
        [
            (by_block, f32),
            ((rows, LANES), f32),
            ((blocks, LANES), bf16),
            ((blocks, LANES, far * LANES), bf16),
            ((blocks, LANES, LANES), bf16),
        ],
        [], 10**10, 10**7, 2,
        near_table, slab_days, turned, local_coupling, remote_coupling, block_inverse, retention,
    )
    same, other = {0: outgoing}, {0: crossed(outgoing, "space", 1)}
    for bits in range(groups - 2, 0, -2):
        (same[bits],) = call(pass_kernel, [(outgoing.shape, bf16)], [], 0, 10**5, 0, pieces[bits], product)
        other[bits] = crossed(same[bits], "space", 1)
    same, other = list(same.values()), list(other.values())
    raw = [pieces[bits] for bits in range(2, groups, 2)]
    slabs = lax.axis_size("tm")
    hops = slabs - 1
    exchange = lambda message: [crossed(message, "tm", bits) for bits in range(hops, 0, -1)][::-1]
    inbox = pltpu.VMEM((slabs, pairs + 1, blocks, LANES), bf16)
    forcing, message = call(
        functools.partial(forward_kernel, dims, len(same)),
        [big, ((pairs + 1, blocks, LANES), bf16)],
        [pltpu.VMEM((2 * held, pairs * days, LANES), bf16), pltpu.VMEM((blocks, pairs * days, LANES), bf16)],
        10**10, 10**7, 2,
        far_table, slab_days, running, remote_weight, inverse, retain, product, *raw, *same, *other,
        apart=range(7, 7 + len(raw)),
    )
    ends = exchange(message)
    states, through = call(
        functools.partial(states_kernel, dims),
        [(by_block, f32), ((blocks, days, LANES), f32)],
        [pltpu.VMEM(*big), pltpu.VMEM((rows, LANES), f32)], 10**9, 10**6, 0, forcing, retain,
    )
    adjoint, message = call(
        functools.partial(adjoint_kernel, dims, hops),
        [big, ((pairs, blocks, LANES), bf16)],
        [inbox, pltpu.VMEM((pairs, blocks, LANES), f32)], 10**10, 10**7, 1,
        slab_days, states, through, retain, inverse, *ends,
    )
    starts = exchange(message)
    (partial,) = call(
        functools.partial(own_kernel, dims), [((rows, LANES), f32)], [], 10**9, 10**6, 0, adjoint, retain, moved
    )
    (variance,) = call(
        functools.partial(variance_kernel, dims, hops),
        [((days, blocks * size), f32)],
        [pltpu.VMEM((rows, LANES), f32), pltpu.VMEM((slabs, pairs, blocks, LANES), bf16), inbox], 10**10, 10**7, 0,
        partial, retain, moved, *starts, *ends,
    )
    return variance


def solution(mesh):
    placed = (
        P("tm", "space", None),
        P("space", None),
        P("space", None),
        P("space", None),
        P("tm"),
        P("space", None, None, None),
        P("space", None, None, None),
        P("space", None, None),
        P("tm", "space"),
    )
    return jax.shard_map(
        local, mesh=mesh, in_specs=placed, out_specs=P("tm", "space"), check_vma=False
    )
```

```python
import functools

import jax
import jax.numpy as jnp
from jax import lax
from jax.experimental import pallas as pl
from jax.experimental.pallas import tpu as pltpu
from jax.sharding import PartitionSpec as P

LANES = 128
VMEM_LIMIT = 20 * 1024 * 1024
TURNED = (((1,), (1,)), ((), ()))


def permutation(size, probes, start, width):
    total = size * probes
    column = lax.broadcasted_iota(jnp.int32, (total, width), 1) + start
    origin = (column % size) * probes + column // size
    row = lax.broadcasted_iota(jnp.int32, (total, width), 0)
    return (row == origin).astype(jnp.float32).astype(jnp.bfloat16)


def doubled(weight):
    zero = jnp.zeros_like(weight)
    return jnp.concatenate(
        [jnp.concatenate([weight, zero], axis=1), jnp.concatenate([zero, weight], axis=1)], axis=0
    )


def outgoing_kernel(dims, shared_hbm, z_hbm, outgoing_ref, shared_ref, z_ref, listed, arrived):
    days, blocks, size, probes = dims
    count = outgoing_ref.shape[0]
    parts = arrived.shape[0]
    part = days // parts
    copies = [
        pltpu.make_async_copy(z_hbm.at[pl.ds(i * part, part)], z_ref.at[pl.ds(i * part, part)], arrived.at[i])
        for i in range(parts)
    ]
    listing = pltpu.make_async_copy(shared_hbm, shared_ref, listed)
    listing.start()
    for copy in copies:
        copy.start()
    row = lax.broadcasted_iota(jnp.int32, (part, part * blocks), 0)
    column = lax.broadcasted_iota(jnp.int32, (part, part * blocks), 1)
    move = permutation(size, probes, 0, 2 * LANES)
    listing.wait()
    picks = [(column == row * blocks + shared_ref[0, m]).astype(jnp.float32) for m in range(count)]
    picks = jnp.concatenate(picks, axis=0).astype(jnp.bfloat16)
    picked = []
    for i, copy in enumerate(copies):
        copy.wait()
        z = z_ref[pl.ds(i * part, part)].reshape(part * blocks, size * probes)
        picked.append(jnp.dot(picks, z, preferred_element_type=jnp.float32))
    picked = jnp.concatenate([rows[m * part : (m + 1) * part] for m in range(count) for rows in picked], axis=0)
    step = 2 * LANES
    shift = step // size
    ranges = size * probes // step
    shifted = [picked] + [pltpu.roll(picked, size * probes - i * shift, 1) for i in range(1, ranges)]
    shifted = jnp.concatenate(shifted, axis=0).astype(jnp.bfloat16)
    moved = jnp.dot(shifted, move, preferred_element_type=jnp.float32)
    moved = moved.astype(jnp.bfloat16)
    for pair in range(size * probes // LANES):
        for m in range(count):
            row, lane = (pair // 2 * count + m) * days, pair % 2 * LANES
            outgoing_ref[m, pl.ds(pair * days, days), :] = moved[row : row + days, lane : lane + LANES]


def turn_kernel(dims, z_ref, moved_ref, turned_ref, stage):
    days, blocks, size, probes = dims
    pairs = size * probes // LANES
    z = z_ref[...].reshape(days * blocks, size * probes)
    step = 2 * LANES
    for start in range(0, size * probes, step):
        moved = jnp.dot(z, permutation(size, probes, start, step), preferred_element_type=jnp.float32)
        for half in range(2):
            pair = start // LANES + half
            tile = moved[:, half * LANES : (half + 1) * LANES]
            stage[pair] = tile
            moved_ref[pair] = tile.astype(jnp.bfloat16)
    for block in range(blocks):
        for pair in range(pairs):
            rows = stage[pair, pl.ds(block, days, stride=blocks), :]
            turned_ref[block, pl.ds(pair * days, days), :] = rows.astype(jnp.bfloat16)


def local_kernel(
    dims, links_ref, days_ref, turned_ref, weight_ref, remote_weight_ref, inverse_ref, retention_ref,
    running_ref, retain_ref, product_ref, remote_doubled_ref, inverse_doubled_ref,
):
    days, blocks, size, probes = dims
    count = links_ref.shape[0]
    for block in range(blocks):
        near = jnp.concatenate([turned_ref[links_ref[k, block]] for k in range(count)], axis=1)
        weight = jnp.concatenate([doubled(weight_ref[block, k]) for k in range(count)], axis=1)
        total = lax.dot_general(near, weight, TURNED, preferred_element_type=jnp.float32)
        running_ref[block] = turned_ref[block].astype(jnp.float32) - total
        remote_doubled_ref[block] = jnp.concatenate(
            [doubled(remote_weight_ref[block, k]) for k in range(remote_weight_ref.shape[1])], axis=1
        )
        inverse_doubled_ref[block] = doubled(inverse_ref[block])
    observed = days_ref[0]
    shape = (days, LANES)
    first = lax.broadcasted_iota(jnp.int32, shape, 1) < size
    seen = lax.broadcasted_iota(jnp.int32, shape, 0) < observed
    for block in range(0, blocks, 2):
        factor = jnp.where(seen, retention_ref[:, pl.ds(block * size, LANES)], 1.0)
        other = pltpu.roll(factor, size, 1)
        retain_ref[pl.ds(block, days, stride=blocks), :] = jnp.where(first, factor, other)
        retain_ref[pl.ds(block + 1, days, stride=blocks), :] = jnp.where(first, other, factor)
    product = jnp.ones((blocks, LANES), jnp.float32)
    for day in range(days):
        product = product * retain_ref[pl.ds(day * blocks, blocks), :]
    high = product.astype(jnp.bfloat16).astype(jnp.float32)
    half = lax.broadcasted_iota(jnp.int32, product.shape, 1) < size
    product_ref[...] = jnp.where(half, high, product - high).astype(jnp.bfloat16)


def pass_kernel(piece_ref, product_ref, out_ref):
    out_ref[...] = piece_ref[...]


def forward_kernel(
    dims, pieces, links_ref, days_ref, running_ref, weight_ref, inverse_ref, retain_ref, product_ref, *rest
):
    days, blocks, size, probes = dims
    piece_refs = rest[pieces - 1 : 3 * pieces - 1]
    forcing_ref, message_ref, remote, source = rest[3 * pieces - 1 :]
    pairs = forcing_ref.shape[0]
    count = links_ref.shape[0]
    bound = piece_refs[0].shape[0]
    held = pieces * bound
    me = lax.axis_index("space")
    for k, ref in enumerate(piece_refs):
        chip = (pieces - k) % pieces
        remote[pl.ds(k // pieces * held + chip % pieces * bound, bound)] = ref[...]
    seen = lax.broadcasted_iota(jnp.int32, (days, LANES), 0) < days_ref[0]
    for block in range(blocks):
        places = []
        for k in range(count):
            link = links_ref[k, block]
            distance = (link // bound) ^ me
            places.append((distance % 2) * held + (distance // 2) * bound + link % bound)
        far = jnp.concatenate([remote[place] for place in places], axis=1)
        total = lax.dot_general(far, weight_ref[block], TURNED, preferred_element_type=jnp.float32)
        source[block] = (running_ref[block] - total).astype(jnp.bfloat16)
    for block in range(blocks):
        drive = lax.dot_general(source[block], inverse_ref[block], TURNED, preferred_element_type=jnp.float32)
        for pair in range(pairs):
            forcing_ref[pair, pl.ds(block, days, stride=blocks), :] = jnp.where(
                seen, drive[pair * days : (pair + 1) * days], 0.0
            )
    states = [jnp.zeros((blocks, LANES), jnp.float32)] * pairs
    for day in range(days):
        rows = pl.ds(day * blocks, blocks)
        factor = retain_ref[rows, :]
        for pair in range(pairs):
            states[pair] = factor * states[pair] + forcing_ref[pair, rows, :]
    leave(message_ref, states)
    message_ref[pairs] = product_ref[...]


def leave(message_ref, values):
    for pair, value in enumerate(values):
        message_ref[pair] = value.astype(jnp.bfloat16)


def collect(piece_refs, inbox):
    me = lax.axis_index("tm")
    for k, ref in enumerate(piece_refs):
        inbox[me ^ (k + 1)] = ref[...]


def carried(pairs, inbox, products, backward):
    me, count = lax.axis_index("tm"), inbox.shape[0]
    carries = [jnp.zeros(inbox.shape[2:], jnp.float32)] * pairs
    for slab in range(count - 1, 0, -1) if backward else range(count - 1):
        valid = slab > me if backward else slab < me
        terms = products[slab, pairs].astype(jnp.float32)
        factor = terms + pltpu.roll(terms, LANES // 2, 1)
        for pair in range(pairs):
            update = inbox[slab, pair].astype(jnp.float32) + factor * carries[pair]
            carries[pair] = jnp.where(valid, update, carries[pair])
    return carries


def states_kernel(dims, forcing_ref, retain_ref, states_ref, through_ref, stage, products):
    days, blocks, size, probes = dims
    pairs = forcing_ref.shape[0]
    states = [jnp.zeros((blocks, LANES), jnp.float32)] * pairs
    product = jnp.ones((blocks, LANES), jnp.float32)
    for day in range(days):
        rows = pl.ds(day * blocks, blocks)
        factor = retain_ref[rows, :]
        product = product * factor
        products[rows, :] = product
        for pair in range(pairs):
            states[pair] = factor * states[pair] + forcing_ref[pair, rows, :]
            stage[pair, rows, :] = states[pair]
    for block in range(blocks):
        through_ref[block] = products[pl.ds(block, days, stride=blocks), :]
        for pair in range(pairs):
            states_ref[block, pl.ds(pair * days, days), :] = stage[pair, pl.ds(block, days, stride=blocks), :]


def adjoint_kernel(dims, hops, days_ref, states_ref, through_ref, retain_ref, inverse_ref, *rest):
    days, blocks, size, probes = dims
    adjoint_ref, message_ref, inbox, enter = rest[hops:]
    pairs = adjoint_ref.shape[0]
    collect(rest[:hops], inbox)
    seen = lax.broadcasted_iota(jnp.int32, (days, LANES), 0) < days_ref[0]
    for pair, carry in enumerate(carried(pairs, inbox, inbox, False)):
        enter[pair] = carry
    for block in range(blocks):
        through = through_ref[block]
        stored = [
            (states_ref[block, pl.ds(pair * days, days), :] + through * enter[pair, pl.ds(block, 1), :])
            .astype(jnp.bfloat16)
            for pair in range(pairs)
        ]
        adjoint = jnp.dot(jnp.concatenate(stored, axis=0), inverse_ref[block], preferred_element_type=jnp.float32)
        for pair in range(pairs):
            adjoint_ref[pair, pl.ds(block, days, stride=blocks), :] = jnp.where(
                seen, adjoint[pair * days : (pair + 1) * days], 0.0
            )
    carries = [jnp.zeros((blocks, LANES), jnp.float32)] * pairs
    for day in reversed(range(days)):
        rows = pl.ds(day * blocks, blocks)
        factor = retain_ref[rows, :]
        for pair in range(pairs):
            carries[pair] = factor * (adjoint_ref[pair, rows, :] + carries[pair])
    leave(message_ref, carries)


def own_kernel(dims, adjoint_ref, retain_ref, moved_ref, partial_ref):
    days, blocks, size, probes = dims
    pairs = adjoint_ref.shape[0]
    carries = [jnp.zeros((blocks, LANES), jnp.float32)] * pairs
    for day in reversed(range(days)):
        rows = pl.ds(day * blocks, blocks)
        factor = retain_ref[rows, :]
        total = None
        for pair in range(pairs):
            smoothed = adjoint_ref[pair, rows, :] + carries[pair]
            carries[pair] = factor * smoothed
            term = smoothed * moved_ref[pair, rows, :].astype(jnp.float32)
            total = term if total is None else total + term
        partial_ref[rows, :] = total


def variance_kernel(dims, hops, partial_ref, retain_ref, moved_ref, *rest):
    days, blocks, size, probes = dims
    pairs = moved_ref.shape[0]
    out_hbm, stage, inbox, products, out_ref, left = rest[2 * hops :]
    collect(rest[:hops], inbox)
    collect(rest[hops : 2 * hops], products)
    carries = carried(pairs, inbox, products, True)
    reach = jnp.ones((blocks, LANES), jnp.float32)
    parts = left.shape[0]
    part = days // parts
    lane = lax.broadcasted_iota(jnp.int32, (part, LANES), 1)
    copies = []
    for first in reversed(range(0, days, part)):
        for day in reversed(range(first, first + part)):
            rows = pl.ds(day * blocks, blocks)
            total = None
            for pair in range(pairs):
                term = carries[pair] * moved_ref[pair, rows, :].astype(jnp.float32)
                total = term if total is None else total + term
            stage[rows, :] = partial_ref[rows, :] + reach * total
            reach = reach * retain_ref[rows, :]
        done = pl.ds(first, part)
        for block in range(0, blocks, 2):
            both = [stage[pl.ds(first * blocks + block + half, part, stride=blocks), :] for half in range(2)]
            both = [value + pltpu.roll(value, size, 1) for value in both]
            out_ref[done, pl.ds(block * size, LANES)] = jnp.where(lane < size, both[0], both[1]) * (1.0 / probes)
        copies.append(pltpu.make_async_copy(out_ref.at[done], out_hbm.at[done], left.at[len(copies)]))
        copies[-1].start()
    for copy in copies:
        copy.wait()


def call(kernel, outs, scratch, flops, moved, scalars, *operands, apart=(), limit=VMEM_LIMIT, out_space=pltpu.VMEM):
    in_specs = [
        pl.BlockSpec(memory_space=pltpu.SMEM if i < scalars else pl.ANY if i in apart else pltpu.VMEM)
        for i in range(len(operands))
    ]
    return pl.pallas_call(
        kernel,
        out_shape=[jax.ShapeDtypeStruct(shape, kind) for shape, kind in outs],
        in_specs=in_specs,
        out_specs=[pl.BlockSpec(memory_space=out_space) for _ in outs],
        scratch_shapes=scratch,
        compiler_params=pltpu.CompilerParams(vmem_limit_bytes=limit),
        cost_estimate=pl.CostEstimate(flops=flops, bytes_accessed=moved, transcendentals=0),
    )(*operands)


def crossed(block, axis, bits):
    return lax.ppermute(block, axis, [(i, i ^ bits) for i in range(lax.axis_size(axis))])


def local(
    probes,
    local_links,
    remote_links,
    shared_blocks,
    slab_days,
    local_coupling,
    remote_coupling,
    block_inverse,
    retention,
):
    days, blocks, width = probes.shape
    size = block_inverse.shape[1]
    dims = (days, blocks, size, width // size)
    pairs = width // LANES
    f32, bf16 = jnp.float32, jnp.bfloat16
    bound = shared_blocks.shape[1]
    far = remote_links.shape[1]
    rows = days * blocks
    groups = lax.axis_size("space")
    held = groups // 2 * bound
    near_table, far_table = local_links.T, remote_links.T
    big = ((pairs, rows, LANES), f32)

    (outgoing,) = call(
        functools.partial(outgoing_kernel, dims),
        [((bound, pairs * days, LANES), bf16)],
        [
            pltpu.SMEM(shared_blocks.shape, jnp.int32),
            pltpu.VMEM(probes.shape, bf16),
            pltpu.SemaphoreType.DMA,
            pltpu.SemaphoreType.DMA((2,)),
        ],
        10**9, 4 * 10**6, 0, shared_blocks, probes, apart=(0, 1), limit=63 * 1024 * 1024,
    )
    pieces = {bits: crossed(outgoing, "space", bits) for bits in range(groups - 2, 0, -2)}
    by_block = (blocks, pairs * days, LANES)
    moved, turned = call(
        functools.partial(turn_kernel, dims),
        [((pairs, rows, LANES), bf16), (by_block, bf16)],
        [pltpu.VMEM(*big)], 10**10, 10**7, 0, probes,
    )
    running, retain, product, remote_weight, inverse = call(
        functools.partial(local_kernel, dims),
        [
            (by_block, f32),
            ((rows, LANES), f32),
            ((blocks, LANES), bf16),
            ((blocks, LANES, far * LANES), bf16),
            ((blocks, LANES, LANES), bf16),
        ],
        [], 10**10, 10**7, 2,
        near_table, slab_days, turned, local_coupling, remote_coupling, block_inverse, retention,
    )
    same, other = {0: outgoing}, {0: crossed(outgoing, "space", 1)}
    for bits in range(groups - 2, 0, -2):
        (same[bits],) = call(pass_kernel, [(outgoing.shape, bf16)], [], 0, 10**5, 0, pieces[bits], product)
        other[bits] = crossed(same[bits], "space", 1)
    same, other = list(same.values()), list(other.values())
    raw = [pieces[bits] for bits in range(2, groups, 2)]
    slabs = lax.axis_size("tm")
    hops = slabs - 1
    exchange = lambda message: [crossed(message, "tm", bits) for bits in range(hops, 0, -1)][::-1]
    inbox = pltpu.VMEM((slabs, pairs + 1, blocks, LANES), bf16)
    forcing, message = call(
        functools.partial(forward_kernel, dims, len(same)),
        [big, ((pairs + 1, blocks, LANES), bf16)],
        [pltpu.VMEM((2 * held, pairs * days, LANES), bf16), pltpu.VMEM((blocks, pairs * days, LANES), bf16)],
        10**10, 10**7, 2,
        far_table, slab_days, running, remote_weight, inverse, retain, product, *raw, *same, *other,
        apart=range(7, 7 + len(raw)),
    )
    ends = exchange(message)
    states, through = call(
        functools.partial(states_kernel, dims),
        [(by_block, f32), ((blocks, days, LANES), f32)],
        [pltpu.VMEM(*big), pltpu.VMEM((rows, LANES), f32)], 10**9, 10**6, 0, forcing, retain,
    )
    adjoint, message = call(
        functools.partial(adjoint_kernel, dims, hops),
        [big, ((pairs, blocks, LANES), bf16)],
        [inbox, pltpu.VMEM((pairs, blocks, LANES), f32)], 10**10, 10**7, 1,
        slab_days, states, through, retain, inverse, *ends,
    )
    starts = exchange(message)
    (partial,) = call(
        functools.partial(own_kernel, dims), [((rows, LANES), f32)], [], 10**9, 10**6, 0, adjoint, retain, moved
    )
    (variance,) = call(
        functools.partial(variance_kernel, dims, hops),
        [((days, blocks * size), f32)],
        [
            pltpu.VMEM((rows, LANES), f32),
            pltpu.VMEM((slabs, pairs, blocks, LANES), bf16),
            inbox,
            pltpu.VMEM((days, blocks * size), f32),
            pltpu.SemaphoreType.DMA((2,)),
        ],
        10**10, 10**7, 0, partial, retain, moved, *starts, *ends, out_space=pl.ANY,
    )
    return variance


def solution(mesh):
    placed = (
        P("tm", "space", None),
        P("space", None),
        P("space", None),
        P("space", None),
        P("tm"),
        P("space", None, None, None),
        P("space", None, None, None),
        P("space", None, None),
        P("tm", "space"),
    )
    return jax.shard_map(
        local, mesh=mesh, in_specs=placed, out_specs=P("tm", "space"), check_vma=False
    )
```

```python
import functools

import jax
import jax.numpy as jnp
from jax import lax
from jax.experimental import pallas as pl
from jax.experimental.pallas import tpu as pltpu
from jax.sharding import PartitionSpec as P

LANES = 128
VMEM_LIMIT = 20 * 1024 * 1024
TURNED = (((1,), (1,)), ((), ()))


def permutation(size, probes, start, width):
    total = size * probes
    column = lax.broadcasted_iota(jnp.int32, (total, width), 1) + start
    origin = (column % size) * probes + column // size
    row = lax.broadcasted_iota(jnp.int32, (total, width), 0)
    return (row == origin).astype(jnp.float32).astype(jnp.bfloat16)


def turned_pair(weight):
    return doubled(weight).astype(jnp.float32).T.astype(jnp.bfloat16)


def doubled(weight):
    zero = jnp.zeros_like(weight)
    return jnp.concatenate(
        [jnp.concatenate([weight, zero], axis=1), jnp.concatenate([zero, weight], axis=1)], axis=0
    )


def outgoing_kernel(dims, shared_hbm, z_hbm, outgoing_ref, shared_ref, z_ref, listed, arrived):
    days, blocks, size, probes = dims
    count = outgoing_ref.shape[0]
    parts = arrived.shape[0]
    part = days // parts
    copies = [
        pltpu.make_async_copy(z_hbm.at[pl.ds(i * part, part)], z_ref.at[pl.ds(i * part, part)], arrived.at[i])
        for i in range(parts)
    ]
    listing = pltpu.make_async_copy(shared_hbm, shared_ref, listed)
    listing.start()
    for copy in copies:
        copy.start()
    row = lax.broadcasted_iota(jnp.int32, (part, part * blocks), 0)
    column = lax.broadcasted_iota(jnp.int32, (part, part * blocks), 1)
    step = 2 * LANES
    shift, ranges = step // size, size * probes // step
    move = permutation(size, probes, 0, step)
    listing.wait()
    picks = [(column == row * blocks + shared_ref[0, m]).astype(jnp.float32) for m in range(count)]
    picks = jnp.concatenate(picks, axis=0).astype(jnp.bfloat16)
    for i, copy in enumerate(copies):
        copy.wait()
        z = z_ref[pl.ds(i * part, part)].reshape(part * blocks, size * probes)
        picked = jnp.dot(picks, z, preferred_element_type=jnp.float32)
        shifted = [picked] + [pltpu.roll(picked, size * probes - k * shift, 1) for k in range(1, ranges)]
        shifted = jnp.concatenate(shifted, axis=0).astype(jnp.bfloat16)
        moved = jnp.dot(shifted, move, preferred_element_type=jnp.float32).astype(jnp.bfloat16)
        for pair in range(size * probes // LANES):
            for m in range(count):
                row, lane = (pair // 2 * count + m) * part, pair % 2 * LANES
                outgoing_ref[m, pl.ds(pair * days + i * part, part), :] = moved[row : row + part, lane : lane + LANES]


def turn_kernel(dims, z_ref, moved_ref, turned_ref, stage):
    days, blocks, size, probes = dims
    pairs = size * probes // LANES
    z = z_ref[...].reshape(days * blocks, size * probes)
    step = 2 * LANES
    for start in range(0, size * probes, step):
        moved = jnp.dot(z, permutation(size, probes, start, step), preferred_element_type=jnp.float32)
        for half in range(2):
            pair = start // LANES + half
            tile = moved[:, half * LANES : (half + 1) * LANES]
            stage[pair] = tile
            moved_ref[pair] = tile.astype(jnp.bfloat16)
    for block in range(blocks):
        for pair in range(pairs):
            rows = stage[pair, pl.ds(block, days, stride=blocks), :]
            turned_ref[block, pl.ds(pair * days, days), :] = rows.astype(jnp.bfloat16)


def local_kernel(
    dims, links_ref, days_ref, turned_ref, weight_ref, remote_weight_ref, inverse_ref, retention_ref,
    running_ref, retain_ref, product_ref, remote_turned_ref, inverse_turned_ref, inverse_doubled_ref,
):
    days, blocks, size, probes = dims
    count = links_ref.shape[0]
    for block in range(blocks):
        near = jnp.concatenate([turned_ref[links_ref[k, block]] for k in range(count)], axis=1)
        weight = jnp.concatenate([doubled(weight_ref[block, k]) for k in range(count)], axis=1)
        total = lax.dot_general(near, weight, TURNED, preferred_element_type=jnp.float32)
        running_ref[block] = turned_ref[block].astype(jnp.float32) - total
        remote_turned_ref[block] = jnp.concatenate(
            [turned_pair(remote_weight_ref[block, k]) for k in range(remote_weight_ref.shape[1])], axis=0
        )
        inverse_turned_ref[block] = turned_pair(inverse_ref[block])
        inverse_doubled_ref[block] = doubled(inverse_ref[block])
    observed = days_ref[0]
    shape = (days, LANES)
    first = lax.broadcasted_iota(jnp.int32, shape, 1) < size
    seen = lax.broadcasted_iota(jnp.int32, shape, 0) < observed
    for block in range(0, blocks, 2):
        factor = jnp.where(seen, retention_ref[:, pl.ds(block * size, LANES)], 1.0)
        other = pltpu.roll(factor, size, 1)
        retain_ref[pl.ds(block, days, stride=blocks), :] = jnp.where(first, factor, other)
        retain_ref[pl.ds(block + 1, days, stride=blocks), :] = jnp.where(first, other, factor)
    product = jnp.ones((blocks, LANES), jnp.float32)
    for day in range(days):
        product = product * retain_ref[pl.ds(day * blocks, blocks), :]
    high = product.astype(jnp.bfloat16).astype(jnp.float32)
    half = lax.broadcasted_iota(jnp.int32, product.shape, 1) < size
    product_ref[...] = jnp.where(half, high, product - high).astype(jnp.bfloat16)


def pass_kernel(piece_ref, product_ref, out_ref):
    out_ref[...] = piece_ref[...]


def forward_kernel(
    dims, pieces, links_ref, days_ref, running_ref, weight_ref, inverse_ref, retain_ref, product_ref, *rest
):
    days, blocks, size, probes = dims
    piece_refs = rest[pieces - 1 : 3 * pieces - 1]
    forcing_ref, message_ref, remote, source = rest[3 * pieces - 1 :]
    pairs = forcing_ref.shape[0]
    count = links_ref.shape[0]
    bound = piece_refs[0].shape[0]
    held = pieces * bound
    me = lax.axis_index("space")
    for k, ref in enumerate(piece_refs):
        chip = (pieces - k) % pieces
        remote[pl.ds(k // pieces * held + chip % pieces * bound, bound)] = ref[...]
    seen = lax.broadcasted_iota(jnp.int32, (days, LANES), 0) < days_ref[0]
    for block in range(blocks):
        places = []
        for k in range(count):
            link = links_ref[k, block]
            distance = (link // bound) ^ me
            places.append((distance % 2) * held + (distance // 2) * bound + link % bound)
        far = jnp.concatenate([remote[place] for place in places], axis=1)
        total = jnp.dot(far, weight_ref[block], preferred_element_type=jnp.float32)
        source[block] = (running_ref[block] - total).astype(jnp.bfloat16)
    for block in range(blocks):
        drive = jnp.dot(source[block], inverse_ref[block], preferred_element_type=jnp.float32)
        for pair in range(pairs):
            forcing_ref[pair, pl.ds(block, days, stride=blocks), :] = jnp.where(
                seen, drive[pair * days : (pair + 1) * days], 0.0
            )
    states = [jnp.zeros((blocks, LANES), jnp.float32)] * pairs
    for day in range(days):
        rows = pl.ds(day * blocks, blocks)
        factor = retain_ref[rows, :]
        for pair in range(pairs):
            states[pair] = factor * states[pair] + forcing_ref[pair, rows, :]
    leave(message_ref, states)
    message_ref[pairs] = product_ref[...]


def leave(message_ref, values):
    for pair, value in enumerate(values):
        message_ref[pair] = value.astype(jnp.bfloat16)


def collect(piece_refs, inbox):
    me = lax.axis_index("tm")
    for k, ref in enumerate(piece_refs):
        inbox[me ^ (k + 1)] = ref[...]


def carried(pairs, inbox, products, backward):
    me, count = lax.axis_index("tm"), inbox.shape[0]
    carries = [jnp.zeros(inbox.shape[2:], jnp.float32)] * pairs
    for slab in range(count - 1, 0, -1) if backward else range(count - 1):
        valid = slab > me if backward else slab < me
        terms = products[slab, pairs].astype(jnp.float32)
        factor = terms + pltpu.roll(terms, LANES // 2, 1)
        for pair in range(pairs):
            update = inbox[slab, pair].astype(jnp.float32) + factor * carries[pair]
            carries[pair] = jnp.where(valid, update, carries[pair])
    return carries


def states_kernel(dims, forcing_ref, retain_ref, states_ref, through_ref, stage, products):
    days, blocks, size, probes = dims
    pairs = forcing_ref.shape[0]
    states = [jnp.zeros((blocks, LANES), jnp.float32)] * pairs
    product = jnp.ones((blocks, LANES), jnp.float32)
    for day in range(days):
        rows = pl.ds(day * blocks, blocks)
        factor = retain_ref[rows, :]
        product = product * factor
        products[rows, :] = product
        for pair in range(pairs):
            states[pair] = factor * states[pair] + forcing_ref[pair, rows, :]
            stage[pair, rows, :] = states[pair]
    for block in range(blocks):
        through_ref[block] = products[pl.ds(block, days, stride=blocks), :]
        for pair in range(pairs):
            states_ref[block, pl.ds(pair * days, days), :] = stage[pair, pl.ds(block, days, stride=blocks), :]


def adjoint_kernel(dims, hops, days_ref, states_ref, through_ref, retain_ref, inverse_ref, *rest):
    days, blocks, size, probes = dims
    adjoint_ref, message_ref, inbox, enter = rest[hops:]
    pairs = adjoint_ref.shape[0]
    collect(rest[:hops], inbox)
    seen = lax.broadcasted_iota(jnp.int32, (days, LANES), 0) < days_ref[0]
    for pair, carry in enumerate(carried(pairs, inbox, inbox, False)):
        enter[pair] = carry
    for block in range(blocks):
        through = through_ref[block]
        stored = [
            (states_ref[block, pl.ds(pair * days, days), :] + through * enter[pair, pl.ds(block, 1), :])
            .astype(jnp.bfloat16)
            for pair in range(pairs)
        ]
        adjoint = jnp.dot(jnp.concatenate(stored, axis=0), inverse_ref[block], preferred_element_type=jnp.float32)
        for pair in range(pairs):
            adjoint_ref[pair, pl.ds(block, days, stride=blocks), :] = jnp.where(
                seen, adjoint[pair * days : (pair + 1) * days], 0.0
            )
    carries = [jnp.zeros((blocks, LANES), jnp.float32)] * pairs
    for day in reversed(range(days)):
        rows = pl.ds(day * blocks, blocks)
        factor = retain_ref[rows, :]
        for pair in range(pairs):
            carries[pair] = factor * (adjoint_ref[pair, rows, :] + carries[pair])
    leave(message_ref, carries)


def own_kernel(dims, adjoint_ref, retain_ref, moved_ref, partial_ref):
    days, blocks, size, probes = dims
    pairs = adjoint_ref.shape[0]
    carries = [jnp.zeros((blocks, LANES), jnp.float32)] * pairs
    for day in reversed(range(days)):
        rows = pl.ds(day * blocks, blocks)
        factor = retain_ref[rows, :]
        total = None
        for pair in range(pairs):
            smoothed = adjoint_ref[pair, rows, :] + carries[pair]
            carries[pair] = factor * smoothed
            term = smoothed * moved_ref[pair, rows, :].astype(jnp.float32)
            total = term if total is None else total + term
        partial_ref[rows, :] = total


def variance_kernel(dims, hops, partial_ref, retain_ref, moved_ref, *rest):
    days, blocks, size, probes = dims
    pairs = moved_ref.shape[0]
    out_hbm, stage, inbox, products, out_ref, left = rest[2 * hops :]
    collect(rest[:hops], inbox)
    collect(rest[hops : 2 * hops], products)
    carries = carried(pairs, inbox, products, True)
    reach = jnp.ones((blocks, LANES), jnp.float32)
    parts = left.shape[0]
    part = days // parts
    lane = lax.broadcasted_iota(jnp.int32, (part, LANES), 1)
    copies = []
    for first in reversed(range(0, days, part)):
        for day in reversed(range(first, first + part)):
            rows = pl.ds(day * blocks, blocks)
            total = None
            for pair in range(pairs):
                term = carries[pair] * moved_ref[pair, rows, :].astype(jnp.float32)
                total = term if total is None else total + term
            stage[rows, :] = partial_ref[rows, :] + reach * total
            reach = reach * retain_ref[rows, :]
        done = pl.ds(first, part)
        for block in range(0, blocks, 2):
            both = [stage[pl.ds(first * blocks + block + half, part, stride=blocks), :] for half in range(2)]
            both = [value + pltpu.roll(value, size, 1) for value in both]
            out_ref[done, pl.ds(block * size, LANES)] = jnp.where(lane < size, both[0], both[1]) * (1.0 / probes)
        copies.append(pltpu.make_async_copy(out_ref.at[done], out_hbm.at[done], left.at[len(copies)]))
        copies[-1].start()
    for copy in copies:
        copy.wait()


def call(kernel, outs, scratch, flops, moved, scalars, *operands, apart=(), limit=VMEM_LIMIT, out_space=pltpu.VMEM):
    in_specs = [
        pl.BlockSpec(memory_space=pltpu.SMEM if i < scalars else pl.ANY if i in apart else pltpu.VMEM)
        for i in range(len(operands))
    ]
    return pl.pallas_call(
        kernel,
        out_shape=[jax.ShapeDtypeStruct(shape, kind) for shape, kind in outs],
        in_specs=in_specs,
        out_specs=[pl.BlockSpec(memory_space=out_space) for _ in outs],
        scratch_shapes=scratch,
        compiler_params=pltpu.CompilerParams(vmem_limit_bytes=limit),
        cost_estimate=pl.CostEstimate(flops=flops, bytes_accessed=moved, transcendentals=0),
    )(*operands)


def crossed(block, axis, bits):
    return lax.ppermute(block, axis, [(i, i ^ bits) for i in range(lax.axis_size(axis))])


def local(
    probes,
    local_links,
    remote_links,
    shared_blocks,
    slab_days,
    local_coupling,
    remote_coupling,
    block_inverse,
    retention,
):
    days, blocks, width = probes.shape
    size = block_inverse.shape[1]
    dims = (days, blocks, size, width // size)
    pairs = width // LANES
    f32, bf16 = jnp.float32, jnp.bfloat16
    bound = shared_blocks.shape[1]
    far = remote_links.shape[1]
    rows = days * blocks
    groups = lax.axis_size("space")
    held = groups // 2 * bound
    near_table, far_table = local_links.T, remote_links.T
    big = ((pairs, rows, LANES), f32)

    (outgoing,) = call(
        functools.partial(outgoing_kernel, dims),
        [((bound, pairs * days, LANES), bf16)],
        [
            pltpu.SMEM(shared_blocks.shape, jnp.int32),
            pltpu.VMEM(probes.shape, bf16),
            pltpu.SemaphoreType.DMA,
            pltpu.SemaphoreType.DMA((days // 16,)),
        ],
        10**9, 4 * 10**6, 0, shared_blocks, probes, apart=(0, 1), limit=63 * 1024 * 1024,
    )
    pieces = {bits: crossed(outgoing, "space", bits) for bits in range(groups - 2, 0, -2)}
    by_block = (blocks, pairs * days, LANES)
    moved, turned = call(
        functools.partial(turn_kernel, dims),
        [((pairs, rows, LANES), bf16), (by_block, bf16)],
        [pltpu.VMEM(*big)], 10**10, 10**7, 0, probes,
    )
    running, retain, product, remote_weight, inverse_turned, inverse = call(
        functools.partial(local_kernel, dims),
        [
            (by_block, f32),
            ((rows, LANES), f32),
            ((blocks, LANES), bf16),
            ((blocks, far * LANES, LANES), bf16),
            ((blocks, LANES, LANES), bf16),
            ((blocks, LANES, LANES), bf16),
        ],
        [], 10**10, 10**7, 2,
        near_table, slab_days, turned, local_coupling, remote_coupling, block_inverse, retention,
    )
    same, other = {0: outgoing}, {0: crossed(outgoing, "space", 1)}
    for bits in range(groups - 2, 0, -2):
        (same[bits],) = call(pass_kernel, [(outgoing.shape, bf16)], [], 0, 10**5, 0, pieces[bits], product)
        other[bits] = crossed(same[bits], "space", 1)
    same, other = list(same.values()), list(other.values())
    raw = [pieces[bits] for bits in range(2, groups, 2)]
    slabs = lax.axis_size("tm")
    hops = slabs - 1
    exchange = lambda message: [crossed(message, "tm", bits) for bits in range(hops, 0, -1)][::-1]
    inbox = pltpu.VMEM((slabs, pairs + 1, blocks, LANES), bf16)
    forcing, message = call(
        functools.partial(forward_kernel, dims, len(same)),
        [big, ((pairs + 1, blocks, LANES), bf16)],
        [pltpu.VMEM((2 * held, pairs * days, LANES), bf16), pltpu.VMEM((blocks, pairs * days, LANES), bf16)],
        10**10, 10**7, 2,
        far_table, slab_days, running, remote_weight, inverse_turned, retain, product, *raw, *same, *other,
        apart=range(7, 7 + len(raw)),
    )
    ends = exchange(message)
    states, through = call(
        functools.partial(states_kernel, dims),
        [(by_block, f32), ((blocks, days, LANES), f32)],
        [pltpu.VMEM(*big), pltpu.VMEM((rows, LANES), f32)], 10**9, 10**6, 0, forcing, retain,
    )
    adjoint, message = call(
        functools.partial(adjoint_kernel, dims, hops),
        [big, ((pairs, blocks, LANES), bf16)],
        [inbox, pltpu.VMEM((pairs, blocks, LANES), f32)], 10**10, 10**7, 1,
        slab_days, states, through, retain, inverse, *ends,
    )
    starts = exchange(message)
    (partial,) = call(
        functools.partial(own_kernel, dims), [((rows, LANES), f32)], [], 10**9, 10**6, 0, adjoint, retain, moved
    )
    (variance,) = call(
        functools.partial(variance_kernel, dims, hops),
        [((days, blocks * size), f32)],
        [
            pltpu.VMEM((rows, LANES), f32),
            pltpu.VMEM((slabs, pairs, blocks, LANES), bf16),
            inbox,
            pltpu.VMEM((days, blocks * size), f32),
            pltpu.SemaphoreType.DMA((2,)),
        ],
        10**10, 10**7, 0, partial, retain, moved, *starts, *ends, out_space=pl.ANY,
    )
    return variance


def solution(mesh):
    placed = (
        P("tm", "space", None),
        P("space", None),
        P("space", None),
        P("space", None),
        P("tm"),
        P("space", None, None, None),
        P("space", None, None, None),
        P("space", None, None),
        P("tm", "space"),
    )
    return jax.shard_map(
        local, mesh=mesh, in_specs=placed, out_specs=P("tm", "space"), check_vma=False
    )
```

```python
import functools

import jax
import jax.numpy as jnp
from jax import lax
from jax.experimental import pallas as pl
from jax.experimental.pallas import tpu as pltpu
from jax.sharding import PartitionSpec as P

LANES = 128
VMEM_LIMIT = 20 * 1024 * 1024
TURNED = (((1,), (1,)), ((), ()))


def permutation(size, probes, start, width):
    total = size * probes
    column = lax.broadcasted_iota(jnp.int32, (total, width), 1) + start
    origin = (column % size) * probes + column // size
    row = lax.broadcasted_iota(jnp.int32, (total, width), 0)
    return (row == origin).astype(jnp.float32).astype(jnp.bfloat16)


def doubled(weight):
    zero = jnp.zeros_like(weight)
    return jnp.concatenate(
        [jnp.concatenate([weight, zero], axis=1), jnp.concatenate([zero, weight], axis=1)], axis=0
    )


def outgoing_kernel(dims, shared_hbm, z_hbm, outgoing_ref, shared_ref, z_ref, listed, arrived):
    days, blocks, size, probes = dims
    count = outgoing_ref.shape[0]
    parts = arrived.shape[0]
    part = days // parts
    copies = [
        pltpu.make_async_copy(z_hbm.at[pl.ds(i * part, part)], z_ref.at[pl.ds(i * part, part)], arrived.at[i])
        for i in range(parts)
    ]
    listing = pltpu.make_async_copy(shared_hbm, shared_ref, listed)
    listing.start()
    for copy in copies:
        copy.start()
    row = lax.broadcasted_iota(jnp.int32, (part, part * blocks), 0)
    column = lax.broadcasted_iota(jnp.int32, (part, part * blocks), 1)
    move = permutation(size, probes, 0, 2 * LANES)
    listing.wait()
    picks = [(column == row * blocks + shared_ref[0, m]).astype(jnp.float32) for m in range(count)]
    picks = jnp.concatenate(picks, axis=0).astype(jnp.bfloat16)
    picked = []
    for i, copy in enumerate(copies):
        copy.wait()
        z = z_ref[pl.ds(i * part, part)].reshape(part * blocks, size * probes)
        picked.append(jnp.dot(picks, z, preferred_element_type=jnp.float32))
    picked = jnp.concatenate([rows[m * part : (m + 1) * part] for m in range(count) for rows in picked], axis=0)
    step = 2 * LANES
    shift = step // size
    ranges = size * probes // step
    shifted = [picked] + [pltpu.roll(picked, size * probes - i * shift, 1) for i in range(1, ranges)]
    shifted = jnp.concatenate(shifted, axis=0).astype(jnp.bfloat16)
    moved = jnp.dot(shifted, move, preferred_element_type=jnp.float32)
    moved = moved.astype(jnp.bfloat16)
    for pair in range(size * probes // LANES):
        for m in range(count):
            row, lane = (pair // 2 * count + m) * days, pair % 2 * LANES
            outgoing_ref[m, pl.ds(pair * days, days), :] = moved[row : row + days, lane : lane + LANES]


def turn_kernel(dims, z_ref, moved_ref, turned_ref, stage):
    days, blocks, size, probes = dims
    pairs = size * probes // LANES
    z = z_ref[...].reshape(days * blocks, size * probes)
    step = 2 * LANES
    for start in range(0, size * probes, step):
        moved = jnp.dot(z, permutation(size, probes, start, step), preferred_element_type=jnp.float32)
        for half in range(2):
            pair = start // LANES + half
            tile = moved[:, half * LANES : (half + 1) * LANES]
            stage[pair] = tile
            moved_ref[pair] = tile.astype(jnp.bfloat16)
    for block in range(blocks):
        for pair in range(pairs):
            rows = stage[pair, pl.ds(block, days, stride=blocks), :]
            turned_ref[block, pl.ds(pair * days, days), :] = rows.astype(jnp.bfloat16)


def local_kernel(
    dims, links_ref, days_ref, turned_ref, weight_ref, remote_weight_ref, inverse_ref, retention_ref,
    running_ref, retain_ref, product_ref, remote_doubled_ref, inverse_doubled_ref, through_ref, beyond_ref, stage,
):
    days, blocks, size, probes = dims
    count = links_ref.shape[0]
    for block in range(blocks):
        near = jnp.concatenate([turned_ref[links_ref[k, block]] for k in range(count)], axis=1)
        weight = jnp.concatenate([doubled(weight_ref[block, k]) for k in range(count)], axis=1)
        total = lax.dot_general(near, weight, TURNED, preferred_element_type=jnp.float32)
        running_ref[block] = turned_ref[block].astype(jnp.float32) - total
        remote_doubled_ref[block] = jnp.concatenate(
            [doubled(remote_weight_ref[block, k]) for k in range(remote_weight_ref.shape[1])], axis=1
        )
        inverse_doubled_ref[block] = doubled(inverse_ref[block])
    observed = days_ref[0]
    shape = (days, LANES)
    first = lax.broadcasted_iota(jnp.int32, shape, 1) < size
    seen = lax.broadcasted_iota(jnp.int32, shape, 0) < observed
    for block in range(0, blocks, 2):
        factor = jnp.where(seen, retention_ref[:, pl.ds(block * size, LANES)], 1.0)
        other = pltpu.roll(factor, size, 1)
        retain_ref[pl.ds(block, days, stride=blocks), :] = jnp.where(first, factor, other)
        retain_ref[pl.ds(block + 1, days, stride=blocks), :] = jnp.where(first, other, factor)
    product = jnp.ones((blocks, LANES), jnp.float32)
    for day in range(days):
        rows = pl.ds(day * blocks, blocks)
        product = product * retain_ref[rows, :]
        stage[0, rows, :] = product
    after = jnp.ones((blocks, LANES), jnp.float32)
    for day in reversed(range(days)):
        rows = pl.ds(day * blocks, blocks)
        stage[1, rows, :] = after
        after = after * retain_ref[rows, :]
    for block in range(blocks):
        through_ref[block] = stage[0, pl.ds(block, days, stride=blocks), :]
        beyond_ref[block] = stage[1, pl.ds(block, days, stride=blocks), :]
    high = product.astype(jnp.bfloat16).astype(jnp.float32)
    half = lax.broadcasted_iota(jnp.int32, product.shape, 1) < size
    product_ref[...] = jnp.where(half, high, product - high).astype(jnp.bfloat16)


def pass_kernel(*refs):
    *piece_refs, product_ref, out_ref = refs
    count = piece_refs[0].shape[0]
    for k, ref in enumerate(piece_refs):
        out_ref[pl.ds(k * count, count)] = ref[...]


def forward_kernel(
    dims, pieces, links_ref, days_ref, running_ref, weight_ref, inverse_ref, beyond_ref, product_ref, *rest
):
    days, blocks, size, probes = dims
    piece_refs = rest[pieces - 1 : -5]
    forcing_ref, message_ref, remote, source, ends = rest[-5:]
    pairs = forcing_ref.shape[0]
    count = links_ref.shape[0]
    bound = piece_refs[0].shape[0]
    held = pieces * bound
    me = lax.axis_index("space")
    arrived = [ref.at[pl.ds(start, bound)] for ref in piece_refs for start in range(0, ref.shape[0], bound)]
    for k, ref in enumerate(arrived):
        chip = (pieces - k) % pieces
        remote[pl.ds(k // pieces * held + chip * bound, bound)] = ref[...]
    seen = lax.broadcasted_iota(jnp.int32, (days, LANES), 0) < days_ref[0]
    for block in range(blocks):
        places = []
        for k in range(count):
            link = links_ref[k, block]
            distance = (link // bound) ^ me
            places.append((distance % 2) * held + (distance // 2) * bound + link % bound)
        far = jnp.concatenate([remote[place] for place in places], axis=1)
        total = lax.dot_general(far, weight_ref[block], TURNED, preferred_element_type=jnp.float32)
        source[block] = (running_ref[block] - total).astype(jnp.bfloat16)
    for block in range(blocks):
        drive = lax.dot_general(source[block], inverse_ref[block], TURNED, preferred_element_type=jnp.float32)
        beyond = beyond_ref[block]
        for pair in range(pairs):
            tile = jnp.where(seen, drive[pair * days : (pair + 1) * days], 0.0)
            forcing_ref[pair, pl.ds(block, days, stride=blocks), :] = tile
            ends[pair, pl.ds(block, 1), :] = jnp.sum(beyond * tile, axis=0, keepdims=True)
    leave(message_ref, [ends[pair] for pair in range(pairs)])
    message_ref[pairs] = product_ref[...]


def leave(message_ref, values):
    for pair, value in enumerate(values):
        message_ref[pair] = value.astype(jnp.bfloat16)


def collect(piece_refs, inbox):
    me = lax.axis_index("tm")
    for k, ref in enumerate(piece_refs):
        inbox[me ^ (k + 1)] = ref[...]


def carried(pairs, inbox, products, backward):
    me, count = lax.axis_index("tm"), inbox.shape[0]
    carries = [jnp.zeros(inbox.shape[2:], jnp.float32)] * pairs
    for slab in range(count - 1, 0, -1) if backward else range(count - 1):
        valid = slab > me if backward else slab < me
        terms = products[slab, pairs].astype(jnp.float32)
        factor = terms + pltpu.roll(terms, LANES // 2, 1)
        for pair in range(pairs):
            update = inbox[slab, pair].astype(jnp.float32) + factor * carries[pair]
            carries[pair] = jnp.where(valid, update, carries[pair])
    return carries


def states_kernel(dims, forcing_ref, retain_ref, states_ref, stage):
    days, blocks, size, probes = dims
    pairs = forcing_ref.shape[0]
    states = [jnp.zeros((blocks, LANES), jnp.float32)] * pairs
    for day in range(days):
        rows = pl.ds(day * blocks, blocks)
        factor = retain_ref[rows, :]
        for pair in range(pairs):
            states[pair] = factor * states[pair] + forcing_ref[pair, rows, :]
            stage[pair, rows, :] = states[pair]
    for block in range(blocks):
        for pair in range(pairs):
            states_ref[block, pl.ds(pair * days, days), :] = stage[pair, pl.ds(block, days, stride=blocks), :]


def adjoint_kernel(dims, hops, days_ref, states_ref, through_ref, inverse_ref, *rest):
    days, blocks, size, probes = dims
    adjoint_ref, message_ref, inbox, enter, starts = rest[hops:]
    pairs = adjoint_ref.shape[0]
    collect(rest[:hops], inbox)
    seen = lax.broadcasted_iota(jnp.int32, (days, LANES), 0) < days_ref[0]
    for pair, carry in enumerate(carried(pairs, inbox, inbox, False)):
        enter[pair] = carry
    for block in range(blocks):
        through = through_ref[block]
        stored = [
            (states_ref[block, pl.ds(pair * days, days), :] + through * enter[pair, pl.ds(block, 1), :])
            .astype(jnp.bfloat16)
            for pair in range(pairs)
        ]
        adjoint = jnp.dot(jnp.concatenate(stored, axis=0), inverse_ref[block], preferred_element_type=jnp.float32)
        for pair in range(pairs):
            tile = jnp.where(seen, adjoint[pair * days : (pair + 1) * days], 0.0)
            adjoint_ref[pair, pl.ds(block, days, stride=blocks), :] = tile
            starts[pair, pl.ds(block, 1), :] = jnp.sum(through * tile, axis=0, keepdims=True)
    leave(message_ref, [starts[pair] for pair in range(pairs)])


def own_kernel(dims, adjoint_ref, retain_ref, moved_ref, partial_ref):
    days, blocks, size, probes = dims
    pairs = adjoint_ref.shape[0]
    carries = [jnp.zeros((blocks, LANES), jnp.float32)] * pairs
    for day in reversed(range(days)):
        rows = pl.ds(day * blocks, blocks)
        factor = retain_ref[rows, :]
        total = None
        for pair in range(pairs):
            smoothed = adjoint_ref[pair, rows, :] + carries[pair]
            carries[pair] = factor * smoothed
            term = smoothed * moved_ref[pair, rows, :].astype(jnp.float32)
            total = term if total is None else total + term
        partial_ref[rows, :] = total


def variance_kernel(dims, hops, partial_ref, retain_ref, moved_ref, *rest):
    days, blocks, size, probes = dims
    pairs = moved_ref.shape[0]
    out_hbm, stage, inbox, products, out_ref, left = rest[2 * hops :]
    collect(rest[:hops], inbox)
    collect(rest[hops : 2 * hops], products)
    carries = carried(pairs, inbox, products, True)
    reach = jnp.ones((blocks, LANES), jnp.float32)
    parts = left.shape[0]
    part = days // parts
    lane = lax.broadcasted_iota(jnp.int32, (part, LANES), 1)
    copies = []
    for first in reversed(range(0, days, part)):
        for day in reversed(range(first, first + part)):
            rows = pl.ds(day * blocks, blocks)
            total = None
            for pair in range(pairs):
                term = carries[pair] * moved_ref[pair, rows, :].astype(jnp.float32)
                total = term if total is None else total + term
            stage[rows, :] = partial_ref[rows, :] + reach * total
            reach = reach * retain_ref[rows, :]
        done = pl.ds(first, part)
        for block in range(0, blocks, 2):
            both = [stage[pl.ds(first * blocks + block + half, part, stride=blocks), :] for half in range(2)]
            both = [value + pltpu.roll(value, size, 1) for value in both]
            out_ref[done, pl.ds(block * size, LANES)] = jnp.where(lane < size, both[0], both[1]) * (1.0 / probes)
        copies.append(pltpu.make_async_copy(out_ref.at[done], out_hbm.at[done], left.at[len(copies)]))
        copies[-1].start()
    for copy in copies:
        copy.wait()


def call(kernel, outs, scratch, flops, moved, scalars, *operands, apart=(), limit=VMEM_LIMIT, out_space=pltpu.VMEM):
    in_specs = [
        pl.BlockSpec(memory_space=pltpu.SMEM if i < scalars else pl.ANY if i in apart else pltpu.VMEM)
        for i in range(len(operands))
    ]
    return pl.pallas_call(
        kernel,
        out_shape=[jax.ShapeDtypeStruct(shape, kind) for shape, kind in outs],
        in_specs=in_specs,
        out_specs=[pl.BlockSpec(memory_space=out_space) for _ in outs],
        scratch_shapes=scratch,
        compiler_params=pltpu.CompilerParams(vmem_limit_bytes=limit),
        cost_estimate=pl.CostEstimate(flops=flops, bytes_accessed=moved, transcendentals=0),
    )(*operands)


def crossed(block, axis, bits):
    return lax.ppermute(block, axis, [(i, i ^ bits) for i in range(lax.axis_size(axis))])


def local(
    probes,
    local_links,
    remote_links,
    shared_blocks,
    slab_days,
    local_coupling,
    remote_coupling,
    block_inverse,
    retention,
):
    days, blocks, width = probes.shape
    size = block_inverse.shape[1]
    dims = (days, blocks, size, width // size)
    pairs = width // LANES
    f32, bf16 = jnp.float32, jnp.bfloat16
    bound = shared_blocks.shape[1]
    far = remote_links.shape[1]
    rows = days * blocks
    groups = lax.axis_size("space")
    held = groups // 2 * bound
    near_table, far_table = local_links.T, remote_links.T
    big = ((pairs, rows, LANES), f32)

    (outgoing,) = call(
        functools.partial(outgoing_kernel, dims),
        [((bound, pairs * days, LANES), bf16)],
        [
            pltpu.SMEM(shared_blocks.shape, jnp.int32),
            pltpu.VMEM(probes.shape, bf16),
            pltpu.SemaphoreType.DMA,
            pltpu.SemaphoreType.DMA((2,)),
        ],
        10**9, 4 * 10**6, 0, shared_blocks, probes, apart=(0, 1), limit=63 * 1024 * 1024,
    )
    pieces = {bits: crossed(outgoing, "space", bits) for bits in range(groups - 2, 0, -2)}
    by_block = (blocks, pairs * days, LANES)
    moved, turned = call(
        functools.partial(turn_kernel, dims),
        [((pairs, rows, LANES), bf16), (by_block, bf16)],
        [pltpu.VMEM(*big)], 10**10, 10**7, 0, probes,
    )
    running, retain, product, remote_weight, inverse, through, beyond = call(
        functools.partial(local_kernel, dims),
        [
            (by_block, f32),
            ((rows, LANES), f32),
            ((blocks, LANES), bf16),
            ((blocks, LANES, far * LANES), bf16),
            ((blocks, LANES, LANES), bf16),
            ((blocks, days, LANES), f32),
            ((blocks, days, LANES), f32),
        ],
        [pltpu.VMEM((2, rows, LANES), f32)], 10**10, 10**7, 2,
        near_table, slab_days, turned, local_coupling, remote_coupling, block_inverse, retention,
    )
    same = [outgoing]
    for batch in ([groups - 2], list(range(groups - 4, 0, -2))):
        shape = (len(batch) * bound, pairs * days, LANES)
        same += call(pass_kernel, [(shape, bf16)], [], 0, 10**5, 0, *[pieces[bits] for bits in batch], product)
    other = [crossed(piece, "space", 1) for piece in same]
    raw = [pieces[bits] for bits in range(2, groups, 2)]
    slabs = lax.axis_size("tm")
    hops = slabs - 1
    exchange = lambda message: [crossed(message, "tm", bits) for bits in range(hops, 0, -1)][::-1]
    inbox = pltpu.VMEM((slabs, pairs + 1, blocks, LANES), bf16)
    values = pltpu.VMEM((pairs, blocks, LANES), f32)
    forcing, message = call(
        functools.partial(forward_kernel, dims, groups // 2),
        [big, ((pairs + 1, blocks, LANES), bf16)],
        [pltpu.VMEM((2 * held, pairs * days, LANES), bf16), pltpu.VMEM(by_block, bf16), values], 10**10, 10**7, 2,
        far_table, slab_days, running, remote_weight, inverse, beyond, product, *raw, *same, *other,
        apart=range(7, 7 + len(raw)),
    )
    ends = exchange(message)
    (states,) = call(
        functools.partial(states_kernel, dims), [(by_block, f32)], [pltpu.VMEM(*big)], 10**9, 10**6, 0, forcing, retain
    )
    adjoint, message = call(
        functools.partial(adjoint_kernel, dims, hops),
        [big, ((pairs, blocks, LANES), bf16)],
        [inbox, values, values], 10**10, 10**7, 1, slab_days, states, through, inverse, *ends,
    )
    starts = exchange(message)
    (partial,) = call(
        functools.partial(own_kernel, dims), [((rows, LANES), f32)], [], 10**9, 10**6, 0, adjoint, retain, moved
    )
    (variance,) = call(
        functools.partial(variance_kernel, dims, hops),
        [((days, blocks * size), f32)],
        [
            pltpu.VMEM((rows, LANES), f32),
            pltpu.VMEM((slabs, pairs, blocks, LANES), bf16),
            inbox,
            pltpu.VMEM((days, blocks * size), f32),
            pltpu.SemaphoreType.DMA((2,)),
        ],
        10**10, 10**7, 0, partial, retain, moved, *starts, *ends, out_space=pl.ANY,
    )
    return variance


def solution(mesh):
    placed = (
        P("tm", "space", None),
        P("space", None),
        P("space", None),
        P("space", None),
        P("tm"),
        P("space", None, None, None),
        P("space", None, None, None),
        P("space", None, None),
        P("tm", "space"),
    )
    return jax.shard_map(
        local, mesh=mesh, in_specs=placed, out_specs=P("tm", "space"), check_vma=False
    )
```

```python
import functools

import jax
import jax.numpy as jnp
from jax import lax
from jax.experimental import pallas as pl
from jax.experimental.pallas import tpu as pltpu
from jax.sharding import PartitionSpec as P

LANES = 128
VMEM_LIMIT = 20 * 1024 * 1024
TURNED = (((1,), (1,)), ((), ()))


def permutation(size, probes, start, width):
    total = size * probes
    column = lax.broadcasted_iota(jnp.int32, (total, width), 1) + start
    origin = (column % size) * probes + column // size
    row = lax.broadcasted_iota(jnp.int32, (total, width), 0)
    return (row == origin).astype(jnp.float32).astype(jnp.bfloat16)


def doubled(weight):
    zero = jnp.zeros_like(weight)
    return jnp.concatenate(
        [jnp.concatenate([weight, zero], axis=1), jnp.concatenate([zero, weight], axis=1)], axis=0
    )


def outgoing_kernel(dims, shared_hbm, z_hbm, outgoing_ref, shared_ref, z_ref, listed, arrived):
    days, blocks, size, probes = dims
    count = outgoing_ref.shape[0]
    parts = arrived.shape[0]
    part = days // parts
    copies = [
        pltpu.make_async_copy(z_hbm.at[pl.ds(i * part, part)], z_ref.at[pl.ds(i * part, part)], arrived.at[i])
        for i in range(parts)
    ]
    listing = pltpu.make_async_copy(shared_hbm, shared_ref, listed)
    listing.start()
    for copy in copies:
        copy.start()
    row = lax.broadcasted_iota(jnp.int32, (part, part * blocks), 0)
    column = lax.broadcasted_iota(jnp.int32, (part, part * blocks), 1)
    move = permutation(size, probes, 0, 2 * LANES)
    listing.wait()
    picks = [(column == row * blocks + shared_ref[0, m]).astype(jnp.float32) for m in range(count)]
    picks = jnp.concatenate(picks, axis=0).astype(jnp.bfloat16)
    picked = []
    for i, copy in enumerate(copies):
        copy.wait()
        z = z_ref[pl.ds(i * part, part)].reshape(part * blocks, size * probes)
        picked.append(jnp.dot(picks, z, preferred_element_type=jnp.float32))
    picked = jnp.concatenate([rows[m * part : (m + 1) * part] for m in range(count) for rows in picked], axis=0)
    step = 2 * LANES
    shift = step // size
    ranges = size * probes // step
    shifted = [picked] + [pltpu.roll(picked, size * probes - i * shift, 1) for i in range(1, ranges)]
    shifted = jnp.concatenate(shifted, axis=0).astype(jnp.bfloat16)
    moved = jnp.dot(shifted, move, preferred_element_type=jnp.float32)
    moved = moved.astype(jnp.bfloat16)
    for pair in range(size * probes // LANES):
        for m in range(count):
            row, lane = (pair // 2 * count + m) * days, pair % 2 * LANES
            outgoing_ref[m, pl.ds(pair * days, days), :] = moved[row : row + days, lane : lane + LANES]


def turn_kernel(dims, z_ref, moved_ref, turned_ref, stage):
    days, blocks, size, probes = dims
    pairs = size * probes // LANES
    z = z_ref[...].reshape(days * blocks, size * probes)
    step = 2 * LANES
    for start in range(0, size * probes, step):
        moved = jnp.dot(z, permutation(size, probes, start, step), preferred_element_type=jnp.float32)
        for half in range(2):
            pair = start // LANES + half
            tile = moved[:, half * LANES : (half + 1) * LANES]
            stage[pair] = tile
            moved_ref[pair] = tile.astype(jnp.bfloat16)
    for block in range(blocks):
        for pair in range(pairs):
            rows = stage[pair, pl.ds(block, days, stride=blocks), :]
            turned_ref[block, pl.ds(pair * days, days), :] = rows.astype(jnp.bfloat16)


def local_kernel(
    dims, links_ref, days_ref, turned_ref, weight_ref, remote_weight_ref, inverse_ref, retention_ref,
    running_ref, retain_ref, product_ref, remote_doubled_ref, inverse_doubled_ref, through_ref, beyond_ref, stage,
):
    days, blocks, size, probes = dims
    count = links_ref.shape[0]
    for block in range(blocks):
        near = jnp.concatenate([turned_ref[links_ref[k, block]] for k in range(count)], axis=1)
        weight = jnp.concatenate([doubled(weight_ref[block, k]) for k in range(count)], axis=1)
        total = lax.dot_general(near, weight, TURNED, preferred_element_type=jnp.float32)
        running_ref[block] = turned_ref[block].astype(jnp.float32) - total
        remote_doubled_ref[block] = jnp.concatenate(
            [doubled(remote_weight_ref[block, k]) for k in range(remote_weight_ref.shape[1])], axis=1
        )
        inverse_doubled_ref[block] = doubled(inverse_ref[block])
    observed = days_ref[0]
    shape = (days, LANES)
    first = lax.broadcasted_iota(jnp.int32, shape, 1) < size
    seen = lax.broadcasted_iota(jnp.int32, shape, 0) < observed
    for block in range(0, blocks, 2):
        factor = jnp.where(seen, retention_ref[:, pl.ds(block * size, LANES)], 1.0)
        other = pltpu.roll(factor, size, 1)
        retain_ref[pl.ds(block, days, stride=blocks), :] = jnp.where(first, factor, other)
        retain_ref[pl.ds(block + 1, days, stride=blocks), :] = jnp.where(first, other, factor)
    product = jnp.ones((blocks, LANES), jnp.float32)
    for day in range(days):
        rows = pl.ds(day * blocks, blocks)
        product = product * retain_ref[rows, :]
        stage[0, rows, :] = product
    after = jnp.ones((blocks, LANES), jnp.float32)
    for day in reversed(range(days)):
        rows = pl.ds(day * blocks, blocks)
        stage[1, rows, :] = after
        after = after * retain_ref[rows, :]
    for block in range(blocks):
        through_ref[block] = stage[0, pl.ds(block, days, stride=blocks), :]
        beyond_ref[block] = stage[1, pl.ds(block, days, stride=blocks), :]
    high = product.astype(jnp.bfloat16).astype(jnp.float32)
    half = lax.broadcasted_iota(jnp.int32, product.shape, 1) < size
    product_ref[...] = jnp.where(half, high, product - high).astype(jnp.bfloat16)


def pass_kernel(*refs):
    *piece_refs, product_ref, out_ref = refs
    count = piece_refs[0].shape[0]
    for k, ref in enumerate(piece_refs):
        out_ref[pl.ds(k * count, count)] = ref[...]


def forward_kernel(
    dims, batches, links_ref, days_ref, running_ref, weight_ref, inverse_ref, beyond_ref, product_ref, *rest
):
    days, blocks, size, probes = dims
    piece_refs = rest[-5 - 2 * len(batches) : -5]
    forcing_ref, message_ref, remote, source, ends = rest[-5:]
    pairs = forcing_ref.shape[0]
    count = links_ref.shape[0]
    held = remote.shape[0] // 2
    bound = piece_refs[0].shape[0] // len(batches[0])
    me = lax.axis_index("space")
    for core in range(2):
        for ref, batch in zip(piece_refs[core * len(batches) :], batches):
            for place, bits in enumerate(batch):
                if bits not in batch[:place]:
                    remote[pl.ds(core * held + bits // 2 * bound, bound)] = ref[pl.ds(place * bound, bound)]
    seen = lax.broadcasted_iota(jnp.int32, (days, LANES), 0) < days_ref[0]
    for block in range(blocks):
        places = []
        for k in range(count):
            link = links_ref[k, block]
            distance = (link // bound) ^ me
            places.append((distance % 2) * held + (distance // 2) * bound + link % bound)
        far = jnp.concatenate([remote[place] for place in places], axis=1)
        total = lax.dot_general(far, weight_ref[block], TURNED, preferred_element_type=jnp.float32)
        source[block] = (running_ref[block] - total).astype(jnp.bfloat16)
    for block in range(blocks):
        drive = lax.dot_general(source[block], inverse_ref[block], TURNED, preferred_element_type=jnp.float32)
        beyond = beyond_ref[block]
        for pair in range(pairs):
            tile = jnp.where(seen, drive[pair * days : (pair + 1) * days], 0.0)
            forcing_ref[pair, pl.ds(block, days, stride=blocks), :] = tile
            ends[pair, pl.ds(block, 1), :] = jnp.sum(beyond * tile, axis=0, keepdims=True)
    leave(message_ref, [ends[pair] for pair in range(pairs)])
    message_ref[pairs] = product_ref[...]


def leave(message_ref, values):
    for pair, value in enumerate(values):
        message_ref[pair] = value.astype(jnp.bfloat16)


def collect(piece_refs, inbox):
    me = lax.axis_index("tm")
    for k, ref in enumerate(piece_refs):
        inbox[me ^ (k + 1)] = ref[...]


def carried(pairs, inbox, products, backward):
    me, count = lax.axis_index("tm"), inbox.shape[0]
    carries = [jnp.zeros(inbox.shape[2:], jnp.float32)] * pairs
    for slab in range(count - 1, 0, -1) if backward else range(count - 1):
        valid = slab > me if backward else slab < me
        terms = products[slab, pairs].astype(jnp.float32)
        factor = terms + pltpu.roll(terms, LANES // 2, 1)
        for pair in range(pairs):
            update = inbox[slab, pair].astype(jnp.float32) + factor * carries[pair]
            carries[pair] = jnp.where(valid, update, carries[pair])
    return carries


def states_kernel(dims, forcing_ref, retain_ref, states_ref, stage):
    days, blocks, size, probes = dims
    pairs = forcing_ref.shape[0]
    states = [jnp.zeros((blocks, LANES), jnp.float32)] * pairs
    for day in range(days):
        rows = pl.ds(day * blocks, blocks)
        factor = retain_ref[rows, :]
        for pair in range(pairs):
            states[pair] = factor * states[pair] + forcing_ref[pair, rows, :]
            stage[pair, rows, :] = states[pair]
    for block in range(blocks):
        for pair in range(pairs):
            states_ref[block, pl.ds(pair * days, days), :] = stage[pair, pl.ds(block, days, stride=blocks), :]


def adjoint_kernel(dims, hops, days_ref, states_ref, through_ref, inverse_ref, *rest):
    days, blocks, size, probes = dims
    adjoint_ref, message_ref, inbox, enter, starts = rest[hops:]
    pairs = adjoint_ref.shape[0]
    collect(rest[:hops], inbox)
    seen = lax.broadcasted_iota(jnp.int32, (days, LANES), 0) < days_ref[0]
    for pair, carry in enumerate(carried(pairs, inbox, inbox, False)):
        enter[pair] = carry
    for block in range(blocks):
        through = through_ref[block]
        stored = [
            (states_ref[block, pl.ds(pair * days, days), :] + through * enter[pair, pl.ds(block, 1), :])
            .astype(jnp.bfloat16)
            for pair in range(pairs)
        ]
        adjoint = jnp.dot(jnp.concatenate(stored, axis=0), inverse_ref[block], preferred_element_type=jnp.float32)
        for pair in range(pairs):
            tile = jnp.where(seen, adjoint[pair * days : (pair + 1) * days], 0.0)
            adjoint_ref[pair, pl.ds(block, days, stride=blocks), :] = tile
            starts[pair, pl.ds(block, 1), :] = jnp.sum(through * tile, axis=0, keepdims=True)
    leave(message_ref, [starts[pair] for pair in range(pairs)])


def own_kernel(dims, adjoint_ref, retain_ref, moved_ref, partial_ref):
    days, blocks, size, probes = dims
    pairs = adjoint_ref.shape[0]
    carries = [jnp.zeros((blocks, LANES), jnp.float32)] * pairs
    for day in reversed(range(days)):
        rows = pl.ds(day * blocks, blocks)
        factor = retain_ref[rows, :]
        total = None
        for pair in range(pairs):
            smoothed = adjoint_ref[pair, rows, :] + carries[pair]
            carries[pair] = factor * smoothed
            term = smoothed * moved_ref[pair, rows, :].astype(jnp.float32)
            total = term if total is None else total + term
        partial_ref[rows, :] = total


def variance_kernel(dims, hops, partial_ref, retain_ref, moved_ref, *rest):
    days, blocks, size, probes = dims
    pairs = moved_ref.shape[0]
    out_hbm, stage, inbox, products, out_ref, left = rest[2 * hops :]
    collect(rest[:hops], inbox)
    collect(rest[hops : 2 * hops], products)
    carries = carried(pairs, inbox, products, True)
    reach = jnp.ones((blocks, LANES), jnp.float32)
    parts = left.shape[0]
    part = days // parts
    lane = lax.broadcasted_iota(jnp.int32, (part, LANES), 1)
    copies = []
    for first in reversed(range(0, days, part)):
        for day in reversed(range(first, first + part)):
            rows = pl.ds(day * blocks, blocks)
            total = None
            for pair in range(pairs):
                term = carries[pair] * moved_ref[pair, rows, :].astype(jnp.float32)
                total = term if total is None else total + term
            stage[rows, :] = partial_ref[rows, :] + reach * total
            reach = reach * retain_ref[rows, :]
        done = pl.ds(first, part)
        for block in range(0, blocks, 2):
            both = [stage[pl.ds(first * blocks + block + half, part, stride=blocks), :] for half in range(2)]
            both = [value + pltpu.roll(value, size, 1) for value in both]
            out_ref[done, pl.ds(block * size, LANES)] = jnp.where(lane < size, both[0], both[1]) * (1.0 / probes)
        copies.append(pltpu.make_async_copy(out_ref.at[done], out_hbm.at[done], left.at[len(copies)]))
        copies[-1].start()
    for copy in copies:
        copy.wait()


def call(kernel, outs, scratch, flops, moved, scalars, *operands, apart=(), limit=VMEM_LIMIT, out_space=pltpu.VMEM):
    in_specs = [
        pl.BlockSpec(memory_space=pltpu.SMEM if i < scalars else pl.ANY if i in apart else pltpu.VMEM)
        for i in range(len(operands))
    ]
    return pl.pallas_call(
        kernel,
        out_shape=[jax.ShapeDtypeStruct(shape, kind) for shape, kind in outs],
        in_specs=in_specs,
        out_specs=[pl.BlockSpec(memory_space=out_space) for _ in outs],
        scratch_shapes=scratch,
        compiler_params=pltpu.CompilerParams(vmem_limit_bytes=limit),
        cost_estimate=pl.CostEstimate(flops=flops, bytes_accessed=moved, transcendentals=0),
    )(*operands)


def crossed(block, axis, bits):
    return lax.ppermute(block, axis, [(i, i ^ bits) for i in range(lax.axis_size(axis))])


def local(
    probes,
    local_links,
    remote_links,
    shared_blocks,
    slab_days,
    local_coupling,
    remote_coupling,
    block_inverse,
    retention,
):
    days, blocks, width = probes.shape
    size = block_inverse.shape[1]
    dims = (days, blocks, size, width // size)
    pairs = width // LANES
    f32, bf16 = jnp.float32, jnp.bfloat16
    bound = shared_blocks.shape[1]
    far = remote_links.shape[1]
    rows = days * blocks
    groups = lax.axis_size("space")
    held = groups // 2 * bound
    near_table, far_table = local_links.T, remote_links.T
    big = ((pairs, rows, LANES), f32)

    (outgoing,) = call(
        functools.partial(outgoing_kernel, dims),
        [((bound, pairs * days, LANES), bf16)],
        [
            pltpu.SMEM(shared_blocks.shape, jnp.int32),
            pltpu.VMEM(probes.shape, bf16),
            pltpu.SemaphoreType.DMA,
            pltpu.SemaphoreType.DMA((2,)),
        ],
        10**9, 4 * 10**6, 0, shared_blocks, probes, apart=(0, 1), limit=63 * 1024 * 1024,
    )
    pieces = {bits: crossed(outgoing, "space", bits) for bits in range(groups - 2, 0, -2)}
    by_block = (blocks, pairs * days, LANES)
    moved, turned = call(
        functools.partial(turn_kernel, dims),
        [((pairs, rows, LANES), bf16), (by_block, bf16)],
        [pltpu.VMEM(*big)], 10**10, 10**7, 0, probes,
    )
    running, retain, product, remote_weight, inverse, through, beyond = call(
        functools.partial(local_kernel, dims),
        [
            (by_block, f32),
            ((rows, LANES), f32),
            ((blocks, LANES), bf16),
            ((blocks, LANES, far * LANES), bf16),
            ((blocks, LANES, LANES), bf16),
            ((blocks, days, LANES), f32),
            ((blocks, days, LANES), f32),
        ],
        [pltpu.VMEM((2, rows, LANES), f32)], 10**10, 10**7, 2,
        near_table, slab_days, turned, local_coupling, remote_coupling, block_inverse, retention,
    )
    pieces[0] = outgoing
    batches = [0, groups - 2, groups - 2], list(range(groups - 4, 0, -2))
    same = []
    for batch in batches:
        shape = (len(batch) * bound, pairs * days, LANES)
        same += call(pass_kernel, [(shape, bf16)], [], 0, 10**5, 0, *[pieces[bits] for bits in batch], product)
    other = [crossed(piece, "space", 1) for piece in same]
    raw = [pieces[bits] for bits in range(2, groups, 2)]
    slabs = lax.axis_size("tm")
    hops = slabs - 1
    exchange = lambda message: [crossed(message, "tm", bits) for bits in range(hops, 0, -1)][::-1]
    inbox = pltpu.VMEM((slabs, pairs + 1, blocks, LANES), bf16)
    values = pltpu.VMEM((pairs, blocks, LANES), f32)
    forcing, message = call(
        functools.partial(forward_kernel, dims, batches),
        [big, ((pairs + 1, blocks, LANES), bf16)],
        [pltpu.VMEM((2 * held, pairs * days, LANES), bf16), pltpu.VMEM(by_block, bf16), values], 10**10, 10**7, 2,
        far_table, slab_days, running, remote_weight, inverse, beyond, product, *raw, *same, *other,
        apart=range(7, 7 + len(raw)),
    )
    ends = exchange(message)
    (states,) = call(
        functools.partial(states_kernel, dims), [(by_block, f32)], [pltpu.VMEM(*big)], 10**9, 10**6, 0, forcing, retain
    )
    adjoint, message = call(
        functools.partial(adjoint_kernel, dims, hops),
        [big, ((pairs, blocks, LANES), bf16)],
        [inbox, values, values], 10**10, 10**7, 1, slab_days, states, through, inverse, *ends,
    )
    starts = exchange(message)
    (partial,) = call(
        functools.partial(own_kernel, dims), [((rows, LANES), f32)], [], 10**9, 10**6, 0, adjoint, retain, moved
    )
    (variance,) = call(
        functools.partial(variance_kernel, dims, hops),
        [((days, blocks * size), f32)],
        [
            pltpu.VMEM((rows, LANES), f32),
            pltpu.VMEM((slabs, pairs, blocks, LANES), bf16),
            inbox,
            pltpu.VMEM((days, blocks * size), f32),
            pltpu.SemaphoreType.DMA((2,)),
        ],
        10**10, 10**7, 0, partial, retain, moved, *starts, *ends, out_space=pl.ANY,
    )
    return variance


def solution(mesh):
    placed = (
        P("tm", "space", None),
        P("space", None),
        P("space", None),
        P("space", None),
        P("tm"),
        P("space", None, None, None),
        P("space", None, None, None),
        P("space", None, None),
        P("tm", "space"),
    )
    return jax.shard_map(
        local, mesh=mesh, in_specs=placed, out_specs=P("tm", "space"), check_vma=False
    )
```

```python
import functools

import jax
import jax.numpy as jnp
from jax import lax
from jax.experimental import pallas as pl
from jax.experimental.pallas import tpu as pltpu
from jax.sharding import PartitionSpec as P

LANES = 128
VMEM_LIMIT = 20 * 1024 * 1024
TURNED = (((1,), (1,)), ((), ()))


def permutation(size, probes, start, width):
    total = size * probes
    column = lax.broadcasted_iota(jnp.int32, (total, width), 1) + start
    origin = (column % size) * probes + column // size
    row = lax.broadcasted_iota(jnp.int32, (total, width), 0)
    return (row == origin).astype(jnp.float32).astype(jnp.bfloat16)


def doubled(weight):
    zero = jnp.zeros_like(weight)
    return jnp.concatenate(
        [jnp.concatenate([weight, zero], axis=1), jnp.concatenate([zero, weight], axis=1)], axis=0
    )


def outgoing_kernel(dims, shared_hbm, z_hbm, outgoing_ref, shared_ref, z_ref, listed, arrived):
    days, blocks, size, probes = dims
    count = outgoing_ref.shape[0]
    parts = arrived.shape[0]
    part = days // parts
    copies = [
        pltpu.make_async_copy(z_hbm.at[pl.ds(i * part, part)], z_ref.at[pl.ds(i * part, part)], arrived.at[i])
        for i in range(parts)
    ]
    listing = pltpu.make_async_copy(shared_hbm, shared_ref, listed)
    listing.start()
    for copy in copies:
        copy.start()
    row = lax.broadcasted_iota(jnp.int32, (part, part * blocks), 0)
    column = lax.broadcasted_iota(jnp.int32, (part, part * blocks), 1)
    move = permutation(size, probes, 0, 2 * LANES)
    listing.wait()
    picks = [(column == row * blocks + shared_ref[0, m]).astype(jnp.float32) for m in range(count)]
    picks = jnp.concatenate(picks, axis=0).astype(jnp.bfloat16)
    picked = []
    for i, copy in enumerate(copies):
        copy.wait()
        z = z_ref[pl.ds(i * part, part)].reshape(part * blocks, size * probes)
        picked.append(jnp.dot(picks, z, preferred_element_type=jnp.float32))
    picked = jnp.concatenate([rows[m * part : (m + 1) * part] for m in range(count) for rows in picked], axis=0)
    step = 2 * LANES
    shift = step // size
    ranges = size * probes // step
    shifted = [picked] + [pltpu.roll(picked, size * probes - i * shift, 1) for i in range(1, ranges)]
    shifted = jnp.concatenate(shifted, axis=0).astype(jnp.bfloat16)
    moved = jnp.dot(shifted, move, preferred_element_type=jnp.float32)
    moved = moved.astype(jnp.bfloat16)
    for pair in range(size * probes // LANES):
        for m in range(count):
            row, lane = (pair // 2 * count + m) * days, pair % 2 * LANES
            outgoing_ref[m, pl.ds(pair * days, days), :] = moved[row : row + days, lane : lane + LANES]


def turn_kernel(dims, z_ref, moved_ref, turned_ref, stage):
    days, blocks, size, probes = dims
    pairs = size * probes // LANES
    z = z_ref[...].reshape(days * blocks, size * probes)
    step = 2 * LANES
    for start in range(0, size * probes, step):
        moved = jnp.dot(z, permutation(size, probes, start, step), preferred_element_type=jnp.float32)
        for half in range(2):
            pair = start // LANES + half
            tile = moved[:, half * LANES : (half + 1) * LANES]
            stage[pair] = tile
            moved_ref[pair] = tile.astype(jnp.bfloat16)
    for block in range(blocks):
        for pair in range(pairs):
            rows = stage[pair, pl.ds(block, days, stride=blocks), :]
            turned_ref[block, pl.ds(pair * days, days), :] = rows.astype(jnp.bfloat16)


def local_kernel(
    dims, links_ref, turned_ref, weight_ref, remote_weight_ref, inverse_ref,
    running_ref, remote_doubled_ref, inverse_doubled_ref,
):
    days, blocks, size, probes = dims
    count = links_ref.shape[0]
    for block in range(blocks):
        near = jnp.concatenate([turned_ref[links_ref[k, block]] for k in range(count)], axis=1)
        weight = jnp.concatenate([doubled(weight_ref[block, k]) for k in range(count)], axis=1)
        total = lax.dot_general(near, weight, TURNED, preferred_element_type=jnp.float32)
        running_ref[block] = turned_ref[block].astype(jnp.float32) - total
        remote_doubled_ref[block] = jnp.concatenate(
            [doubled(remote_weight_ref[block, k]) for k in range(remote_weight_ref.shape[1])], axis=1
        )
        inverse_doubled_ref[block] = doubled(inverse_ref[block])


def retain_kernel(
    dims, days_ref, retention_ref, retain_ref, product_ref, through_ref, beyond_ref, active_ref, stage
):
    days, blocks, size, probes = dims
    observed = days_ref[0]
    shape = (days, LANES)
    first = lax.broadcasted_iota(jnp.int32, shape, 1) < size
    seen = lax.broadcasted_iota(jnp.int32, shape, 0) < observed
    active_ref[...] = jnp.where(seen, 1.0, 0.0)
    for block in range(0, blocks, 2):
        factor = jnp.where(seen, retention_ref[:, pl.ds(block * size, LANES)], 1.0)
        other = pltpu.roll(factor, size, 1)
        retain_ref[pl.ds(block, days, stride=blocks), :] = jnp.where(first, factor, other)
        retain_ref[pl.ds(block + 1, days, stride=blocks), :] = jnp.where(first, other, factor)
    product = jnp.ones((blocks, LANES), jnp.float32)
    for day in range(days):
        rows = pl.ds(day * blocks, blocks)
        product = product * retain_ref[rows, :]
        stage[0, rows, :] = product
    after = jnp.ones((blocks, LANES), jnp.float32)
    for day in reversed(range(days)):
        rows = pl.ds(day * blocks, blocks)
        stage[1, rows, :] = after
        after = after * retain_ref[rows, :]
    for block in range(blocks):
        through_ref[block] = stage[0, pl.ds(block, days, stride=blocks), :]
        beyond_ref[block] = stage[1, pl.ds(block, days, stride=blocks), :]
    high = product.astype(jnp.bfloat16).astype(jnp.float32)
    half = lax.broadcasted_iota(jnp.int32, product.shape, 1) < size
    product_ref[...] = jnp.where(half, high, product - high).astype(jnp.bfloat16)


def pass_kernel(*refs):
    *piece_refs, before_ref, out_ref = refs
    count = piece_refs[0].shape[0]
    for k, ref in enumerate(piece_refs):
        out_ref[pl.ds(k * count, count)] = ref[...]


def forward_kernel(
    dims, batches, links_ref, active_ref, running_ref, weight_ref, inverse_ref, beyond_ref, product_ref, *rest
):
    days, blocks, size, probes = dims
    piece_refs = rest[-5 - 2 * len(batches) : -5]
    forcing_ref, message_ref, remote, source, ends = rest[-5:]
    pairs = forcing_ref.shape[0]
    count = links_ref.shape[0]
    held = remote.shape[0] // 2
    bound = piece_refs[0].shape[0] // len(batches[0])
    me = lax.axis_index("space")
    for core in range(2):
        for ref, batch in zip(piece_refs[core * len(batches) :], batches):
            for place, bits in enumerate(batch):
                if bits not in batch[:place]:
                    remote[pl.ds(core * held + bits // 2 * bound, bound)] = ref[pl.ds(place * bound, bound)]
    active = active_ref[...]
    for block in range(blocks):
        places = []
        for k in range(count):
            link = links_ref[k, block]
            distance = (link // bound) ^ me
            places.append((distance % 2) * held + (distance // 2) * bound + link % bound)
        far = jnp.concatenate([remote[place] for place in places], axis=1)
        total = lax.dot_general(far, weight_ref[block], TURNED, preferred_element_type=jnp.float32)
        source[block] = (running_ref[block] - total).astype(jnp.bfloat16)
    for block in range(blocks):
        drive = lax.dot_general(source[block], inverse_ref[block], TURNED, preferred_element_type=jnp.float32)
        beyond = beyond_ref[block]
        for pair in range(pairs):
            tile = active * drive[pair * days : (pair + 1) * days]
            forcing_ref[pair, pl.ds(block, days, stride=blocks), :] = tile
            ends[pair, pl.ds(block, 1), :] = jnp.sum(beyond * tile, axis=0, keepdims=True)
    leave(message_ref, [ends[pair] for pair in range(pairs)])
    message_ref[pairs] = product_ref[...]


def leave(message_ref, values):
    for pair, value in enumerate(values):
        message_ref[pair] = value.astype(jnp.bfloat16)


def collect(piece_refs, inbox):
    me = lax.axis_index("tm")
    for k, ref in enumerate(piece_refs):
        inbox[me ^ (k + 1)] = ref[...]


def carried(pairs, inbox, products, backward):
    me, count = lax.axis_index("tm"), inbox.shape[0]
    carries = [jnp.zeros(inbox.shape[2:], jnp.float32)] * pairs
    for slab in range(count - 1, 0, -1) if backward else range(count - 1):
        valid = slab > me if backward else slab < me
        terms = products[slab, pairs].astype(jnp.float32)
        factor = terms + pltpu.roll(terms, LANES // 2, 1)
        for pair in range(pairs):
            update = inbox[slab, pair].astype(jnp.float32) + factor * carries[pair]
            carries[pair] = jnp.where(valid, update, carries[pair])
    return carries


def states_kernel(dims, forcing_ref, retain_ref, states_ref, stage):
    days, blocks, size, probes = dims
    pairs = forcing_ref.shape[0]
    states = [jnp.zeros((blocks, LANES), jnp.float32)] * pairs
    for day in range(days):
        rows = pl.ds(day * blocks, blocks)
        factor = retain_ref[rows, :]
        for pair in range(pairs):
            states[pair] = factor * states[pair] + forcing_ref[pair, rows, :]
            stage[pair, rows, :] = states[pair]
    for block in range(blocks):
        for pair in range(pairs):
            states_ref[block, pl.ds(pair * days, days), :] = stage[pair, pl.ds(block, days, stride=blocks), :]


def adjoint_kernel(dims, hops, active_ref, states_ref, through_ref, inverse_ref, *rest):
    days, blocks, size, probes = dims
    adjoint_ref, message_ref, inbox, enter, starts = rest[hops:]
    pairs = adjoint_ref.shape[0]
    collect(rest[:hops], inbox)
    active = active_ref[...]
    for pair, carry in enumerate(carried(pairs, inbox, inbox, False)):
        enter[pair] = carry
    for block in range(blocks):
        through = through_ref[block]
        stored = [
            (states_ref[block, pl.ds(pair * days, days), :] + through * enter[pair, pl.ds(block, 1), :])
            .astype(jnp.bfloat16)
            for pair in range(pairs)
        ]
        adjoint = jnp.dot(jnp.concatenate(stored, axis=0), inverse_ref[block], preferred_element_type=jnp.float32)
        for pair in range(pairs):
            tile = active * adjoint[pair * days : (pair + 1) * days]
            adjoint_ref[pair, pl.ds(block, days, stride=blocks), :] = tile
            starts[pair, pl.ds(block, 1), :] = jnp.sum(through * tile, axis=0, keepdims=True)
    leave(message_ref, [starts[pair] for pair in range(pairs)])


def own_kernel(dims, adjoint_ref, retain_ref, moved_ref, partial_ref):
    days, blocks, size, probes = dims
    pairs = adjoint_ref.shape[0]
    carries = [jnp.zeros((blocks, LANES), jnp.float32)] * pairs
    for day in reversed(range(days)):
        rows = pl.ds(day * blocks, blocks)
        factor = retain_ref[rows, :]
        total = None
        for pair in range(pairs):
            smoothed = adjoint_ref[pair, rows, :] + carries[pair]
            carries[pair] = factor * smoothed
            term = smoothed * moved_ref[pair, rows, :].astype(jnp.float32)
            total = term if total is None else total + term
        partial_ref[rows, :] = total


def variance_kernel(dims, hops, partial_ref, retain_ref, moved_ref, *rest):
    days, blocks, size, probes = dims
    pairs = moved_ref.shape[0]
    out_hbm, stage, inbox, products, out_ref, left = rest[2 * hops :]
    collect(rest[:hops], inbox)
    collect(rest[hops : 2 * hops], products)
    carries = carried(pairs, inbox, products, True)
    reach = jnp.ones((blocks, LANES), jnp.float32)
    parts = left.shape[0]
    part = days // parts
    lane = lax.broadcasted_iota(jnp.int32, (part, LANES), 1)
    copies = []
    for first in reversed(range(0, days, part)):
        for day in reversed(range(first, first + part)):
            rows = pl.ds(day * blocks, blocks)
            total = None
            for pair in range(pairs):
                term = carries[pair] * moved_ref[pair, rows, :].astype(jnp.float32)
                total = term if total is None else total + term
            stage[rows, :] = partial_ref[rows, :] + reach * total
            reach = reach * retain_ref[rows, :]
        done = pl.ds(first, part)
        for block in range(0, blocks, 2):
            both = [stage[pl.ds(first * blocks + block + half, part, stride=blocks), :] for half in range(2)]
            both = [value + pltpu.roll(value, size, 1) for value in both]
            out_ref[done, pl.ds(block * size, LANES)] = jnp.where(lane < size, both[0], both[1]) * (1.0 / probes)
        copies.append(pltpu.make_async_copy(out_ref.at[done], out_hbm.at[done], left.at[len(copies)]))
        copies[-1].start()
    for copy in copies:
        copy.wait()


def call(kernel, outs, scratch, flops, moved, scalars, *operands, apart=(), limit=VMEM_LIMIT, out_space=pltpu.VMEM):
    in_specs = [
        pl.BlockSpec(memory_space=pltpu.SMEM if i < scalars else pl.ANY if i in apart else pltpu.VMEM)
        for i in range(len(operands))
    ]
    return pl.pallas_call(
        kernel,
        out_shape=[jax.ShapeDtypeStruct(shape, kind) for shape, kind in outs],
        in_specs=in_specs,
        out_specs=[pl.BlockSpec(memory_space=out_space) for _ in outs],
        scratch_shapes=scratch,
        compiler_params=pltpu.CompilerParams(vmem_limit_bytes=limit),
        cost_estimate=pl.CostEstimate(flops=flops, bytes_accessed=moved, transcendentals=0),
    )(*operands)


def crossed(block, axis, bits):
    return lax.ppermute(block, axis, [(i, i ^ bits) for i in range(lax.axis_size(axis))])


def local(
    probes,
    local_links,
    remote_links,
    shared_blocks,
    slab_days,
    local_coupling,
    remote_coupling,
    block_inverse,
    retention,
):
    days, blocks, width = probes.shape
    size = block_inverse.shape[1]
    dims = (days, blocks, size, width // size)
    pairs = width // LANES
    f32, bf16 = jnp.float32, jnp.bfloat16
    bound = shared_blocks.shape[1]
    far = remote_links.shape[1]
    rows = days * blocks
    groups = lax.axis_size("space")
    held = groups // 2 * bound
    near_table, far_table = local_links.T, remote_links.T
    big = ((pairs, rows, LANES), f32)

    (outgoing,) = call(
        functools.partial(outgoing_kernel, dims),
        [((bound, pairs * days, LANES), bf16)],
        [
            pltpu.SMEM(shared_blocks.shape, jnp.int32),
            pltpu.VMEM(probes.shape, bf16),
            pltpu.SemaphoreType.DMA,
            pltpu.SemaphoreType.DMA((2,)),
        ],
        10**9, 4 * 10**6, 0, shared_blocks, probes, apart=(0, 1), limit=63 * 1024 * 1024,
    )
    pieces = {bits: crossed(outgoing, "space", bits) for bits in range(groups - 2, 0, -2)}
    by_block = (blocks, pairs * days, LANES)
    moved, turned = call(
        functools.partial(turn_kernel, dims),
        [((pairs, rows, LANES), bf16), (by_block, bf16)],
        [pltpu.VMEM(*big)], 10**10, 10**7, 0, probes,
    )
    running, remote_weight, inverse = call(
        functools.partial(local_kernel, dims),
        [(by_block, f32), ((blocks, LANES, far * LANES), bf16), ((blocks, LANES, LANES), bf16)],
        [], 10**10, 10**7, 1, near_table, turned, local_coupling, remote_coupling, block_inverse,
    )
    retain, product, through, beyond, active = call(
        functools.partial(retain_kernel, dims),
        [
            ((rows, LANES), f32),
            ((blocks, LANES), bf16),
            ((blocks, days, LANES), f32),
            ((blocks, days, LANES), f32),
            ((days, LANES), f32),
        ],
        [pltpu.VMEM((2, rows, LANES), f32)], 10**6, 10**5, 1, slab_days, retention,
    )
    pieces[0] = outgoing
    batches = [0, groups - 2, groups - 2], list(range(groups - 4, 0, -2))
    same = []
    for batch in batches:
        shape = (len(batch) * bound, pairs * days, LANES)
        same += call(pass_kernel, [(shape, bf16)], [], 0, 10**5, 0, *[pieces[bits] for bits in batch], inverse)
    other = [crossed(piece, "space", 1) for piece in same]
    raw = [pieces[bits] for bits in range(2, groups, 2)]
    slabs = lax.axis_size("tm")
    hops = slabs - 1
    exchange = lambda message: [crossed(message, "tm", bits) for bits in range(hops, 0, -1)][::-1]
    inbox = pltpu.VMEM((slabs, pairs + 1, blocks, LANES), bf16)
    values = pltpu.VMEM((pairs, blocks, LANES), f32)
    forcing, message = call(
        functools.partial(forward_kernel, dims, batches),
        [big, ((pairs + 1, blocks, LANES), bf16)],
        [pltpu.VMEM((2 * held, pairs * days, LANES), bf16), pltpu.VMEM(by_block, bf16), values], 10**10, 10**7, 1,
        far_table, active, running, remote_weight, inverse, beyond, product, *raw, *same, *other,
        apart=range(7, 7 + len(raw)),
    )
    ends = exchange(message)
    (states,) = call(
        functools.partial(states_kernel, dims), [(by_block, f32)], [pltpu.VMEM(*big)], 10**9, 10**6, 0, forcing, retain
    )
    adjoint, message = call(
        functools.partial(adjoint_kernel, dims, hops),
        [big, ((pairs, blocks, LANES), bf16)],
        [inbox, values, values], 10**10, 10**7, 0, active, states, through, inverse, *ends,
    )
    starts = exchange(message)
    (partial,) = call(
        functools.partial(own_kernel, dims), [((rows, LANES), f32)], [], 10**9, 10**6, 0, adjoint, retain, moved
    )
    (variance,) = call(
        functools.partial(variance_kernel, dims, hops),
        [((days, blocks * size), f32)],
        [
            pltpu.VMEM((rows, LANES), f32),
            pltpu.VMEM((slabs, pairs, blocks, LANES), bf16),
            inbox,
            pltpu.VMEM((days, blocks * size), f32),
            pltpu.SemaphoreType.DMA((2,)),
        ],
        10**10, 10**7, 0, partial, retain, moved, *starts, *ends, out_space=pl.ANY,
    )
    return variance


def solution(mesh):
    placed = (
        P("tm", "space", None),
        P("space", None),
        P("space", None),
        P("space", None),
        P("tm"),
        P("space", None, None, None),
        P("space", None, None, None),
        P("space", None, None),
        P("tm", "space"),
    )
    return jax.shard_map(
        local, mesh=mesh, in_specs=placed, out_specs=P("tm", "space"), check_vma=False
    )
```

```python
import functools

import jax
import jax.numpy as jnp
from jax import lax
from jax.experimental import pallas as pl
from jax.experimental.pallas import tpu as pltpu
from jax.sharding import PartitionSpec as P

LANES = 128
VMEM_LIMIT = 20 * 1024 * 1024
TURNED = (((1,), (1,)), ((), ()))


def permutation(size, probes, start, width):
    total = size * probes
    column = lax.broadcasted_iota(jnp.int32, (total, width), 1) + start
    origin = (column % size) * probes + column // size
    row = lax.broadcasted_iota(jnp.int32, (total, width), 0)
    return (row == origin).astype(jnp.float32).astype(jnp.bfloat16)


def doubled(weight):
    zero = jnp.zeros_like(weight)
    return jnp.concatenate(
        [jnp.concatenate([weight, zero], axis=1), jnp.concatenate([zero, weight], axis=1)], axis=0
    )


def outgoing_kernel(dims, shared_hbm, z_hbm, outgoing_ref, shared_ref, z_ref, listed, arrived):
    days, blocks, size, probes = dims
    count = outgoing_ref.shape[0]
    parts = arrived.shape[0]
    part = days // parts
    copies = [
        pltpu.make_async_copy(z_hbm.at[pl.ds(i * part, part)], z_ref.at[pl.ds(i * part, part)], arrived.at[i])
        for i in range(parts)
    ]
    listing = pltpu.make_async_copy(shared_hbm, shared_ref, listed)
    listing.start()
    for copy in copies:
        copy.start()
    row = lax.broadcasted_iota(jnp.int32, (part, part * blocks), 0)
    column = lax.broadcasted_iota(jnp.int32, (part, part * blocks), 1)
    move = permutation(size, probes, 0, 2 * LANES)
    listing.wait()
    picks = [(column == row * blocks + shared_ref[0, m]).astype(jnp.float32) for m in range(count)]
    picks = jnp.concatenate(picks, axis=0).astype(jnp.bfloat16)
    picked = []
    for i, copy in enumerate(copies):
        copy.wait()
        z = z_ref[pl.ds(i * part, part)].reshape(part * blocks, size * probes)
        picked.append(jnp.dot(picks, z, preferred_element_type=jnp.float32))
    picked = jnp.concatenate([rows[m * part : (m + 1) * part] for m in range(count) for rows in picked], axis=0)
    step = 2 * LANES
    shift = step // size
    ranges = size * probes // step
    shifted = [picked] + [pltpu.roll(picked, size * probes - i * shift, 1) for i in range(1, ranges)]
    shifted = jnp.concatenate(shifted, axis=0).astype(jnp.bfloat16)
    moved = jnp.dot(shifted, move, preferred_element_type=jnp.float32)
    moved = moved.astype(jnp.bfloat16)
    for pair in range(size * probes // LANES):
        for m in range(count):
            row, lane = (pair // 2 * count + m) * days, pair % 2 * LANES
            outgoing_ref[m, pl.ds(pair * days, days), :] = moved[row : row + days, lane : lane + LANES]


def turn_kernel(dims, z_ref, moved_ref, turned_ref, stage):
    days, blocks, size, probes = dims
    pairs = size * probes // LANES
    z = z_ref[...].reshape(days * blocks, size * probes)
    step = 2 * LANES
    for start in range(0, size * probes, step):
        moved = jnp.dot(z, permutation(size, probes, start, step), preferred_element_type=jnp.float32)
        for half in range(2):
            pair = start // LANES + half
            tile = moved[:, half * LANES : (half + 1) * LANES]
            stage[pair] = tile
            moved_ref[pair] = tile.astype(jnp.bfloat16)
    for block in range(blocks):
        for pair in range(pairs):
            rows = stage[pair, pl.ds(block, days, stride=blocks), :]
            turned_ref[block, pl.ds(pair * days, days), :] = rows.astype(jnp.bfloat16)


def local_kernel(
    dims, links_ref, turned_ref, weight_ref, remote_weight_ref, inverse_ref,
    running_ref, remote_doubled_ref, inverse_doubled_ref,
):
    days, blocks, size, probes = dims
    count = links_ref.shape[0]
    for block in range(blocks):
        near = jnp.concatenate([turned_ref[links_ref[k, block]] for k in range(count)], axis=1)
        weight = jnp.concatenate([doubled(weight_ref[block, k]) for k in range(count)], axis=1)
        total = lax.dot_general(near, weight, TURNED, preferred_element_type=jnp.float32)
        running_ref[block] = turned_ref[block].astype(jnp.float32) - total
        remote_doubled_ref[block] = jnp.concatenate(
            [doubled(remote_weight_ref[block, k]) for k in range(remote_weight_ref.shape[1])], axis=1
        )
        inverse_doubled_ref[block] = doubled(inverse_ref[block])


def retain_kernel(
    dims, days_ref, retention_ref, retain_ref, product_ref, through_ref, beyond_ref, active_ref, stage
):
    days, blocks, size, probes = dims
    observed = days_ref[0]
    shape = (days, LANES)
    first = lax.broadcasted_iota(jnp.int32, shape, 1) < size
    seen = lax.broadcasted_iota(jnp.int32, shape, 0) < observed
    active_ref[...] = jnp.where(seen, 1.0, 0.0)
    for block in range(0, blocks, 2):
        factor = jnp.where(seen, retention_ref[:, pl.ds(block * size, LANES)], 1.0)
        other = pltpu.roll(factor, size, 1)
        retain_ref[pl.ds(block, days, stride=blocks), :] = jnp.where(first, factor, other)
        retain_ref[pl.ds(block + 1, days, stride=blocks), :] = jnp.where(first, other, factor)
    product = jnp.ones((blocks, LANES), jnp.float32)
    for day in range(days):
        rows = pl.ds(day * blocks, blocks)
        product = product * retain_ref[rows, :]
        stage[0, rows, :] = product
    after = jnp.ones((blocks, LANES), jnp.float32)
    for day in reversed(range(days)):
        rows = pl.ds(day * blocks, blocks)
        stage[1, rows, :] = after
        after = after * retain_ref[rows, :]
    for block in range(blocks):
        through_ref[block] = stage[0, pl.ds(block, days, stride=blocks), :]
        beyond_ref[block] = stage[1, pl.ds(block, days, stride=blocks), :]
    high = product.astype(jnp.bfloat16).astype(jnp.float32)
    half = lax.broadcasted_iota(jnp.int32, product.shape, 1) < size
    product_ref[...] = jnp.where(half, high, product - high).astype(jnp.bfloat16)


def pass_kernel(*refs):
    *piece_refs, before_ref, out_ref = refs
    count = piece_refs[0].shape[0]
    for k, ref in enumerate(piece_refs):
        out_ref[pl.ds(k * count, count)] = ref[...]


def forward_kernel(
    dims, batches, links_ref, active_ref, running_ref, weight_ref, inverse_ref, beyond_ref, product_ref, *rest
):
    days, blocks, size, probes = dims
    piece_refs = rest[-5 - 2 * len(batches) : -5]
    forcing_ref, message_ref, remote, source, ends = rest[-5:]
    pairs = forcing_ref.shape[0]
    count = links_ref.shape[0]
    held = remote.shape[0] // 2
    bound = piece_refs[0].shape[0] // len(batches[0])
    me = lax.axis_index("space")
    for core in range(2):
        for ref, batch in zip(piece_refs[core * len(batches) :], batches):
            for place, bits in enumerate(batch):
                if bits not in batch[:place]:
                    remote[pl.ds(core * held + bits // 2 * bound, bound)] = ref[pl.ds(place * bound, bound)]
    active = active_ref[...]
    def make_source(block, _):
        places = []
        for k in range(count):
            link = links_ref[k, block]
            distance = (link // bound) ^ me
            places.append((distance % 2) * held + (distance // 2) * bound + link % bound)
        far = jnp.concatenate([remote[place] for place in places], axis=1)
        total = lax.dot_general(far, weight_ref[block], TURNED, preferred_element_type=jnp.float32)
        source[block] = (running_ref[block] - total).astype(jnp.bfloat16)
        return _

    def make_forcing(block, _):
        drive = lax.dot_general(source[block], inverse_ref[block], TURNED, preferred_element_type=jnp.float32)
        beyond = beyond_ref[block]
        for pair in range(pairs):
            tile = active * drive[pair * days : (pair + 1) * days]
            forcing_ref[pair, pl.ds(block, days, stride=blocks), :] = tile
            ends[pair, pl.ds(block, 1), :] = jnp.sum(beyond * tile, axis=0, keepdims=True)
        return _

    lax.fori_loop(0, blocks, make_source, 0, unroll=4)
    lax.fori_loop(0, blocks, make_forcing, 0, unroll=4)
    leave(message_ref, [ends[pair] for pair in range(pairs)])
    message_ref[pairs] = product_ref[...]


def leave(message_ref, values):
    for pair, value in enumerate(values):
        message_ref[pair] = value.astype(jnp.bfloat16)


def collect(piece_refs, inbox):
    me = lax.axis_index("tm")
    for k, ref in enumerate(piece_refs):
        inbox[me ^ (k + 1)] = ref[...]


def carried(pairs, inbox, products, backward):
    me, count = lax.axis_index("tm"), inbox.shape[0]
    carries = [jnp.zeros(inbox.shape[2:], jnp.float32)] * pairs
    for slab in range(count - 1, 0, -1) if backward else range(count - 1):
        valid = slab > me if backward else slab < me
        terms = products[slab, pairs].astype(jnp.float32)
        factor = terms + pltpu.roll(terms, LANES // 2, 1)
        for pair in range(pairs):
            update = inbox[slab, pair].astype(jnp.float32) + factor * carries[pair]
            carries[pair] = jnp.where(valid, update, carries[pair])
    return carries


def states_kernel(dims, forcing_ref, retain_ref, states_ref, stage):
    days, blocks, size, probes = dims
    pairs = forcing_ref.shape[0]
    states = [jnp.zeros((blocks, LANES), jnp.float32)] * pairs
    for day in range(days):
        rows = pl.ds(day * blocks, blocks)
        factor = retain_ref[rows, :]
        for pair in range(pairs):
            states[pair] = factor * states[pair] + forcing_ref[pair, rows, :]
            stage[pair, rows, :] = states[pair]
    for block in range(blocks):
        for pair in range(pairs):
            states_ref[block, pl.ds(pair * days, days), :] = stage[pair, pl.ds(block, days, stride=blocks), :]


def adjoint_kernel(dims, hops, active_ref, states_ref, through_ref, inverse_ref, *rest):
    days, blocks, size, probes = dims
    adjoint_ref, message_ref, inbox, enter, starts = rest[hops:]
    pairs = adjoint_ref.shape[0]
    collect(rest[:hops], inbox)
    active = active_ref[...]
    for pair, carry in enumerate(carried(pairs, inbox, inbox, False)):
        enter[pair] = carry
    def make_adjoint(block, _):
        through = through_ref[block]
        stored = [
            (states_ref[block, pl.ds(pair * days, days), :] + through * enter[pair, pl.ds(block, 1), :])
            .astype(jnp.bfloat16)
            for pair in range(pairs)
        ]
        adjoint = jnp.dot(jnp.concatenate(stored, axis=0), inverse_ref[block], preferred_element_type=jnp.float32)
        for pair in range(pairs):
            tile = active * adjoint[pair * days : (pair + 1) * days]
            adjoint_ref[pair, pl.ds(block, days, stride=blocks), :] = tile
            starts[pair, pl.ds(block, 1), :] = jnp.sum(through * tile, axis=0, keepdims=True)
        return _

    lax.fori_loop(0, blocks, make_adjoint, 0, unroll=4)
    leave(message_ref, [starts[pair] for pair in range(pairs)])


def own_kernel(dims, adjoint_ref, retain_ref, moved_ref, partial_ref):
    days, blocks, size, probes = dims
    pairs = adjoint_ref.shape[0]
    carries = [jnp.zeros((blocks, LANES), jnp.float32)] * pairs
    for day in reversed(range(days)):
        rows = pl.ds(day * blocks, blocks)
        factor = retain_ref[rows, :]
        total = None
        for pair in range(pairs):
            smoothed = adjoint_ref[pair, rows, :] + carries[pair]
            carries[pair] = factor * smoothed
            term = smoothed * moved_ref[pair, rows, :].astype(jnp.float32)
            total = term if total is None else total + term
        partial_ref[rows, :] = total


def variance_kernel(dims, hops, partial_ref, retain_ref, moved_ref, *rest):
    days, blocks, size, probes = dims
    pairs = moved_ref.shape[0]
    out_hbm, stage, inbox, products, out_ref, left = rest[2 * hops :]
    collect(rest[:hops], inbox)
    collect(rest[hops : 2 * hops], products)
    carries = carried(pairs, inbox, products, True)
    reach = jnp.ones((blocks, LANES), jnp.float32)
    parts = left.shape[0]
    part = days // parts
    lane = lax.broadcasted_iota(jnp.int32, (part, LANES), 1)
    copies = []
    for first in reversed(range(0, days, part)):
        def finish(step, reach, first=first):
            rows = pl.ds(pl.multiple_of((first + part - 1 - step) * blocks, blocks), blocks)
            total = None
            for pair in range(pairs):
                term = carries[pair] * moved_ref[pair, rows, :].astype(jnp.float32)
                total = term if total is None else total + term
            stage[rows, :] = partial_ref[rows, :] + reach * total
            return reach * retain_ref[rows, :]

        reach = lax.fori_loop(0, part, finish, reach, unroll=8)
        done = pl.ds(first, part)
        for block in range(0, blocks, 2):
            both = [stage[pl.ds(first * blocks + block + half, part, stride=blocks), :] for half in range(2)]
            both = [value + pltpu.roll(value, size, 1) for value in both]
            out_ref[done, pl.ds(block * size, LANES)] = jnp.where(lane < size, both[0], both[1]) * (1.0 / probes)
        copies.append(pltpu.make_async_copy(out_ref.at[done], out_hbm.at[done], left.at[len(copies)]))
        copies[-1].start()
    for copy in copies:
        copy.wait()


def call(kernel, outs, scratch, flops, moved, scalars, *operands, apart=(), limit=VMEM_LIMIT, out_space=pltpu.VMEM):
    in_specs = [
        pl.BlockSpec(memory_space=pltpu.SMEM if i < scalars else pl.ANY if i in apart else pltpu.VMEM)
        for i in range(len(operands))
    ]
    return pl.pallas_call(
        kernel,
        out_shape=[jax.ShapeDtypeStruct(shape, kind) for shape, kind in outs],
        in_specs=in_specs,
        out_specs=[pl.BlockSpec(memory_space=out_space) for _ in outs],
        scratch_shapes=scratch,
        compiler_params=pltpu.CompilerParams(vmem_limit_bytes=limit),
        cost_estimate=pl.CostEstimate(flops=flops, bytes_accessed=moved, transcendentals=0),
    )(*operands)


def crossed(block, axis, bits):
    return lax.ppermute(block, axis, [(i, i ^ bits) for i in range(lax.axis_size(axis))])


def local(
    probes,
    local_links,
    remote_links,
    shared_blocks,
    slab_days,
    local_coupling,
    remote_coupling,
    block_inverse,
    retention,
):
    days, blocks, width = probes.shape
    size = block_inverse.shape[1]
    dims = (days, blocks, size, width // size)
    pairs = width // LANES
    f32, bf16 = jnp.float32, jnp.bfloat16
    bound = shared_blocks.shape[1]
    far = remote_links.shape[1]
    rows = days * blocks
    groups = lax.axis_size("space")
    held = groups // 2 * bound
    near_table, far_table = local_links.T, remote_links.T
    big = ((pairs, rows, LANES), f32)

    (outgoing,) = call(
        functools.partial(outgoing_kernel, dims),
        [((bound, pairs * days, LANES), bf16)],
        [
            pltpu.SMEM(shared_blocks.shape, jnp.int32),
            pltpu.VMEM(probes.shape, bf16),
            pltpu.SemaphoreType.DMA,
            pltpu.SemaphoreType.DMA((2,)),
        ],
        10**9, 4 * 10**6, 0, shared_blocks, probes, apart=(0, 1), limit=63 * 1024 * 1024,
    )
    pieces = {bits: crossed(outgoing, "space", bits) for bits in range(groups - 2, 0, -2)}
    by_block = (blocks, pairs * days, LANES)
    moved, turned = call(
        functools.partial(turn_kernel, dims),
        [((pairs, rows, LANES), bf16), (by_block, bf16)],
        [pltpu.VMEM(*big)], 10**10, 10**7, 0, probes,
    )
    running, remote_weight, inverse = call(
        functools.partial(local_kernel, dims),
        [(by_block, f32), ((blocks, LANES, far * LANES), bf16), ((blocks, LANES, LANES), bf16)],
        [], 10**10, 10**7, 1, near_table, turned, local_coupling, remote_coupling, block_inverse,
    )
    retain, product, through, beyond, active = call(
        functools.partial(retain_kernel, dims),
        [
            ((rows, LANES), f32),
            ((blocks, LANES), bf16),
            ((blocks, days, LANES), f32),
            ((blocks, days, LANES), f32),
            ((days, LANES), f32),
        ],
        [pltpu.VMEM((2, rows, LANES), f32)], 10**6, 10**5, 1, slab_days, retention,
    )
    pieces[0] = outgoing
    batches = [0, groups - 2, groups - 2], list(range(groups - 4, 0, -2))
    same = []
    for batch in batches:
        shape = (len(batch) * bound, pairs * days, LANES)
        same += call(pass_kernel, [(shape, bf16)], [], 0, 10**5, 0, *[pieces[bits] for bits in batch], inverse)
    other = [crossed(piece, "space", 1) for piece in same]
    raw = [pieces[bits] for bits in range(2, groups, 2)]
    slabs = lax.axis_size("tm")
    hops = slabs - 1
    exchange = lambda message: [crossed(message, "tm", bits) for bits in range(hops, 0, -1)][::-1]
    inbox = pltpu.VMEM((slabs, pairs + 1, blocks, LANES), bf16)
    values = pltpu.VMEM((pairs, blocks, LANES), f32)
    forcing, message = call(
        functools.partial(forward_kernel, dims, batches),
        [big, ((pairs + 1, blocks, LANES), bf16)],
        [pltpu.VMEM((2 * held, pairs * days, LANES), bf16), pltpu.VMEM(by_block, bf16), values], 10**10, 10**7, 1,
        far_table, active, running, remote_weight, inverse, beyond, product, *raw, *same, *other,
        apart=range(7, 7 + len(raw)),
    )
    ends = exchange(message)
    (states,) = call(
        functools.partial(states_kernel, dims), [(by_block, f32)], [pltpu.VMEM(*big)], 10**9, 10**6, 0, forcing, retain
    )
    adjoint, message = call(
        functools.partial(adjoint_kernel, dims, hops),
        [big, ((pairs, blocks, LANES), bf16)],
        [inbox, values, values], 10**10, 10**7, 0, active, states, through, inverse, *ends,
    )
    starts = exchange(message)
    (partial,) = call(
        functools.partial(own_kernel, dims), [((rows, LANES), f32)], [], 10**9, 10**6, 0, adjoint, retain, moved
    )
    (variance,) = call(
        functools.partial(variance_kernel, dims, hops),
        [((days, blocks * size), f32)],
        [
            pltpu.VMEM((rows, LANES), f32),
            pltpu.VMEM((slabs, pairs, blocks, LANES), bf16),
            inbox,
            pltpu.VMEM((days, blocks * size), f32),
            pltpu.SemaphoreType.DMA((2,)),
        ],
        10**10, 10**7, 0, partial, retain, moved, *starts, *ends, out_space=pl.ANY,
    )
    return variance


def solution(mesh):
    placed = (
        P("tm", "space", None),
        P("space", None),
        P("space", None),
        P("space", None),
        P("tm"),
        P("space", None, None, None),
        P("space", None, None, None),
        P("space", None, None),
        P("tm", "space"),
    )
    return jax.shard_map(
        local, mesh=mesh, in_specs=placed, out_specs=P("tm", "space"), check_vma=False
    )
```

```python
import functools

import jax
import jax.numpy as jnp
from jax import lax
from jax.experimental import pallas as pl
from jax.experimental.pallas import tpu as pltpu
from jax.sharding import PartitionSpec as P

LANES = 128
VMEM_LIMIT = 20 * 1024 * 1024
TURNED = (((1,), (1,)), ((), ()))


def permutation(size, probes, start, width):
    total = size * probes
    column = lax.broadcasted_iota(jnp.int32, (total, width), 1) + start
    origin = (column % size) * probes + column // size
    row = lax.broadcasted_iota(jnp.int32, (total, width), 0)
    return (row == origin).astype(jnp.float32).astype(jnp.bfloat16)


def doubled(weight):
    zero = jnp.zeros_like(weight)
    return jnp.concatenate(
        [jnp.concatenate([weight, zero], axis=1), jnp.concatenate([zero, weight], axis=1)], axis=0
    )


def outgoing_kernel(dims, shared_hbm, z_hbm, outgoing_ref, shared_ref, z_ref, listed, arrived):
    days, blocks, size, probes = dims
    count = outgoing_ref.shape[0]
    parts = arrived.shape[0]
    part = days // parts
    copies = [
        pltpu.make_async_copy(z_hbm.at[pl.ds(i * part, part)], z_ref.at[pl.ds(i * part, part)], arrived.at[i])
        for i in range(parts)
    ]
    listing = pltpu.make_async_copy(shared_hbm, shared_ref, listed)
    listing.start()
    for copy in copies:
        copy.start()
    row = lax.broadcasted_iota(jnp.int32, (part, part * blocks), 0)
    column = lax.broadcasted_iota(jnp.int32, (part, part * blocks), 1)
    move = permutation(size, probes, 0, 2 * LANES)
    listing.wait()
    picks = [(column == row * blocks + shared_ref[0, m]).astype(jnp.float32) for m in range(count)]
    picks = jnp.concatenate(picks, axis=0).astype(jnp.bfloat16)
    picked = []
    for i, copy in enumerate(copies):
        copy.wait()
        z = z_ref[pl.ds(i * part, part)].reshape(part * blocks, size * probes)
        picked.append(jnp.dot(picks, z, preferred_element_type=jnp.float32))
    picked = jnp.concatenate([rows[m * part : (m + 1) * part] for m in range(count) for rows in picked], axis=0)
    step = 2 * LANES
    shift = step // size
    ranges = size * probes // step
    shifted = [picked] + [pltpu.roll(picked, size * probes - i * shift, 1) for i in range(1, ranges)]
    shifted = jnp.concatenate(shifted, axis=0).astype(jnp.bfloat16)
    moved = jnp.dot(shifted, move, preferred_element_type=jnp.float32)
    moved = moved.astype(jnp.bfloat16)
    for pair in range(size * probes // LANES):
        for m in range(count):
            row, lane = (pair // 2 * count + m) * days, pair % 2 * LANES
            outgoing_ref[m, pl.ds(pair * days, days), :] = moved[row : row + days, lane : lane + LANES]


def turn_kernel(dims, z_ref, moved_ref, turned_ref, stage):
    days, blocks, size, probes = dims
    pairs = size * probes // LANES
    z = z_ref[...].reshape(days * blocks, size * probes)
    step = 2 * LANES
    for start in range(0, size * probes, step):
        moved = jnp.dot(z, permutation(size, probes, start, step), preferred_element_type=jnp.float32)
        for half in range(2):
            pair = start // LANES + half
            tile = moved[:, half * LANES : (half + 1) * LANES]
            stage[pair] = tile
            moved_ref[pair] = tile.astype(jnp.bfloat16)
    for block in range(blocks):
        for pair in range(pairs):
            rows = stage[pair, pl.ds(block, days, stride=blocks), :]
            turned_ref[block, pl.ds(pair * days, days), :] = rows.astype(jnp.bfloat16)


def local_kernel(
    dims, links_ref, turned_ref, weight_ref, remote_weight_ref, inverse_ref,
    running_ref, remote_doubled_ref, inverse_doubled_ref,
):
    days, blocks, size, probes = dims
    count = links_ref.shape[0]
    for block in range(blocks):
        near = jnp.concatenate([turned_ref[links_ref[k, block]] for k in range(count)], axis=1)
        weight = jnp.concatenate([doubled(weight_ref[block, k]) for k in range(count)], axis=1)
        total = lax.dot_general(near, weight, TURNED, preferred_element_type=jnp.float32)
        running_ref[block] = turned_ref[block].astype(jnp.float32) - total
        remote_doubled_ref[block] = jnp.concatenate(
            [doubled(remote_weight_ref[block, k]) for k in range(remote_weight_ref.shape[1])], axis=1
        )
        inverse_doubled_ref[block] = doubled(inverse_ref[block])


def retain_kernel(
    dims, days_ref, retention_ref, retain_ref, product_ref, through_ref, beyond_ref, active_ref, stage
):
    days, blocks, size, probes = dims
    observed = days_ref[0]
    shape = (days, LANES)
    first = lax.broadcasted_iota(jnp.int32, shape, 1) < size
    seen = lax.broadcasted_iota(jnp.int32, shape, 0) < observed
    active_ref[...] = jnp.where(seen, 1.0, 0.0)
    for block in range(0, blocks, 2):
        factor = jnp.where(seen, retention_ref[:, pl.ds(block * size, LANES)], 1.0)
        other = pltpu.roll(factor, size, 1)
        retain_ref[pl.ds(block, days, stride=blocks), :] = jnp.where(first, factor, other)
        retain_ref[pl.ds(block + 1, days, stride=blocks), :] = jnp.where(first, other, factor)
    product = jnp.ones((blocks, LANES), jnp.float32)
    for day in range(days):
        rows = pl.ds(day * blocks, blocks)
        product = product * retain_ref[rows, :]
        stage[0, rows, :] = product
    after = jnp.ones((blocks, LANES), jnp.float32)
    for day in reversed(range(days)):
        rows = pl.ds(day * blocks, blocks)
        stage[1, rows, :] = after
        after = after * retain_ref[rows, :]
    for block in range(blocks):
        through_ref[block] = stage[0, pl.ds(block, days, stride=blocks), :]
        beyond_ref[block] = stage[1, pl.ds(block, days, stride=blocks), :]
    high = product.astype(jnp.bfloat16).astype(jnp.float32)
    half = lax.broadcasted_iota(jnp.int32, product.shape, 1) < size
    product_ref[...] = jnp.where(half, high, product - high).astype(jnp.bfloat16)


def pass_kernel(*refs):
    *piece_refs, before_ref, out_ref = refs
    count = piece_refs[0].shape[0]
    for k, ref in enumerate(piece_refs):
        out_ref[pl.ds(k * count, count)] = ref[...]
    filled = len(piece_refs) * count
    if filled < out_ref.shape[0]:
        room = out_ref.shape[0] - filled
        out_ref[pl.ds(filled, room)] = piece_refs[0][pl.ds(0, room)]


def forward_kernel(
    dims, batches, links_ref, active_ref, running_ref, weight_ref, inverse_ref, beyond_ref, product_ref, *rest
):
    days, blocks, size, probes = dims
    piece_refs = rest[-5 - 2 * len(batches) : -5]
    forcing_ref, message_ref, remote, source, ends = rest[-5:]
    pairs = forcing_ref.shape[0]
    count = links_ref.shape[0]
    held = remote.shape[0] // 2
    bound = held // (lax.axis_size("space") // 2)
    me = lax.axis_index("space")
    for core in range(2):
        for ref, batch in zip(piece_refs[core * len(batches) :], batches):
            for place, bits in enumerate(batch):
                remote[pl.ds(core * held + bits // 2 * bound, bound)] = ref[pl.ds(place * bound, bound)]
    active = active_ref[...]
    for block in range(blocks):
        places = []
        for k in range(count):
            link = links_ref[k, block]
            distance = (link // bound) ^ me
            places.append((distance % 2) * held + (distance // 2) * bound + link % bound)
        far = jnp.concatenate([remote[place] for place in places], axis=1)
        total = lax.dot_general(far, weight_ref[block], TURNED, preferred_element_type=jnp.float32)
        source[block] = (running_ref[block] - total).astype(jnp.bfloat16)
    for block in range(blocks):
        drive = lax.dot_general(source[block], inverse_ref[block], TURNED, preferred_element_type=jnp.float32)
        beyond = beyond_ref[block]
        for pair in range(pairs):
            tile = active * drive[pair * days : (pair + 1) * days]
            forcing_ref[pair, pl.ds(block, days, stride=blocks), :] = tile
            ends[pair, pl.ds(block, 1), :] = jnp.sum(beyond * tile, axis=0, keepdims=True)
    leave(message_ref, [ends[pair] for pair in range(pairs)])
    message_ref[pairs] = product_ref[...]


def leave(message_ref, values):
    for pair, value in enumerate(values):
        message_ref[pair] = value.astype(jnp.bfloat16)


def collect(piece_refs, inbox):
    me = lax.axis_index("tm")
    for k, ref in enumerate(piece_refs):
        inbox[me ^ (k + 1)] = ref[...]


def carried(pairs, inbox, products, backward):
    me, count = lax.axis_index("tm"), inbox.shape[0]
    carries = [jnp.zeros(inbox.shape[2:], jnp.float32)] * pairs
    for slab in range(count - 1, 0, -1) if backward else range(count - 1):
        valid = slab > me if backward else slab < me
        terms = products[slab, pairs].astype(jnp.float32)
        factor = terms + pltpu.roll(terms, LANES // 2, 1)
        for pair in range(pairs):
            update = inbox[slab, pair].astype(jnp.float32) + factor * carries[pair]
            carries[pair] = jnp.where(valid, update, carries[pair])
    return carries


def states_kernel(dims, forcing_ref, retain_ref, states_ref, stage):
    days, blocks, size, probes = dims
    pairs = forcing_ref.shape[0]
    states = [jnp.zeros((blocks, LANES), jnp.float32)] * pairs
    for day in range(days):
        rows = pl.ds(day * blocks, blocks)
        factor = retain_ref[rows, :]
        for pair in range(pairs):
            states[pair] = factor * states[pair] + forcing_ref[pair, rows, :]
            stage[pair, rows, :] = states[pair]
    for block in range(blocks):
        for pair in range(pairs):
            states_ref[block, pl.ds(pair * days, days), :] = stage[pair, pl.ds(block, days, stride=blocks), :]


def adjoint_kernel(dims, hops, active_ref, states_ref, through_ref, inverse_ref, *rest):
    days, blocks, size, probes = dims
    adjoint_ref, message_ref, inbox, enter, starts = rest[hops:]
    pairs = adjoint_ref.shape[0]
    collect(rest[:hops], inbox)
    active = active_ref[...]
    for pair, carry in enumerate(carried(pairs, inbox, inbox, False)):
        enter[pair] = carry
    for block in range(blocks):
        through = through_ref[block]
        stored = [
            (states_ref[block, pl.ds(pair * days, days), :] + through * enter[pair, pl.ds(block, 1), :])
            .astype(jnp.bfloat16)
            for pair in range(pairs)
        ]
        adjoint = jnp.dot(jnp.concatenate(stored, axis=0), inverse_ref[block], preferred_element_type=jnp.float32)
        for pair in range(pairs):
            tile = active * adjoint[pair * days : (pair + 1) * days]
            adjoint_ref[pair, pl.ds(block, days, stride=blocks), :] = tile
            starts[pair, pl.ds(block, 1), :] = jnp.sum(through * tile, axis=0, keepdims=True)
    leave(message_ref, [starts[pair] for pair in range(pairs)])


def own_kernel(dims, adjoint_ref, retain_ref, moved_ref, partial_ref):
    days, blocks, size, probes = dims
    pairs = adjoint_ref.shape[0]
    carries = [jnp.zeros((blocks, LANES), jnp.float32)] * pairs
    for day in reversed(range(days)):
        rows = pl.ds(day * blocks, blocks)
        factor = retain_ref[rows, :]
        total = None
        for pair in range(pairs):
            smoothed = adjoint_ref[pair, rows, :] + carries[pair]
            carries[pair] = factor * smoothed
            term = smoothed * moved_ref[pair, rows, :].astype(jnp.float32)
            total = term if total is None else total + term
        partial_ref[rows, :] = total


def variance_kernel(dims, hops, partial_ref, retain_ref, moved_ref, *rest):
    days, blocks, size, probes = dims
    pairs = moved_ref.shape[0]
    out_hbm, stage, inbox, products, out_ref, left = rest[2 * hops :]
    collect(rest[:hops], inbox)
    collect(rest[hops : 2 * hops], products)
    carries = carried(pairs, inbox, products, True)
    reach = jnp.ones((blocks, LANES), jnp.float32)
    parts = left.shape[0]
    part = days // parts
    lane = lax.broadcasted_iota(jnp.int32, (part, LANES), 1)
    copies = []
    for first in reversed(range(0, days, part)):
        for day in reversed(range(first, first + part)):
            rows = pl.ds(day * blocks, blocks)
            total = None
            for pair in range(pairs):
                term = carries[pair] * moved_ref[pair, rows, :].astype(jnp.float32)
                total = term if total is None else total + term
            stage[rows, :] = partial_ref[rows, :] + reach * total
            reach = reach * retain_ref[rows, :]
        done = pl.ds(first, part)
        for block in range(0, blocks, 2):
            both = [stage[pl.ds(first * blocks + block + half, part, stride=blocks), :] for half in range(2)]
            both = [value + pltpu.roll(value, size, 1) for value in both]
            out_ref[done, pl.ds(block * size, LANES)] = jnp.where(lane < size, both[0], both[1]) * (1.0 / probes)
        copies.append(pltpu.make_async_copy(out_ref.at[done], out_hbm.at[done], left.at[len(copies)]))
        copies[-1].start()
    for copy in copies:
        copy.wait()


def call(kernel, outs, scratch, flops, moved, scalars, *operands, apart=(), limit=VMEM_LIMIT, out_space=pltpu.VMEM):
    in_specs = [
        pl.BlockSpec(memory_space=pltpu.SMEM if i < scalars else pl.ANY if i in apart else pltpu.VMEM)
        for i in range(len(operands))
    ]
    return pl.pallas_call(
        kernel,
        out_shape=[jax.ShapeDtypeStruct(shape, kind) for shape, kind in outs],
        in_specs=in_specs,
        out_specs=[pl.BlockSpec(memory_space=out_space) for _ in outs],
        scratch_shapes=scratch,
        compiler_params=pltpu.CompilerParams(vmem_limit_bytes=limit),
        cost_estimate=pl.CostEstimate(flops=flops, bytes_accessed=moved, transcendentals=0),
    )(*operands)


def crossed(block, axis, bits):
    return lax.ppermute(block, axis, [(i, i ^ bits) for i in range(lax.axis_size(axis))])


def local(
    probes,
    local_links,
    remote_links,
    shared_blocks,
    slab_days,
    local_coupling,
    remote_coupling,
    block_inverse,
    retention,
):
    days, blocks, width = probes.shape
    size = block_inverse.shape[1]
    dims = (days, blocks, size, width // size)
    pairs = width // LANES
    f32, bf16 = jnp.float32, jnp.bfloat16
    bound = shared_blocks.shape[1]
    far = remote_links.shape[1]
    rows = days * blocks
    groups = lax.axis_size("space")
    held = groups // 2 * bound
    near_table, far_table = local_links.T, remote_links.T
    big = ((pairs, rows, LANES), f32)

    (outgoing,) = call(
        functools.partial(outgoing_kernel, dims),
        [((bound, pairs * days, LANES), bf16)],
        [
            pltpu.SMEM(shared_blocks.shape, jnp.int32),
            pltpu.VMEM(probes.shape, bf16),
            pltpu.SemaphoreType.DMA,
            pltpu.SemaphoreType.DMA((2,)),
        ],
        10**9, 4 * 10**6, 0, shared_blocks, probes, apart=(0, 1), limit=63 * 1024 * 1024,
    )
    pieces = {bits: crossed(outgoing, "space", bits) for bits in range(groups - 2, 0, -2)}
    by_block = (blocks, pairs * days, LANES)
    moved, turned = call(
        functools.partial(turn_kernel, dims),
        [((pairs, rows, LANES), bf16), (by_block, bf16)],
        [pltpu.VMEM(*big)], 10**10, 10**7, 0, probes,
    )
    running, remote_weight, inverse = call(
        functools.partial(local_kernel, dims),
        [(by_block, f32), ((blocks, LANES, far * LANES), bf16), ((blocks, LANES, LANES), bf16)],
        [], 10**10, 10**7, 1, near_table, turned, local_coupling, remote_coupling, block_inverse,
    )
    retain, product, through, beyond, active = call(
        functools.partial(retain_kernel, dims),
        [
            ((rows, LANES), f32),
            ((blocks, LANES), bf16),
            ((blocks, days, LANES), f32),
            ((blocks, days, LANES), f32),
            ((days, LANES), f32),
        ],
        [pltpu.VMEM((2, rows, LANES), f32)], 10**6, 10**5, 1, slab_days, retention,
    )
    pieces[0] = outgoing
    batches = [0, groups - 2], list(range(groups - 4, 0, -2))
    same = []
    for extra, batch in zip((1, 0), batches):
        shape = (len(batch) * bound + extra, pairs * days, LANES)
        same += call(pass_kernel, [(shape, bf16)], [], 0, 10**5, 0, *[pieces[bits] for bits in batch], inverse)
    other = [crossed(piece, "space", 1) for piece in same]
    raw = [pieces[bits] for bits in range(2, groups, 2)]
    slabs = lax.axis_size("tm")
    hops = slabs - 1
    exchange = lambda message: [crossed(message, "tm", bits) for bits in range(hops, 0, -1)][::-1]
    inbox = pltpu.VMEM((slabs, pairs + 1, blocks, LANES), bf16)
    values = pltpu.VMEM((pairs, blocks, LANES), f32)
    forcing, message = call(
        functools.partial(forward_kernel, dims, batches),
        [big, ((pairs + 1, blocks, LANES), bf16)],
        [pltpu.VMEM((2 * held, pairs * days, LANES), bf16), pltpu.VMEM(by_block, bf16), values], 10**10, 10**7, 1,
        far_table, active, running, remote_weight, inverse, beyond, product, *raw, *same, *other,
        apart=range(7, 7 + len(raw)),
    )
    ends = exchange(message)
    (states,) = call(
        functools.partial(states_kernel, dims), [(by_block, f32)], [pltpu.VMEM(*big)], 10**9, 10**6, 0, forcing, retain
    )
    adjoint, message = call(
        functools.partial(adjoint_kernel, dims, hops),
        [big, ((pairs, blocks, LANES), bf16)],
        [inbox, values, values], 10**10, 10**7, 0, active, states, through, inverse, *ends,
    )
    starts = exchange(message)
    (partial,) = call(
        functools.partial(own_kernel, dims), [((rows, LANES), f32)], [], 10**9, 10**6, 0, adjoint, retain, moved
    )
    (variance,) = call(
        functools.partial(variance_kernel, dims, hops),
        [((days, blocks * size), f32)],
        [
            pltpu.VMEM((rows, LANES), f32),
            pltpu.VMEM((slabs, pairs, blocks, LANES), bf16),
            inbox,
            pltpu.VMEM((days, blocks * size), f32),
            pltpu.SemaphoreType.DMA((2,)),
        ],
        10**10, 10**7, 0, partial, retain, moved, *starts, *ends, out_space=pl.ANY,
    )
    return variance


def solution(mesh):
    placed = (
        P("tm", "space", None),
        P("space", None),
        P("space", None),
        P("space", None),
        P("tm"),
        P("space", None, None, None),
        P("space", None, None, None),
        P("space", None, None),
        P("tm", "space"),
    )
    return jax.shard_map(
        local, mesh=mesh, in_specs=placed, out_specs=P("tm", "space"), check_vma=False
    )
```

```python
import functools

import jax
import jax.numpy as jnp
from jax import lax
from jax.experimental import pallas as pl
from jax.experimental.pallas import tpu as pltpu
from jax.sharding import PartitionSpec as P

LANES = 128
VMEM_LIMIT = 20 * 1024 * 1024
TURNED = (((1,), (1,)), ((), ()))


def permutation(size, probes, start, width):
    total = size * probes
    column = lax.broadcasted_iota(jnp.int32, (total, width), 1) + start
    origin = (column % size) * probes + column // size
    row = lax.broadcasted_iota(jnp.int32, (total, width), 0)
    return (row == origin).astype(jnp.float32).astype(jnp.bfloat16)


def doubled(weight):
    zero = jnp.zeros_like(weight)
    return jnp.concatenate(
        [jnp.concatenate([weight, zero], axis=1), jnp.concatenate([zero, weight], axis=1)], axis=0
    )


def outgoing_kernel(dims, shared_hbm, z_hbm, outgoing_ref, shared_ref, z_ref, listed, arrived):
    days, blocks, size, probes = dims
    count = outgoing_ref.shape[0]
    parts = arrived.shape[0]
    part = days // parts
    copies = [
        pltpu.make_async_copy(z_hbm.at[pl.ds(i * part, part)], z_ref.at[pl.ds(i * part, part)], arrived.at[i])
        for i in range(parts)
    ]
    listing = pltpu.make_async_copy(shared_hbm, shared_ref, listed)
    listing.start()
    for copy in copies:
        copy.start()
    row = lax.broadcasted_iota(jnp.int32, (part, part * blocks), 0)
    column = lax.broadcasted_iota(jnp.int32, (part, part * blocks), 1)
    move = permutation(size, probes, 0, 2 * LANES)
    listing.wait()
    picks = [(column == row * blocks + shared_ref[0, m]).astype(jnp.float32) for m in range(count)]
    picks = jnp.concatenate(picks, axis=0).astype(jnp.bfloat16)
    picked = []
    for i, copy in enumerate(copies):
        copy.wait()
        z = z_ref[pl.ds(i * part, part)].reshape(part * blocks, size * probes)
        picked.append(jnp.dot(picks, z, preferred_element_type=jnp.float32))
    picked = jnp.concatenate([rows[m * part : (m + 1) * part] for m in range(count) for rows in picked], axis=0)
    step = 2 * LANES
    shift = step // size
    ranges = size * probes // step
    shifted = [picked] + [pltpu.roll(picked, size * probes - i * shift, 1) for i in range(1, ranges)]
    shifted = jnp.concatenate(shifted, axis=0).astype(jnp.bfloat16)
    moved = jnp.dot(shifted, move, preferred_element_type=jnp.float32)
    moved = moved.astype(jnp.bfloat16)
    for pair in range(size * probes // LANES):
        for m in range(count):
            row, lane = (pair // 2 * count + m) * days, pair % 2 * LANES
            outgoing_ref[m, pl.ds(pair * days, days), :] = moved[row : row + days, lane : lane + LANES]


def turn_kernel(dims, z_ref, before_ref, moved_ref, turned_ref, stage):
    days, blocks, size, probes = dims
    pairs = size * probes // LANES
    z = z_ref[...].reshape(days * blocks, size * probes)
    step = 2 * LANES
    for start in range(0, size * probes, step):
        moved = jnp.dot(z, permutation(size, probes, start, step), preferred_element_type=jnp.float32)
        for half in range(2):
            pair = start // LANES + half
            tile = moved[:, half * LANES : (half + 1) * LANES]
            stage[pair] = tile
            moved_ref[pair] = tile.astype(jnp.bfloat16)
    for block in range(blocks):
        for pair in range(pairs):
            rows = stage[pair, pl.ds(block, days, stride=blocks), :]
            turned_ref[block, pl.ds(pair * days, days), :] = rows.astype(jnp.bfloat16)


def local_kernel(
    dims, links_ref, turned_ref, weight_ref, remote_weight_ref, inverse_ref,
    running_ref, remote_doubled_ref, inverse_doubled_ref,
):
    days, blocks, size, probes = dims
    count = links_ref.shape[0]
    for block in range(blocks):
        near = jnp.concatenate([turned_ref[links_ref[k, block]] for k in range(count)], axis=1)
        weight = jnp.concatenate([doubled(weight_ref[block, k]) for k in range(count)], axis=1)
        total = lax.dot_general(near, weight, TURNED, preferred_element_type=jnp.float32)
        running_ref[block] = turned_ref[block].astype(jnp.float32) - total
        remote_doubled_ref[block] = jnp.concatenate(
            [doubled(remote_weight_ref[block, k]) for k in range(remote_weight_ref.shape[1])], axis=1
        )
        inverse_doubled_ref[block] = doubled(inverse_ref[block])


def retain_kernel(
    dims, days_ref, retention_ref, retain_ref, product_ref, through_ref, beyond_ref, active_ref, stage
):
    days, blocks, size, probes = dims
    observed = days_ref[0]
    shape = (days, LANES)
    first = lax.broadcasted_iota(jnp.int32, shape, 1) < size
    seen = lax.broadcasted_iota(jnp.int32, shape, 0) < observed
    active_ref[...] = jnp.where(seen, 1.0, 0.0)
    for block in range(0, blocks, 2):
        factor = jnp.where(seen, retention_ref[:, pl.ds(block * size, LANES)], 1.0)
        other = pltpu.roll(factor, size, 1)
        retain_ref[pl.ds(block, days, stride=blocks), :] = jnp.where(first, factor, other)
        retain_ref[pl.ds(block + 1, days, stride=blocks), :] = jnp.where(first, other, factor)
    product = jnp.ones((blocks, LANES), jnp.float32)
    for day in range(days):
        rows = pl.ds(day * blocks, blocks)
        product = product * retain_ref[rows, :]
        stage[0, rows, :] = product
    after = jnp.ones((blocks, LANES), jnp.float32)
    for day in reversed(range(days)):
        rows = pl.ds(day * blocks, blocks)
        stage[1, rows, :] = after
        after = after * retain_ref[rows, :]
    for block in range(blocks):
        through_ref[block] = stage[0, pl.ds(block, days, stride=blocks), :]
        beyond_ref[block] = stage[1, pl.ds(block, days, stride=blocks), :]
    high = product.astype(jnp.bfloat16).astype(jnp.float32)
    half = lax.broadcasted_iota(jnp.int32, product.shape, 1) < size
    product_ref[...] = jnp.where(half, high, product - high).astype(jnp.bfloat16)


def pass_kernel(*refs):
    *piece_refs, before_ref, out_ref = refs
    count = piece_refs[0].shape[0]
    for k, ref in enumerate(piece_refs):
        out_ref[pl.ds(k * count, count)] = ref[...]
    filled = len(piece_refs) * count
    if filled < out_ref.shape[0]:
        room = out_ref.shape[0] - filled
        out_ref[pl.ds(filled, room)] = piece_refs[0][pl.ds(0, room)]


def forward_kernel(
    dims, batches, links_ref, active_ref, running_ref, weight_ref, inverse_ref, beyond_ref, product_ref, *rest
):
    days, blocks, size, probes = dims
    piece_refs = rest[-5 - 2 * len(batches) : -5]
    forcing_ref, message_ref, remote, source, ends = rest[-5:]
    pairs = forcing_ref.shape[0]
    count = links_ref.shape[0]
    held = remote.shape[0] // 2
    bound = held // (lax.axis_size("space") // 2)
    me = lax.axis_index("space")
    for core in range(2):
        for ref, batch in zip(piece_refs[core * len(batches) :], batches):
            for place, bits in enumerate(batch):
                remote[pl.ds(core * held + bits // 2 * bound, bound)] = ref[pl.ds(place * bound, bound)]
    active = active_ref[...]
    for block in range(blocks):
        places = []
        for k in range(count):
            link = links_ref[k, block]
            distance = (link // bound) ^ me
            places.append((distance % 2) * held + (distance // 2) * bound + link % bound)
        far = jnp.concatenate([remote[place] for place in places], axis=1)
        total = lax.dot_general(far, weight_ref[block], TURNED, preferred_element_type=jnp.float32)
        source[block] = (running_ref[block] - total).astype(jnp.bfloat16)
    for block in range(blocks):
        drive = lax.dot_general(source[block], inverse_ref[block], TURNED, preferred_element_type=jnp.float32)
        beyond = beyond_ref[block]
        for pair in range(pairs):
            tile = active * drive[pair * days : (pair + 1) * days]
            forcing_ref[pair, pl.ds(block, days, stride=blocks), :] = tile
            ends[pair, pl.ds(block, 1), :] = jnp.sum(beyond * tile, axis=0, keepdims=True)
    leave(message_ref, [ends[pair] for pair in range(pairs)])
    message_ref[pairs] = product_ref[...]


def leave(message_ref, values):
    for pair, value in enumerate(values):
        message_ref[pair] = value.astype(jnp.bfloat16)


def collect(piece_refs, inbox):
    me = lax.axis_index("tm")
    for k, ref in enumerate(piece_refs):
        inbox[me ^ (k + 1)] = ref[...]


def carried(pairs, inbox, products, backward):
    me, count = lax.axis_index("tm"), inbox.shape[0]
    carries = [jnp.zeros(inbox.shape[2:], jnp.float32)] * pairs
    for slab in range(count - 1, 0, -1) if backward else range(count - 1):
        valid = slab > me if backward else slab < me
        terms = products[slab, pairs].astype(jnp.float32)
        factor = terms + pltpu.roll(terms, LANES // 2, 1)
        for pair in range(pairs):
            update = inbox[slab, pair].astype(jnp.float32) + factor * carries[pair]
            carries[pair] = jnp.where(valid, update, carries[pair])
    return carries


def states_kernel(dims, forcing_ref, retain_ref, states_ref, stage):
    days, blocks, size, probes = dims
    pairs = forcing_ref.shape[0]
    states = [jnp.zeros((blocks, LANES), jnp.float32)] * pairs
    for day in range(days):
        rows = pl.ds(day * blocks, blocks)
        factor = retain_ref[rows, :]
        for pair in range(pairs):
            states[pair] = factor * states[pair] + forcing_ref[pair, rows, :]
            stage[pair, rows, :] = states[pair]
    for block in range(blocks):
        for pair in range(pairs):
            states_ref[block, pl.ds(pair * days, days), :] = stage[pair, pl.ds(block, days, stride=blocks), :]


def adjoint_kernel(dims, hops, active_ref, states_ref, through_ref, inverse_ref, *rest):
    days, blocks, size, probes = dims
    adjoint_ref, message_ref, inbox, enter, starts = rest[hops:]
    pairs = adjoint_ref.shape[0]
    collect(rest[:hops], inbox)
    active = active_ref[...]
    for pair, carry in enumerate(carried(pairs, inbox, inbox, False)):
        enter[pair] = carry
    for block in range(blocks):
        through = through_ref[block]
        stored = [
            (states_ref[block, pl.ds(pair * days, days), :] + through * enter[pair, pl.ds(block, 1), :])
            .astype(jnp.bfloat16)
            for pair in range(pairs)
        ]
        adjoint = jnp.dot(jnp.concatenate(stored, axis=0), inverse_ref[block], preferred_element_type=jnp.float32)
        for pair in range(pairs):
            tile = active * adjoint[pair * days : (pair + 1) * days]
            adjoint_ref[pair, pl.ds(block, days, stride=blocks), :] = tile
            starts[pair, pl.ds(block, 1), :] = jnp.sum(through * tile, axis=0, keepdims=True)
    leave(message_ref, [starts[pair] for pair in range(pairs)])


def own_kernel(dims, adjoint_ref, retain_ref, moved_ref, partial_ref):
    days, blocks, size, probes = dims
    pairs = adjoint_ref.shape[0]
    carries = [jnp.zeros((blocks, LANES), jnp.float32)] * pairs
    for day in reversed(range(days)):
        rows = pl.ds(day * blocks, blocks)
        factor = retain_ref[rows, :]
        total = None
        for pair in range(pairs):
            smoothed = adjoint_ref[pair, rows, :] + carries[pair]
            carries[pair] = factor * smoothed
            term = smoothed * moved_ref[pair, rows, :].astype(jnp.float32)
            total = term if total is None else total + term
        partial_ref[rows, :] = total


def variance_kernel(dims, hops, partial_ref, retain_ref, moved_ref, *rest):
    days, blocks, size, probes = dims
    pairs = moved_ref.shape[0]
    out_hbm, stage, inbox, products, out_ref, left = rest[2 * hops :]
    collect(rest[:hops], inbox)
    collect(rest[hops : 2 * hops], products)
    carries = carried(pairs, inbox, products, True)
    reach = jnp.ones((blocks, LANES), jnp.float32)
    parts = left.shape[0]
    part = days // parts
    lane = lax.broadcasted_iota(jnp.int32, (part, LANES), 1)
    copies = []
    for first in reversed(range(0, days, part)):
        for day in reversed(range(first, first + part)):
            rows = pl.ds(day * blocks, blocks)
            total = None
            for pair in range(pairs):
                term = carries[pair] * moved_ref[pair, rows, :].astype(jnp.float32)
                total = term if total is None else total + term
            stage[rows, :] = partial_ref[rows, :] + reach * total
            reach = reach * retain_ref[rows, :]
        done = pl.ds(first, part)
        for block in range(0, blocks, 2):
            both = [stage[pl.ds(first * blocks + block + half, part, stride=blocks), :] for half in range(2)]
            both = [value + pltpu.roll(value, size, 1) for value in both]
            out_ref[done, pl.ds(block * size, LANES)] = jnp.where(lane < size, both[0], both[1]) * (1.0 / probes)
        copies.append(pltpu.make_async_copy(out_ref.at[done], out_hbm.at[done], left.at[len(copies)]))
        copies[-1].start()
    for copy in copies:
        copy.wait()


def call(kernel, outs, scratch, flops, moved, scalars, *operands, apart=(), limit=VMEM_LIMIT, out_space=pltpu.VMEM):
    in_specs = [
        pl.BlockSpec(memory_space=pltpu.SMEM if i < scalars else pl.ANY if i in apart else pltpu.VMEM)
        for i in range(len(operands))
    ]
    return pl.pallas_call(
        kernel,
        out_shape=[jax.ShapeDtypeStruct(shape, kind) for shape, kind in outs],
        in_specs=in_specs,
        out_specs=[pl.BlockSpec(memory_space=out_space) for _ in outs],
        scratch_shapes=scratch,
        compiler_params=pltpu.CompilerParams(vmem_limit_bytes=limit),
        cost_estimate=pl.CostEstimate(flops=flops, bytes_accessed=moved, transcendentals=0),
    )(*operands)


def crossed(block, axis, bits):
    return lax.ppermute(block, axis, [(i, i ^ bits) for i in range(lax.axis_size(axis))])


def local(
    probes,
    local_links,
    remote_links,
    shared_blocks,
    slab_days,
    local_coupling,
    remote_coupling,
    block_inverse,
    retention,
):
    days, blocks, width = probes.shape
    size = block_inverse.shape[1]
    dims = (days, blocks, size, width // size)
    pairs = width // LANES
    f32, bf16 = jnp.float32, jnp.bfloat16
    bound = shared_blocks.shape[1]
    far = remote_links.shape[1]
    rows = days * blocks
    groups = lax.axis_size("space")
    held = groups // 2 * bound
    near_table, far_table = local_links.T, remote_links.T
    big = ((pairs, rows, LANES), f32)

    (outgoing,) = call(
        functools.partial(outgoing_kernel, dims),
        [((bound, pairs * days, LANES), bf16)],
        [
            pltpu.SMEM(shared_blocks.shape, jnp.int32),
            pltpu.VMEM(probes.shape, bf16),
            pltpu.SemaphoreType.DMA,
            pltpu.SemaphoreType.DMA((2,)),
        ],
        10**9, 4 * 10**6, 0, shared_blocks, probes, apart=(0, 1), limit=63 * 1024 * 1024,
    )
    own_swapped = crossed(outgoing, "space", 1)
    pieces = {bits: crossed(outgoing, "space", bits) for bits in range(groups - 2, 0, -2)}
    by_block = (blocks, pairs * days, LANES)
    moved, turned = call(
        functools.partial(turn_kernel, dims),
        [((pairs, rows, LANES), bf16), (by_block, bf16)],
        [pltpu.VMEM(*big)], 10**10, 10**7, 0, probes, own_swapped, apart=(1,),
    )
    running, remote_weight, inverse = call(
        functools.partial(local_kernel, dims),
        [(by_block, f32), ((blocks, LANES, far * LANES), bf16), ((blocks, LANES, LANES), bf16)],
        [], 10**10, 10**7, 1, near_table, turned, local_coupling, remote_coupling, block_inverse,
    )
    retain, product, through, beyond, active = call(
        functools.partial(retain_kernel, dims),
        [
            ((rows, LANES), f32),
            ((blocks, LANES), bf16),
            ((blocks, days, LANES), f32),
            ((blocks, days, LANES), f32),
            ((days, LANES), f32),
        ],
        [pltpu.VMEM((2, rows, LANES), f32)], 10**6, 10**5, 1, slab_days, retention,
    )
    pieces[0] = outgoing
    batches = [0], list(range(2, groups - 2, 2)), [groups - 2]
    same, other = [outgoing], [own_swapped]
    for batch in batches[1:]:
        shape = (len(batch) * bound, pairs * days, LANES)
        same += call(pass_kernel, [(shape, bf16)], [], 0, 10**5, 0, *[pieces[bits] for bits in batch], inverse)
        other.append(crossed(same[-1], "space", 1))
    raw = [pieces[bits] for bits in range(groups - 2, 0, -2)]
    slabs = lax.axis_size("tm")
    hops = slabs - 1
    exchange = lambda message: [crossed(message, "tm", bits) for bits in range(hops, 0, -1)][::-1]
    inbox = pltpu.VMEM((slabs, pairs + 1, blocks, LANES), bf16)
    values = pltpu.VMEM((pairs, blocks, LANES), f32)
    forcing, message = call(
        functools.partial(forward_kernel, dims, batches),
        [big, ((pairs + 1, blocks, LANES), bf16)],
        [pltpu.VMEM((2 * held, pairs * days, LANES), bf16), pltpu.VMEM(by_block, bf16), values], 10**10, 10**7, 1,
        far_table, active, running, remote_weight, inverse, beyond, product, *raw, *same, *other,
        apart=range(7, 7 + len(raw)),
    )
    ends = exchange(message)
    (states,) = call(
        functools.partial(states_kernel, dims), [(by_block, f32)], [pltpu.VMEM(*big)], 10**9, 10**6, 0, forcing, retain
    )
    adjoint, message = call(
        functools.partial(adjoint_kernel, dims, hops),
        [big, ((pairs, blocks, LANES), bf16)],
        [inbox, values, values], 10**10, 10**7, 0, active, states, through, inverse, *ends,
    )
    starts = exchange(message)
    (partial,) = call(
        functools.partial(own_kernel, dims), [((rows, LANES), f32)], [], 10**9, 10**6, 0, adjoint, retain, moved
    )
    (variance,) = call(
        functools.partial(variance_kernel, dims, hops),
        [((days, blocks * size), f32)],
        [
            pltpu.VMEM((rows, LANES), f32),
            pltpu.VMEM((slabs, pairs, blocks, LANES), bf16),
            inbox,
            pltpu.VMEM((days, blocks * size), f32),
            pltpu.SemaphoreType.DMA((2,)),
        ],
        10**10, 10**7, 0, partial, retain, moved, *starts, *ends, out_space=pl.ANY,
    )
    return variance


def solution(mesh):
    placed = (
        P("tm", "space", None),
        P("space", None),
        P("space", None),
        P("space", None),
        P("tm"),
        P("space", None, None, None),
        P("space", None, None, None),
        P("space", None, None),
        P("tm", "space"),
    )
    return jax.shard_map(
        local, mesh=mesh, in_specs=placed, out_specs=P("tm", "space"), check_vma=False
    )
```

```python
import functools

import jax
import jax.numpy as jnp
from jax import lax
from jax.experimental import pallas as pl
from jax.experimental.pallas import tpu as pltpu
from jax.sharding import PartitionSpec as P

LANES = 128
VMEM_LIMIT = 20 * 1024 * 1024
TURNED = (((1,), (1,)), ((), ()))


def permutation(size, probes, start, width):
    total = size * probes
    column = lax.broadcasted_iota(jnp.int32, (total, width), 1) + start
    origin = (column % size) * probes + column // size
    row = lax.broadcasted_iota(jnp.int32, (total, width), 0)
    return (row == origin).astype(jnp.float32).astype(jnp.bfloat16)


def doubled(weight):
    zero = jnp.zeros_like(weight)
    return jnp.concatenate(
        [jnp.concatenate([weight, zero], axis=1), jnp.concatenate([zero, weight], axis=1)], axis=0
    )


def outgoing_kernel(dims, shared_hbm, z_hbm, outgoing_ref, shared_ref, z_ref, listed, arrived):
    days, blocks, size, probes = dims
    count = outgoing_ref.shape[0]
    parts = arrived.shape[0]
    part = days // parts
    copies = [
        pltpu.make_async_copy(z_hbm.at[pl.ds(i * part, part)], z_ref.at[pl.ds(i * part, part)], arrived.at[i])
        for i in range(parts)
    ]
    listing = pltpu.make_async_copy(shared_hbm, shared_ref, listed)
    listing.start()
    for copy in copies:
        copy.start()
    row = lax.broadcasted_iota(jnp.int32, (part, part * blocks), 0)
    column = lax.broadcasted_iota(jnp.int32, (part, part * blocks), 1)
    move = permutation(size, probes, 0, 2 * LANES)
    listing.wait()
    picks = [(column == row * blocks + shared_ref[0, m]).astype(jnp.float32) for m in range(count)]
    picks = jnp.concatenate(picks, axis=0).astype(jnp.bfloat16)
    picked = []
    for i, copy in enumerate(copies):
        copy.wait()
        z = z_ref[pl.ds(i * part, part)].reshape(part * blocks, size * probes)
        picked.append(jnp.dot(picks, z, preferred_element_type=jnp.float32))
    picked = jnp.concatenate([rows[m * part : (m + 1) * part] for m in range(count) for rows in picked], axis=0)
    step = 2 * LANES
    shift = step // size
    ranges = size * probes // step
    shifted = [picked] + [pltpu.roll(picked, size * probes - i * shift, 1) for i in range(1, ranges)]
    shifted = jnp.concatenate(shifted, axis=0).astype(jnp.bfloat16)
    moved = jnp.dot(shifted, move, preferred_element_type=jnp.float32)
    moved = moved.astype(jnp.bfloat16)
    for pair in range(size * probes // LANES):
        for m in range(count):
            row, lane = (pair // 2 * count + m) * days, pair % 2 * LANES
            outgoing_ref[m, pl.ds(pair * days, days), :] = moved[row : row + days, lane : lane + LANES]


def turn_kernel(dims, z_ref, moved_ref, turned_ref, stage):
    days, blocks, size, probes = dims
    pairs = size * probes // LANES
    z = z_ref[...].reshape(days * blocks, size * probes)
    step = 2 * LANES
    for start in range(0, size * probes, step):
        moved = jnp.dot(z, permutation(size, probes, start, step), preferred_element_type=jnp.float32)
        for half in range(2):
            pair = start // LANES + half
            tile = moved[:, half * LANES : (half + 1) * LANES]
            stage[pair] = tile
            moved_ref[pair] = tile.astype(jnp.bfloat16)
    for block in range(blocks):
        for pair in range(pairs):
            rows = stage[pair, pl.ds(block, days, stride=blocks), :]
            turned_ref[block, pl.ds(pair * days, days), :] = rows.astype(jnp.bfloat16)


def local_kernel(
    dims, links_ref, turned_ref, weight_ref, remote_weight_ref, inverse_ref,
    running_ref, remote_doubled_ref, inverse_doubled_ref,
):
    days, blocks, size, probes = dims
    count = links_ref.shape[0]
    for block in range(blocks):
        near = jnp.concatenate([turned_ref[links_ref[k, block]] for k in range(count)], axis=1)
        weight = jnp.concatenate([doubled(weight_ref[block, k]) for k in range(count)], axis=1)
        total = lax.dot_general(near, weight, TURNED, preferred_element_type=jnp.float32)
        running_ref[block] = turned_ref[block].astype(jnp.float32) - total
        remote_doubled_ref[block] = jnp.concatenate(
            [doubled(remote_weight_ref[block, k]) for k in range(remote_weight_ref.shape[1])], axis=1
        )
        inverse_doubled_ref[block] = doubled(inverse_ref[block])


def retain_kernel(
    dims, days_ref, retention_ref, retain_ref, product_ref, through_ref, beyond_ref, active_ref, stage
):
    days, blocks, size, probes = dims
    observed = days_ref[0]
    shape = (days, LANES)
    first = lax.broadcasted_iota(jnp.int32, shape, 1) < size
    seen = lax.broadcasted_iota(jnp.int32, shape, 0) < observed
    active_ref[...] = jnp.where(seen, 1.0, 0.0)
    for block in range(0, blocks, 2):
        factor = jnp.where(seen, retention_ref[:, pl.ds(block * size, LANES)], 1.0)
        other = pltpu.roll(factor, size, 1)
        retain_ref[pl.ds(block, days, stride=blocks), :] = jnp.where(first, factor, other)
        retain_ref[pl.ds(block + 1, days, stride=blocks), :] = jnp.where(first, other, factor)
    product = jnp.ones((blocks, LANES), jnp.float32)
    for day in range(days):
        rows = pl.ds(day * blocks, blocks)
        product = product * retain_ref[rows, :]
        stage[0, rows, :] = product
    after = jnp.ones((blocks, LANES), jnp.float32)
    for day in reversed(range(days)):
        rows = pl.ds(day * blocks, blocks)
        stage[1, rows, :] = after
        after = after * retain_ref[rows, :]
    for block in range(blocks):
        through_ref[block] = stage[0, pl.ds(block, days, stride=blocks), :]
        beyond_ref[block] = stage[1, pl.ds(block, days, stride=blocks), :]
    high = product.astype(jnp.bfloat16).astype(jnp.float32)
    half = lax.broadcasted_iota(jnp.int32, product.shape, 1) < size
    product_ref[...] = jnp.where(half, high, product - high).astype(jnp.bfloat16)


def pass_kernel(*refs):
    *piece_refs, before_ref, out_ref = refs
    count = piece_refs[0].shape[0]
    for k, ref in enumerate(piece_refs):
        out_ref[pl.ds(k * count, count)] = ref[...]


def forward_kernel(
    dims, batches, links_ref, active_ref, running_ref, weight_ref, inverse_ref, beyond_ref, product_ref, *rest
):
    days, blocks, size, probes = dims
    piece_refs = rest[-5 - 2 * len(batches) : -5]
    forcing_ref, message_ref, remote, source, ends = rest[-5:]
    pairs = forcing_ref.shape[0]
    count = links_ref.shape[0]
    held = remote.shape[0] // 2
    bound = piece_refs[0].shape[0] // len(batches[0])
    me = lax.axis_index("space")
    for core in range(2):
        for ref, batch in zip(piece_refs[core * len(batches) :], batches):
            for place, bits in enumerate(batch):
                if bits not in batch[:place]:
                    remote[pl.ds(core * held + bits // 2 * bound, bound)] = ref[pl.ds(place * bound, bound)]
    active = active_ref[...]
    for block in range(blocks):
        places = []
        for k in range(count):
            link = links_ref[k, block]
            distance = (link // bound) ^ me
            places.append((distance % 2) * held + (distance // 2) * bound + link % bound)
        far = jnp.concatenate([remote[place] for place in places], axis=1)
        total = lax.dot_general(far, weight_ref[block], TURNED, preferred_element_type=jnp.float32)
        source[block] = (running_ref[block] - total).astype(jnp.bfloat16)
    for block in range(blocks):
        drive = lax.dot_general(source[block], inverse_ref[block], TURNED, preferred_element_type=jnp.float32)
        beyond = beyond_ref[block]
        for pair in range(pairs):
            tile = active * drive[pair * days : (pair + 1) * days]
            forcing_ref[pair, pl.ds(block, days, stride=blocks), :] = tile
            ends[pair, pl.ds(block, 1), :] = jnp.sum(beyond * tile, axis=0, keepdims=True)
    leave(message_ref, [ends[pair] for pair in range(pairs)])
    message_ref[pairs] = product_ref[...]


def leave(message_ref, values):
    for pair, value in enumerate(values):
        message_ref[pair] = value.astype(jnp.bfloat16)


def collect(piece_refs, inbox):
    me = lax.axis_index("tm")
    for k, ref in enumerate(piece_refs):
        inbox[me ^ (k + 1)] = ref[...]


def carried(pairs, inbox, products, backward):
    me, count = lax.axis_index("tm"), inbox.shape[0]
    carries = [jnp.zeros(inbox.shape[2:], jnp.float32)] * pairs
    for slab in range(count - 1, 0, -1) if backward else range(count - 1):
        valid = slab > me if backward else slab < me
        terms = products[slab, pairs].astype(jnp.float32)
        factor = terms + pltpu.roll(terms, LANES // 2, 1)
        for pair in range(pairs):
            update = inbox[slab, pair].astype(jnp.float32) + factor * carries[pair]
            carries[pair] = jnp.where(valid, update, carries[pair])
    return carries


def states_kernel(dims, forcing_ref, retain_ref, states_ref, stage):
    days, blocks, size, probes = dims
    pairs = forcing_ref.shape[0]
    states = [jnp.zeros((blocks, LANES), jnp.float32)] * pairs
    for day in range(days):
        rows = pl.ds(day * blocks, blocks)
        factor = retain_ref[rows, :]
        for pair in range(pairs):
            states[pair] = factor * states[pair] + forcing_ref[pair, rows, :]
            stage[pair, rows, :] = states[pair]
    for block in range(blocks):
        for pair in range(pairs):
            states_ref[block, pl.ds(pair * days, days), :] = stage[pair, pl.ds(block, days, stride=blocks), :]


def adjoint_kernel(dims, hops, active_ref, states_ref, through_ref, inverse_ref, *rest):
    days, blocks, size, probes = dims
    adjoint_ref, message_ref, inbox, enter, starts, stored = rest[hops:]
    pairs = adjoint_ref.shape[0]
    collect(rest[:hops], inbox)
    active = active_ref[...]
    for pair, carry in enumerate(carried(pairs, inbox, inbox, False)):
        enter[pair] = carry
    for block in range(blocks):
        through = through_ref[block]
        for pair in range(pairs):
            rows = pl.ds(pair * days, days)
            state = states_ref[block, rows, :] + through * enter[pair, pl.ds(block, 1), :]
            stored[block, rows, :] = state.astype(jnp.bfloat16)
    for block in range(blocks):
        through = through_ref[block]
        adjoint = jnp.dot(stored[block], inverse_ref[block], preferred_element_type=jnp.float32)
        for pair in range(pairs):
            tile = active * adjoint[pair * days : (pair + 1) * days]
            adjoint_ref[pair, pl.ds(block, days, stride=blocks), :] = tile
            starts[pair, pl.ds(block, 1), :] = jnp.sum(through * tile, axis=0, keepdims=True)
    leave(message_ref, [starts[pair] for pair in range(pairs)])


def own_kernel(dims, adjoint_ref, retain_ref, moved_ref, partial_ref):
    days, blocks, size, probes = dims
    pairs = adjoint_ref.shape[0]
    carries = [jnp.zeros((blocks, LANES), jnp.float32)] * pairs
    for day in reversed(range(days)):
        rows = pl.ds(day * blocks, blocks)
        factor = retain_ref[rows, :]
        total = None
        for pair in range(pairs):
            smoothed = adjoint_ref[pair, rows, :] + carries[pair]
            carries[pair] = factor * smoothed
            term = smoothed * moved_ref[pair, rows, :].astype(jnp.float32)
            total = term if total is None else total + term
        partial_ref[rows, :] = total


def variance_kernel(dims, hops, partial_ref, retain_ref, moved_ref, *rest):
    days, blocks, size, probes = dims
    pairs = moved_ref.shape[0]
    out_hbm, stage, inbox, products, out_ref, left = rest[2 * hops :]
    collect(rest[:hops], inbox)
    collect(rest[hops : 2 * hops], products)
    carries = carried(pairs, inbox, products, True)
    reach = jnp.ones((blocks, LANES), jnp.float32)
    parts = left.shape[0]
    part = days // parts
    lane = lax.broadcasted_iota(jnp.int32, (part, LANES), 1)
    copies = []
    for first in reversed(range(0, days, part)):
        for day in reversed(range(first, first + part)):
            rows = pl.ds(day * blocks, blocks)
            total = None
            for pair in range(pairs):
                term = carries[pair] * moved_ref[pair, rows, :].astype(jnp.float32)
                total = term if total is None else total + term
            stage[rows, :] = partial_ref[rows, :] + reach * total
            reach = reach * retain_ref[rows, :]
        done = pl.ds(first, part)
        for block in range(0, blocks, 2):
            both = [stage[pl.ds(first * blocks + block + half, part, stride=blocks), :] for half in range(2)]
            both = [value + pltpu.roll(value, size, 1) for value in both]
            out_ref[done, pl.ds(block * size, LANES)] = jnp.where(lane < size, both[0], both[1]) * (1.0 / probes)
        copies.append(pltpu.make_async_copy(out_ref.at[done], out_hbm.at[done], left.at[len(copies)]))
        copies[-1].start()
    for copy in copies:
        copy.wait()


def call(kernel, outs, scratch, flops, moved, scalars, *operands, apart=(), limit=VMEM_LIMIT, out_space=pltpu.VMEM):
    in_specs = [
        pl.BlockSpec(memory_space=pltpu.SMEM if i < scalars else pl.ANY if i in apart else pltpu.VMEM)
        for i in range(len(operands))
    ]
    return pl.pallas_call(
        kernel,
        out_shape=[jax.ShapeDtypeStruct(shape, kind) for shape, kind in outs],
        in_specs=in_specs,
        out_specs=[pl.BlockSpec(memory_space=out_space) for _ in outs],
        scratch_shapes=scratch,
        compiler_params=pltpu.CompilerParams(vmem_limit_bytes=limit),
        cost_estimate=pl.CostEstimate(flops=flops, bytes_accessed=moved, transcendentals=0),
    )(*operands)


def crossed(block, axis, bits):
    return lax.ppermute(block, axis, [(i, i ^ bits) for i in range(lax.axis_size(axis))])


def local(
    probes,
    local_links,
    remote_links,
    shared_blocks,
    slab_days,
    local_coupling,
    remote_coupling,
    block_inverse,
    retention,
):
    days, blocks, width = probes.shape
    size = block_inverse.shape[1]
    dims = (days, blocks, size, width // size)
    pairs = width // LANES
    f32, bf16 = jnp.float32, jnp.bfloat16
    bound = shared_blocks.shape[1]
    far = remote_links.shape[1]
    rows = days * blocks
    groups = lax.axis_size("space")
    held = groups // 2 * bound
    near_table, far_table = local_links.T, remote_links.T
    big = ((pairs, rows, LANES), f32)

    (outgoing,) = call(
        functools.partial(outgoing_kernel, dims),
        [((bound, pairs * days, LANES), bf16)],
        [
            pltpu.SMEM(shared_blocks.shape, jnp.int32),
            pltpu.VMEM(probes.shape, bf16),
            pltpu.SemaphoreType.DMA,
            pltpu.SemaphoreType.DMA((2,)),
        ],
        10**9, 4 * 10**6, 0, shared_blocks, probes, apart=(0, 1), limit=63 * 1024 * 1024,
    )
    pieces = {bits: crossed(outgoing, "space", bits) for bits in range(groups - 2, 0, -2)}
    by_block = (blocks, pairs * days, LANES)
    moved, turned = call(
        functools.partial(turn_kernel, dims),
        [((pairs, rows, LANES), bf16), (by_block, bf16)],
        [pltpu.VMEM(*big)], 10**10, 10**7, 0, probes,
    )
    running, remote_weight, inverse = call(
        functools.partial(local_kernel, dims),
        [(by_block, f32), ((blocks, LANES, far * LANES), bf16), ((blocks, LANES, LANES), bf16)],
        [], 10**10, 10**7, 1, near_table, turned, local_coupling, remote_coupling, block_inverse,
    )
    retain, product, through, beyond, active = call(
        functools.partial(retain_kernel, dims),
        [
            ((rows, LANES), f32),
            ((blocks, LANES), bf16),
            ((blocks, days, LANES), f32),
            ((blocks, days, LANES), f32),
            ((days, LANES), f32),
        ],
        [pltpu.VMEM((2, rows, LANES), f32)], 10**6, 10**5, 1, slab_days, retention,
    )
    pieces[0] = outgoing
    batches = [0, groups - 2, groups - 2], list(range(groups - 4, 0, -2))
    same = []
    for batch in batches:
        shape = (len(batch) * bound, pairs * days, LANES)
        same += call(pass_kernel, [(shape, bf16)], [], 0, 10**5, 0, *[pieces[bits] for bits in batch], inverse)
    other = [crossed(piece, "space", 1) for piece in same]
    raw = [pieces[bits] for bits in range(2, groups, 2)]
    slabs = lax.axis_size("tm")
    hops = slabs - 1
    exchange = lambda message: [crossed(message, "tm", bits) for bits in range(hops, 0, -1)][::-1]
    inbox = pltpu.VMEM((slabs, pairs + 1, blocks, LANES), bf16)
    values = pltpu.VMEM((pairs, blocks, LANES), f32)
    forcing, message = call(
        functools.partial(forward_kernel, dims, batches),
        [big, ((pairs + 1, blocks, LANES), bf16)],
        [pltpu.VMEM((2 * held, pairs * days, LANES), bf16), pltpu.VMEM(by_block, bf16), values], 10**10, 10**7, 1,
        far_table, active, running, remote_weight, inverse, beyond, product, *raw, *same, *other,
        apart=range(7, 7 + len(raw)),
    )
    ends = exchange(message)
    (states,) = call(
        functools.partial(states_kernel, dims), [(by_block, f32)], [pltpu.VMEM(*big)], 10**9, 10**6, 0, forcing, retain
    )
    adjoint, message = call(
        functools.partial(adjoint_kernel, dims, hops),
        [big, ((pairs, blocks, LANES), bf16)],
        [inbox, values, values, pltpu.VMEM(by_block, bf16)], 10**10, 10**7, 0, active, states, through, inverse, *ends,
    )
    starts = exchange(message)
    (partial,) = call(
        functools.partial(own_kernel, dims), [((rows, LANES), f32)], [], 10**9, 10**6, 0, adjoint, retain, moved
    )
    (variance,) = call(
        functools.partial(variance_kernel, dims, hops),
        [((days, blocks * size), f32)],
        [
            pltpu.VMEM((rows, LANES), f32),
            pltpu.VMEM((slabs, pairs, blocks, LANES), bf16),
            inbox,
            pltpu.VMEM((days, blocks * size), f32),
            pltpu.SemaphoreType.DMA((2,)),
        ],
        10**10, 10**7, 0, partial, retain, moved, *starts, *ends, out_space=pl.ANY,
    )
    return variance


def solution(mesh):
    placed = (
        P("tm", "space", None),
        P("space", None),
        P("space", None),
        P("space", None),
        P("tm"),
        P("space", None, None, None),
        P("space", None, None, None),
        P("space", None, None),
        P("tm", "space"),
    )
    return jax.shard_map(
        local, mesh=mesh, in_specs=placed, out_specs=P("tm", "space"), check_vma=False
    )
```
